32 devices in a mesh: ctx: 4 (over x, core), exp: 8 (over z, y).
Axes of the slice: x: 2, y: 2, z: 4, core: 2. Of those that a mesh axis runs over, the one named last changes fastest.
Arguments:
- queries: bfloat16 [8, 512, 1024], P('exp', 'ctx'), may hold values from -6 to 6
- keys: bfloat16 [8, 512, 1024], P('exp', 'ctx'), may hold values from -6 to 6
- values: bfloat16 [8, 512, 2048], P('exp', 'ctx'), may hold values from -6 to 6
- out_gate: bfloat16 [8, 512, 2048], P('exp', 'ctx'), may hold values from -6 to 6
- write_rate: float32 [8, 512, 16], P('exp', 'ctx'), may hold values from 0.02 to 0.2
- decay: float32 [8, 512, 16], P('exp', 'ctx'), may hold values from 0.6 to 1
- head_gain: float32 [128], replicated, may hold values from 0.1 to 1.9
- residual: bfloat16 [8, 512, 2048], P('exp', 'ctx'), may hold values from -6 to 6
- out_proj: bfloat16 [2048, 2048], P('ctx'), may hold values from -0.125 to 0.125
- ffn_gain: float32 [2048], replicated, may hold values from 0.25 to 1.75
- expert_ids: int32 [8, 512, 10], P('exp', 'ctx'), may hold values from 0 to 511, all different within a row; in each aligned block of 128 rows (0 to 127, 128 to 255, ..., all dimensions but the last counted through in order) at most 4 rows name the same one
- route_weight: float32 [8, 512, 10], P('exp', 'ctx'), may hold values from 0.1 to 0.4
- w_gate: bfloat16 [32, 2048, 512], P(('ctx', 'exp')), may hold values from -0.125 to 0.125
- w_up: bfloat16 [32, 2048, 512], P(('ctx', 'exp')), may hold values from -0.125 to 0.125
- w_down: bfloat16 [32, 512, 2048], P(('ctx', 'exp')), may hold values from -0.25 to 0.25
- ablate_mask: int32 [8, 512], P('exp', 'ctx'), may hold values 0 or 1
- direction: float32 [2048], replicated, may hold values from -6 to 6
Outputs:
- layer_out: bfloat16 [8, 512, 2048], P('exp', 'ctx')
The draws below stay inside these ranges and needn't reach their ends.
Inputs may be any that keep to these rules, and one draw needn't show every extreme that they name: `expert_ids`: A token's 10 experts differ; within the rows of one device (aligned blocks of 128 tokens of a sequence) no expert is named more than 4 times.
All inputs are finite; a program needn't handle non-finite values. No bound on the sum of `ablate_mask` on one device may be relied on, other than what follows from the above.
Results may differ from the reference program's by a relative error of at most 0.0044.
Values may be sent and summed in bfloat16 or wider, within the bound.
No kernel may reach another device: no remote copies, remote signals or barrier semaphores. Data moves between devices by JAX's collectives and lax.ppermute only.
A program may use at most 128 MiB of HBM per device.

```python
import math
import jax
import jax.numpy as jnp
import numpy as np
from jax import lax

D = 2048
CONTENT_MIXERS = 16
KH = 8
DK = 128
DV = 128
FE = 512
ROUTED = 512
TOP = 10
SHARD_POSITIONS = 128
CAP = 4
EXPERTS = 32
PROMPT_GROUP = 8
SPAN_POSITIONS = 512
N_CTX = 4


def draw_decay(key, part):
    stochastic_seed_parts = jax.random.split(key, 7)
    segment_number = SPAN_POSITIONS // SHARD_POSITIONS
    fast_share = 0.5
    fast_heads = jax.random.uniform(stochastic_seed_parts[0], (PROMPT_GROUP, 1, 1, CONTENT_MIXERS)) < fast_share
    fast_rate = jax.random.uniform(stochastic_seed_parts[1], (PROMPT_GROUP, 1, 1, CONTENT_MIXERS), minval=1.0 / 50.0, maxval=1.0 / 30.0)
    slow_rate = jax.random.uniform(stochastic_seed_parts[2], (PROMPT_GROUP, 1, 1, CONTENT_MIXERS), minval=0.02, maxval=0.2) * (math.log(10.0) / SPAN_POSITIONS)
    reference_frequency = jnp.where(fast_heads, fast_rate, slow_rate)
    segment_multiplier = jnp.exp(jax.random.uniform(stochastic_seed_parts[3], (PROMPT_GROUP, segment_number, 1, CONTENT_MIXERS), minval=math.log(0.6), maxval=math.log(1.6)))
    unevenness_level = jax.random.uniform(stochastic_seed_parts[4], (PROMPT_GROUP, segment_number, SHARD_POSITIONS, CONTENT_MIXERS), minval=0.5, maxval=1.5)
    cluster_occurrences = jax.random.uniform(stochastic_seed_parts[5], (PROMPT_GROUP, segment_number, SHARD_POSITIONS, 1)) < 2.0 / SPAN_POSITIONS
    cluster_surviving = jnp.where(cluster_occurrences, jax.random.uniform(stochastic_seed_parts[6], (PROMPT_GROUP, segment_number, SHARD_POSITIONS, CONTENT_MIXERS), minval=0.7, maxval=0.8), 1.0)
    content_outcomes = jnp.exp(-reference_frequency * segment_multiplier * unevenness_level) * cluster_surviving
    return content_outcomes.reshape(PROMPT_GROUP, SPAN_POSITIONS, CONTENT_MIXERS).astype(jnp.float32)


def with_ends(values, key, low, top_value):
    extent = values.shape
    spot = [jax.random.randint(jax.random.fold_in(key, axis), (), 0, extent[axis]) for axis in range(len(extent))]
    values = values.at[tuple(spot)].set(low)
    longest = extent.index(max(extent))
    spot[longest] = (spot[longest] + 1) % extent[longest]
    return values.at[tuple(spot)].set(top_value)


def shard_levels(own_key, shape, pieces, low, high):
    factor_of = 1.0
    for position, shards_of in pieces:
        heights = jax.random.uniform(jax.random.fold_in(jax.random.fold_in(own_key, 6), position), (shards_of,), jnp.float32, low / len(pieces), high / len(pieces))
        factor_of = factor_of * jnp.repeat(jnp.exp(heights), shape[position] // shards_of).reshape((-1,) + (1,) * (len(shape) - 1 - position))
    return factor_of


def routed_block(key, own, number, rows, amount, top, bound, skew):
    sequence = jax.random.permutation(key, amount)
    crowded, ordinary = load_shares(amount, rows * top, bound, skew, True), load_shares(amount, rows * top, bound, skew, False)
    places = jnp.arange(amount)

    def named(lengths, offset_by):
        used = int((lengths > 0).sum())
        fixed = max(1, used // 4)
        shifted = fixed + (places - fixed + offset_by * (used - fixed)) % max(1, amount - fixed)
        return jnp.zeros((amount,), jnp.int32).at[sequence[jnp.where(places < fixed, places, shifted)]].set(jnp.asarray(lengths, jnp.int32))

    lengths = jnp.where(number % 4 == 0, named(crowded, number // 4), named(ordinary, number - number // 4 - 1))
    mixed = jax.random.permutation(jax.random.fold_in(own, 3), amount)
    source_of, receiver = mixed[0:amount // 2 * 2:2], mixed[1:amount // 2 * 2:2]
    room = jnp.minimum(lengths[source_of] - 1, bound - lengths[receiver]) // 2
    room = jnp.where((source_of == sequence[0]) | (receiver == sequence[0]) | (lengths[receiver] == 0), 0, jnp.maximum(room, 0))
    shifted = jax.random.randint(jax.random.fold_in(own, 4), (amount // 2,), 0, 1 << 20) % (room + 1)
    lengths = lengths.at[source_of].add(-shifted).at[receiver].add(shifted)
    labels = jnp.searchsorted(jnp.cumsum(lengths), jnp.arange(rows * top), side="right").astype(jnp.int32)
    listing = labels.reshape(top, rows).T
    listing = listing[jax.random.permutation(jax.random.fold_in(own, 1), rows)]
    offset_by = jax.random.randint(jax.random.fold_in(own, 2), (rows, 1), 0, top)
    return jnp.take_along_axis(listing, (jnp.arange(top)[None, :] + offset_by) % top, axis=1)


def load_shares(count, total, bound, lean, full):
    portions = [(1 << 20) // math.isqrt(rank ** lean) + 1 for rank in range(1, count + 1)]
    largest = bound if full else min(bound, max(-(-total // count), total * portions[0] // sum(portions)))
    least = 1 if total - largest >= count - 1 else 0
    holding, surplus = [largest] + [least] * (count - 1), total - largest - least * (count - 1)
    while surplus > 0:
        free = [i for i in range(1, count) if holding[i] < largest] or [i for i in range(1, count) if holding[i] < bound]
        whole, left = sum([portions[i] for i in free]), surplus
        for i in free:
            extra = min(bound - holding[i], max(1, left * portions[i] // whole), surplus)
            holding[i] = holding[i] + extra
            surplus = surplus - extra
    return np.array(holding)


def scatter_about(key, extent, width, limit, pieces=(), kind=jnp.bfloat16):
    loudness = shard_levels(key, extent, pieces, -0.22, 0.18) if pieces else 1.0
    values = jax.random.normal(key, extent, jnp.float32) * width * loudness
    return jnp.minimum(jnp.maximum(values, -limit), limit).astype(kind)


def setup_inputs(seed: int = 0) -> dict:
    splits = jax.random.split(jax.random.key(seed), 18)
    queries = scatter_about(splits[0], (PROMPT_GROUP, SPAN_POSITIONS, KH * DK), 1.0, 6.0, ((0, 8), (1, 4)))
    keys = scatter_about(splits[1], (PROMPT_GROUP, SPAN_POSITIONS, KH * DK), 1.0, 6.0, ((0, 8), (1, 4)))
    values = scatter_about(splits[2], (PROMPT_GROUP, SPAN_POSITIONS, CONTENT_MIXERS * DV), 1.0, 6.0, ((0, 8), (1, 4)))
    out_gate = scatter_about(splits[3], (PROMPT_GROUP, SPAN_POSITIONS, CONTENT_MIXERS * DV), 1.0, 6.0, ((0, 8), (1, 4)))
    write_rate = jnp.clip(0.02 + 0.18 * jax.random.uniform(splits[4], (PROMPT_GROUP, SPAN_POSITIONS, CONTENT_MIXERS), jnp.float32) ** shard_levels(splits[4], (PROMPT_GROUP, SPAN_POSITIONS, CONTENT_MIXERS), ((0, 8), (1, 4)), -0.2, 0.2), 0.02, 0.2)
    decay = draw_decay(jax.random.fold_in(splits[17], 71), 0)
    head_gain = jnp.clip(1.0 + 0.18 * jax.random.normal(splits[6], (DV,), jnp.float32), 0.1, 1.9)
    residual = scatter_about(splits[7], (PROMPT_GROUP, SPAN_POSITIONS, D), 1.0, 6.0, ((0, 8), (1, 4)))
    out_proj = scatter_about(splits[8], (CONTENT_MIXERS * DV, D), (CONTENT_MIXERS * DV) ** -0.5, 0.125, ((0, 4),))
    ffn_gain = jnp.clip(1.0 + 0.15 * jax.random.normal(splits[9], (D,), jnp.float32), 0.25, 1.75)
    expert_ids_keys = jax.random.split(jax.random.fold_in(splits[10], 1), PROMPT_GROUP * SPAN_POSITIONS // SHARD_POSITIONS)
    expert_ids_turns = jax.random.permutation(jax.random.fold_in(splits[10], 3), PROMPT_GROUP * SPAN_POSITIONS // SHARD_POSITIONS)
    expert_ids = jax.vmap(lambda own, number: routed_block(jax.random.fold_in(splits[10], 2), own, number, SHARD_POSITIONS, ROUTED, TOP, CAP, 1))(expert_ids_keys, expert_ids_turns).reshape((PROMPT_GROUP, SPAN_POSITIONS, TOP))
    route_weight = jnp.clip(0.1 + 0.3 * jax.random.uniform(splits[11], (PROMPT_GROUP, SPAN_POSITIONS, TOP), jnp.float32) ** shard_levels(splits[11], (PROMPT_GROUP, SPAN_POSITIONS, TOP), ((0, 8), (1, 4)), -0.2, 0.2), 0.1, 0.4)
    w_gate = scatter_about(splits[12], (EXPERTS, D, FE), D ** -0.5, 0.125, ((0, 32),))
    w_up = scatter_about(splits[13], (EXPERTS, D, FE), D ** -0.5, 0.125, ((0, 32),))
    w_down = scatter_about(splits[14], (EXPERTS, FE, D), FE ** -0.5, 0.25, ((0, 32),))
    ablate_mask = with_ends((jax.random.randint(splits[15], (PROMPT_GROUP, SPAN_POSITIONS), 0, 2) < 1).astype(jnp.int32), jax.random.fold_in(splits[15], 1), 0, 1)
    direction = scatter_about(splits[16], (D,), 1.0, 6.0, (), jnp.float32)
    return dict(queries=queries, keys=keys, values=values, out_gate=out_gate, write_rate=write_rate, decay=decay, head_gain=head_gain, residual=residual, out_proj=out_proj, ffn_gain=ffn_gain, expert_ids=expert_ids, route_weight=route_weight, w_gate=w_gate, w_up=w_up, w_down=w_down, ablate_mask=ablate_mask, direction=direction)


HIGHEST = lax.Precision.HIGHEST

def block_maps(query_f, key_unit, value_f, write_f, decay_f):
    length_b = decay_f.shape[-1]
    width_k = key_unit.shape[-1]
    log_decay = jnp.cumsum(jnp.log(decay_f), axis=-1)
    row_ids = lax.broadcasted_iota(jnp.int32, (length_b, length_b), 0)
    col_ids = lax.broadcasted_iota(jnp.int32, (length_b, length_b), 1)
    on_after = (row_ids >= col_ids).astype(jnp.float32)
    strictly = (row_ids > col_ids).astype(jnp.float32)
    ratios = jnp.exp(jnp.minimum(log_decay[..., :, None] - log_decay[..., None, :], 0.0)) * on_after
    cumulative = jnp.exp(log_decay)
    key_dots = jnp.einsum('...id,...jd->...ij', key_unit, key_unit, precision=HIGHEST)
    system = jnp.eye(length_b, dtype=jnp.float32) + write_f[..., :, None] * ratios * strictly * key_dots
    writes = jax.scipy.linalg.solve_triangular(system, write_f[..., None] * value_f, lower=True, unit_diagonal=True)
    erases = jax.scipy.linalg.solve_triangular(system, (write_f * cumulative)[..., None] * key_unit, lower=True, unit_diagonal=True)
    scores = jnp.einsum('...id,...jd->...ij', query_f, key_unit, precision=HIGHEST) * ratios
    local_out = jnp.einsum('...ij,...jv->...iv', scores, writes, precision=HIGHEST)
    query_eff = cumulative[..., None] * query_f - jnp.einsum('...ij,...jd->...id', scores, erases, precision=HIGHEST)
    remaining = jnp.exp(log_decay[..., -1:] - log_decay)
    weighted = remaining[..., None] * key_unit
    carried = jnp.einsum('...jd,...je->...de', weighted, erases, precision=HIGHEST)
    transition = cumulative[..., -1][..., None, None] * jnp.eye(width_k, dtype=jnp.float32) - carried
    offset = jnp.einsum('...jd,...jv->...dv', weighted, writes, precision=HIGHEST)
    return (local_out, query_eff, transition, offset)

def blocks_of_heads(array):
    shaped = array.reshape(PROMPT_GROUP, N_CTX, SHARD_POSITIONS, CONTENT_MIXERS, array.shape[-1])
    return shaped.transpose(1, 0, 3, 2, 4)

def blocks_of_rates(array):
    shaped = array.reshape(PROMPT_GROUP, N_CTX, SHARD_POSITIONS, CONTENT_MIXERS)
    return shaped.transpose(1, 0, 3, 2)

def reference(queries, keys, values, out_gate, write_rate, decay, head_gain, residual, out_proj, ffn_gain, expert_ids, route_weight, w_gate, w_up, w_down, ablate_mask, direction):
    group_size = CONTENT_MIXERS // KH
    query_raw = jnp.repeat(queries.astype(jnp.float32).reshape(PROMPT_GROUP, SPAN_POSITIONS, KH, DK), group_size, axis=2)
    query_f = query_raw / jnp.sqrt(lax.optimization_barrier(jnp.sum(query_raw * query_raw, -1, keepdims=True)) + 1e-06) * DK ** (-0.5)
    key_f = jnp.repeat(keys.astype(jnp.float32).reshape(PROMPT_GROUP, SPAN_POSITIONS, KH, DK), group_size, axis=2)
    key_unit = key_f / jnp.sqrt(lax.optimization_barrier(jnp.sum(key_f * key_f, -1, keepdims=True)) + 1e-06)
    value_f = values.astype(jnp.float32).reshape(PROMPT_GROUP, SPAN_POSITIONS, CONTENT_MIXERS, DV)

    def advance(state, inputs):
        query_b, key_b, value_b, write_b, decay_b = inputs
        local_out, query_eff, transition, offset = block_maps(query_b, key_b, value_b, write_b, decay_b)
        block_out = local_out + jnp.einsum('bhid,bhdv->bhiv', query_eff, state, precision=HIGHEST)
        next_state = jnp.einsum('bhij,bhjv->bhiv', transition, state, precision=HIGHEST) + offset
        return (next_state, block_out)
    start_state = jnp.zeros((PROMPT_GROUP, CONTENT_MIXERS, DK, DV), jnp.float32)
    _, block_outs = lax.scan(advance, start_state, (blocks_of_heads(query_f), blocks_of_heads(key_unit), blocks_of_heads(value_f), blocks_of_rates(write_rate), blocks_of_rates(decay)))
    head_out = block_outs.transpose(1, 0, 3, 2, 4).reshape(PROMPT_GROUP, SPAN_POSITIONS, CONTENT_MIXERS, DV)
    mean_square = lax.optimization_barrier(jnp.mean(head_out * head_out, -1, keepdims=True))
    gate_f = out_gate.astype(jnp.float32).reshape(PROMPT_GROUP, SPAN_POSITIONS, CONTENT_MIXERS, DV)
    normed = head_out / jnp.sqrt(mean_square + 1e-06) * head_gain * jax.nn.silu(gate_f)
    tokens_all = PROMPT_GROUP * SPAN_POSITIONS
    mixed = normed.reshape(tokens_all, CONTENT_MIXERS * DV).astype(jnp.bfloat16)
    projected = jnp.dot(mixed.astype(jnp.float32), out_proj.astype(jnp.float32), preferred_element_type=jnp.float32)
    hidden_sum = residual.reshape(tokens_all, D).astype(jnp.float32) + projected
    ffn_in = (hidden_sum / jnp.sqrt(lax.optimization_barrier(jnp.mean(hidden_sum * hidden_sum, -1, keepdims=True)) + 1e-06) * ffn_gain).astype(jnp.bfloat16)
    blocks = tokens_all // SHARD_POSITIONS
    block_ids_list = expert_ids.reshape(blocks, SHARD_POSITIONS * TOP)
    expert_range = jnp.arange(EXPERTS, dtype=jnp.int32)

    def slot_of(row_list):
        one_hot = (row_list[:, None] == expert_range[None, :]).astype(jnp.int32)
        return lax.optimization_barrier(jnp.sum(jnp.cumsum(one_hot, axis=0) * one_hot, axis=1)) - 1
    slots = lax.map(slot_of, block_ids_list)
    in_window = block_ids_list < EXPERTS
    block_ids = jnp.arange(blocks, dtype=jnp.int32)[:, None]
    token_index = block_ids * SHARD_POSITIONS + jnp.arange(SHARD_POSITIONS * TOP, dtype=jnp.int32)[None, :] // TOP
    row_pick = jnp.where(in_window, block_ids_list, EXPERTS)
    col_pick = jnp.where(in_window, block_ids * CAP + slots, 0)
    index_table = jnp.full((EXPERTS + 1, blocks * CAP), tokens_all, jnp.int32).at[row_pick, col_pick].set(token_index)[:EXPERTS]
    weight_table = jnp.zeros((EXPERTS + 1, blocks * CAP), jnp.float32).at[row_pick, col_pick].set(route_weight.reshape(blocks, SHARD_POSITIONS * TOP))[:EXPERTS]
    padded_in = jnp.concatenate([ffn_in, jnp.zeros((1, D), jnp.bfloat16)], axis=0)

    def expert_step(running, inputs):
        index_row, weight_row, gate_mat, up_mat, down_mat = inputs
        rows_in = padded_in[index_row]
        gate_part = jnp.dot(rows_in.astype(jnp.float32), gate_mat.astype(jnp.float32), preferred_element_type=jnp.float32)
        up_part = jnp.dot(rows_in.astype(jnp.float32), up_mat.astype(jnp.float32), preferred_element_type=jnp.float32)
        activated = (jax.nn.silu(gate_part) * up_part).astype(jnp.bfloat16)
        expert_out = jnp.dot(activated.astype(jnp.float32), down_mat.astype(jnp.float32), preferred_element_type=jnp.float32).astype(jnp.bfloat16)
        running = running.at[index_row].add(weight_row[:, None] * expert_out.astype(jnp.float32))
        return (running, None)
    moe_start = jnp.zeros((tokens_all + 1, D), jnp.float32)
    moe_total, _ = lax.scan(expert_step, moe_start, (index_table, weight_table, w_gate, w_up, w_down))
    combined = hidden_sum + moe_total[:tokens_all]
    unit_dir = direction / jnp.sqrt(jnp.sum(direction * direction) + 1e-06)
    along = jnp.dot(combined, unit_dir, precision=HIGHEST)
    mask_f = ablate_mask.reshape(tokens_all).astype(jnp.float32)
    layer_out = combined - (mask_f * along)[:, None] * unit_dir[None, :]
    return layer_out.astype(jnp.bfloat16).reshape(PROMPT_GROUP, SPAN_POSITIONS, D)
```

```python
import functools

import jax
import jax.numpy as jnp
from jax import lax
from jax.experimental import pallas as pl
from jax.experimental.pallas import tpu as pltpu
from jax.sharding import PartitionSpec as P

DK = 128
CAP = 4
EPS = 1e-06
LANES = 128

bf16 = jnp.bfloat16
f32 = jnp.float32


def mm(a, b):
    return jnp.dot(a, b, preferred_element_type=f32)


def mm_nt(a, b):
    return lax.dot_general(a, b, (((1,), (1,)), ((), ())), preferred_element_type=f32)


def mm_tn(a, b):
    return lax.dot_general(a, b, (((0,), (0,)), ((), ())), preferred_element_type=f32)


def split2(x):
    hi = x.astype(bf16)
    return hi, (x - hi.astype(f32)).astype(bf16)


def split3(x):
    hi = x.astype(bf16)
    rest = x - hi.astype(f32)
    mid = rest.astype(bf16)
    return hi, mid, (rest - mid.astype(f32)).astype(bf16)


def mm3(a, b):
    (ah, al), (bh, bl) = a, b
    return mm(jnp.concatenate([ah, al, ah], axis=1), jnp.concatenate([bh, bh, bl], axis=0))


def iota(shape, dim):
    return lax.broadcasted_iota(jnp.int32, shape, dim)


def compiler_params(mib):
    return pltpu.CompilerParams(vmem_limit_bytes=mib * 1024 * 1024)


def pack_kernel(n, kw, vw, k_ref, q_ref, v_ref, g_ref, w_ref, d_ref, *outs):
    me = lax.axis_index("ctx")
    tokens = k_ref.shape[1]
    heads = d_ref.shape[1]
    ones = (iota((tokens, tokens), 0) <= iota((tokens, tokens), 1)).astype(bf16)
    logs = jnp.log(d_ref[0])
    sums = sum(mm(piece, ones) for piece in reversed(split3(logs)))
    pieces = [*split3(sums), *split3(w_ref[0])]
    aux = jnp.concatenate([p.astype(f32) for p in pieces], axis=0)
    aux = jnp.concatenate([aux, jnp.zeros((LANES - 6 * heads, tokens), f32)], axis=0).astype(bf16)
    for step, out in enumerate(outs):
        to = lax.rem(me + step, n)
        kat = pl.ds(pl.multiple_of(to * kw, LANES), kw)
        vat = pl.ds(pl.multiple_of(to * vw, LANES), vw)
        out[:, 0:kw] = k_ref[0, :, kat]
        out[:, kw : 2 * kw] = q_ref[0, :, kat]
        out[:, 2 * kw : 2 * kw + vw] = v_ref[0, :, vat]
        out[:, 2 * kw + vw : 2 * kw + 2 * vw] = g_ref[0, :, vat]
        out[:, 2 * kw + 2 * vw :] = aux


def mixer_kernel(n, heads, kw, vw, *refs):
    pieces = refs[:n]
    gain_ref, proj_ref = refs[n : n + 2]
    keeps = refs[n + 2 : n + 2 + n // 2]
    gives = refs[n + 2 + n // 2 : n + 2 + n]
    x_ref, inv_ref, score_ref, state_ref, mixed_ref, sems = refs[n + 2 + n :]
    me = lax.axis_index("ctx")
    tokens = pieces[0].shape[0]
    local = vw // DK
    group = vw // kw
    copies = []
    for step in range(n):
        came = lax.rem(me - step + n, n)
        copy = pltpu.make_async_copy(pieces[step], x_ref.at[came], sems.at[step])
        copy.start()
        copies.append(copy)
    for copy in copies:
        copy.wait()

    row, col = iota((tokens, tokens), 0), iota((tokens, tokens), 1)
    apart = lax.bitwise_xor(row, col)
    eye = (row == col).astype(f32)
    r, l = iota((LANES, LANES), 0), iota((LANES, LANES), 1)
    kind = r // heads
    wanted = me * local + lax.rem(l, local)
    pick = (
        (lax.rem(r, heads) == wanted)
        & (l < 2 * local)
        & (kind // 3 == l // local)
    ).astype(bf16)

    def rates(block):
        aux = x_ref[block, :, 2 * kw + 2 * vw :]
        return mm_tn(aux, pick), mm_tn(pick, aux)

    def unit_scales(raw):
        raw_f = raw.astype(f32)
        return lax.rsqrt(jnp.sum(raw_f * raw_f, axis=1, keepdims=True) + EPS)

    def prepare(block, carry):
        as_cols, as_rows = rates(block)
        systems, all_scores = [], []
        for g in range(local // group):
            k = x_ref[block, :, g * DK : (g + 1) * DK]
            q = x_ref[block, :, kw + g * DK : kw + (g + 1) * DK]
            dots = mm_nt(k, k)
            scores = mm_nt(q, k)
            diag = dots * eye
            k_row = lax.rsqrt(jnp.sum(diag, axis=0, keepdims=True) + EPS)
            k_col = lax.rsqrt(jnp.sum(diag, axis=1, keepdims=True) + EPS)
            q_col = unit_scales(q) * DK ** (-0.5)
            dots = dots * k_row * k_col
            scores = scores * k_row * q_col
            for h in range(g * group, (g + 1) * group):
                gap = as_cols[:, h : h + 1] - as_rows[h : h + 1, :]
                ratios = jnp.exp(jnp.minimum(gap, 0.0))
                write = as_cols[:, local + h : local + h + 1]
                systems.append(jnp.where(row > col, write * ratios * dots, 0.0))
                all_scores.append(jnp.where(row >= col, ratios * scores, 0.0))
        near = [jnp.where(apart < 16, s, 0.0) for s in systems]
        inverse = [eye - s for s in near]
        power = [split2(s) for s in near]
        for _ in range(3):
            power = [split2(mm3(p, p)) for p in power]
            inverse = [x + mm3(split2(x), p) for x, p in zip(inverse, power)]
        size = 16
        while size < tokens:
            off = [split2(jnp.where((apart >= size) & (apart < 2 * size), s, 0.0)) for s in systems]
            halves = [split2(x) for x in inverse]
            left = [split2(mm3(x, o)) for x, o in zip(halves, off)]
            inverse = [x - mm3(a, xs) for x, a, xs in zip(inverse, left, halves)]
            size *= 2
        for h in range(local):
            hi, lo = split2(inverse[h])
            inv_ref[block, h, 0] = hi
            inv_ref[block, h, 1] = lo
            score_ref[block, h] = all_scores[h]
        return carry

    lax.fori_loop(0, n, prepare, 0)
    state_ref[...] = jnp.zeros_like(state_ref)
    gain = gain_ref[...]

    def advance(block, carry):
        as_cols, as_rows = rates(block)
        cumulative = jnp.exp(as_cols)
        rows_at = pl.ds(pl.multiple_of(block * tokens, tokens), tokens)
        for g in range(local // group):
            k = x_ref[block, :, g * DK : (g + 1) * DK]
            q = x_ref[block, :, kw + g * DK : kw + (g + 1) * DK]
            k_col = unit_scales(k)
            q_col = unit_scales(q) * DK ** (-0.5)
            both = jnp.concatenate([k, q], axis=0)
            for h in range(g * group, (g + 1) * group):
                state = state_ref[h]
                high, low = split2(state)
                seen = mm(jnp.concatenate([both, both], axis=1), jnp.concatenate([high, low], axis=0))
                v = x_ref[block, :, 2 * kw + h * DK : 2 * kw + (h + 1) * DK].astype(f32)
                cum = cumulative[:, h : h + 1]
                write = as_cols[:, local + h : local + h + 1]
                rhs = write * (v - (cum * k_col) * seen[:tokens])
                delta = mm3((inv_ref[block, h, 0], inv_ref[block, h, 1]), split2(rhs))
                out = (cum * q_col) * seen[tokens:] + mm3(split2(score_ref[block, h]), split2(delta))
                last = as_cols[tokens - 1 : tokens, h : h + 1]
                kept = jnp.exp(last - as_cols[:, h : h + 1]) * k_col
                dh, dl = split2(kept * delta)
                state_ref[h] = jnp.exp(last) * state + mm_tn(
                    jnp.concatenate([k, k], axis=0), jnp.concatenate([dh, dl], axis=0)
                )
                gate = x_ref[
                    block, :, 2 * kw + vw + h * DK : 2 * kw + vw + (h + 1) * DK
                ].astype(f32)
                mean = jnp.mean(out * out, axis=1, keepdims=True)
                normed = out * lax.rsqrt(mean + EPS) * gain * (gate / (1.0 + jnp.exp(-gate)))
                mixed_ref[rows_at, h * DK : (h + 1) * DK] = normed.astype(bf16)
        return carry

    lax.fori_loop(0, n, advance, 0)

    core = lax.rem(me, 2)
    for j in range(n // 2):
        chip = lax.rem(me // 2 + j, n // 2)
        for refs_out, half in ((gives, 1 - core), (keeps, core)):
            at = pl.multiple_of((chip * 2 + half) * tokens, tokens)
            mine = mixed_ref[pl.ds(at, tokens), :]
            width = 512
            for c in range(0, proj_ref.shape[1], width):
                part = mm(mine, proj_ref[:, c : c + width])
                refs_out[j][:, c : c + width] = part.astype(refs_out[j].dtype)


def dispatch_kernel(parts, *refs):
    residual_ref, gain_ref, ids_ref, weight_ref = refs[:4]
    part_refs = refs[4 : 4 + parts]
    hidden_ref, rows_ref, table_ref, flat_ref = refs[4 + parts :]
    tokens, width = hidden_ref.shape
    slots = table_ref.shape[0]
    chunks = width // LANES
    hidden = residual_ref[0].astype(f32)
    for part in part_refs:
        hidden = hidden + part[...].astype(f32)
    hidden_ref[...] = hidden
    mean = jnp.mean(hidden * hidden, axis=1, keepdims=True)
    normed = (hidden * lax.rsqrt(mean + EPS) * gain_ref[...]).astype(bf16)
    slot = iota((slots, tokens), 0)
    expert = slot // CAP
    named = jnp.zeros((slots, tokens), f32)
    weight = jnp.zeros((slots, tokens), f32)
    for j in range(ids_ref.shape[0]):
        hit = ids_ref[j] == expert
        named = named + hit.astype(f32)
        weight = weight + jnp.where(hit, weight_ref[j], 0.0)
    before = (iota((tokens, tokens), 0) < iota((tokens, tokens), 1)).astype(bf16)
    rank = mm(named.astype(bf16), before)
    chosen = jnp.where(rank == lax.rem(slot, CAP).astype(f32), named, 0.0)
    table_ref[...] = chosen * weight
    picker = chosen.astype(bf16)
    step = 512
    for c in range(0, width, step):
        rows = mm(picker, normed[:, c : c + step])
        for i in range(step // LANES):
            flat_ref[pl.ds(c // LANES + i, slots, stride=chunks), :] = rows[:, i * LANES : (i + 1) * LANES]
    rows_ref[...] = flat_ref[...].astype(bf16).reshape(rows_ref.shape)


def expert_kernel(rows_ref, gate_ref, up_ref, down_ref, out_ref, flat_ref, x_ref):
    slots = flat_ref.shape[0] * LANES // x_ref.shape[1]
    width = x_ref.shape[1]
    chunks = width // LANES
    flat_ref[...] = rows_ref[...].reshape(flat_ref.shape).astype(f32)
    for c in range(chunks):
        x_ref[:, c * LANES : (c + 1) * LANES] = flat_ref[pl.ds(c, slots, stride=chunks), :].astype(bf16)
    tile = 128

    def one(t, carry):
        x = x_ref[pl.ds(pl.multiple_of(t * tile, tile), tile), :]
        gate = mm(x, gate_ref[0])
        up = mm(x, up_ref[0])
        act = (gate / (1.0 + jnp.exp(-gate)) * up).astype(bf16)
        step = 512
        for c in range(0, width, step):
            y = mm(act, down_ref[0, :, c : c + step])
            for i in range(step // LANES):
                flat_ref[pl.ds(t * tile * chunks + c // LANES + i, tile, stride=chunks), :] = y[
                    :, i * LANES : (i + 1) * LANES
                ]
        return carry

    lax.fori_loop(0, slots // tile, one, 0)
    out_ref[...] = flat_ref[...].astype(bf16).reshape(out_ref.shape)


def combine_kernel(hidden_ref, table_ref, back_ref, mask_ref, dir_ref, out_ref, flat_ref, ret_ref):
    tokens, width = hidden_ref.shape
    slots = table_ref.shape[0]
    chunks = width // LANES
    flat_ref[...] = back_ref[...].reshape(flat_ref.shape).astype(f32)
    for c in range(chunks):
        got = flat_ref[pl.ds(c, slots, stride=chunks), :].astype(bf16)
        ret_ref[0:slots, c * LANES : (c + 1) * LANES] = got
        ret_ref[slots : 2 * slots, c * LANES : (c + 1) * LANES] = got
    high, low = split2(table_ref[...])
    moe = mm_tn(jnp.concatenate([high, low], axis=0), ret_ref[...])
    combined = hidden_ref[...] + moe
    direction = dir_ref[...]
    unit = direction / jnp.sqrt(jnp.sum(direction * direction, axis=1, keepdims=True) + EPS)
    along = jnp.sum(combined * unit, axis=1, keepdims=True)
    eye = iota((tokens, tokens), 0) == iota((tokens, tokens), 1)
    mask = jnp.sum(jnp.where(eye, mask_ref[...].astype(f32), 0.0), axis=1, keepdims=True)
    out_ref[0] = (combined - (mask * along) * unit).astype(bf16)


def local_part(
    n,
    devices,
    queries,
    keys,
    values,
    out_gate,
    write_rate,
    decay,
    head_gain,
    residual,
    out_proj,
    ffn_gain,
    expert_ids,
    route_weight,
    w_gate,
    w_up,
    w_down,
    ablate_mask,
    direction,
):
    tokens = queries.shape[1]
    heads = write_rate.shape[2]
    width = residual.shape[2]
    kw, vw = keys.shape[2] // n, values.shape[2] // n
    payload = 2 * kw + 2 * vw + LANES
    chips = n // 2
    slots = devices * CAP
    chunks = width // LANES
    shape = jax.ShapeDtypeStruct

    with jax.named_scope("pack"):
        packed = pl.pallas_call(
            functools.partial(pack_kernel, n, kw, vw),
            out_shape=[shape((tokens, payload), bf16)] * n,
            compiler_params=compiler_params(16),
        )(keys, queries, values, out_gate, write_rate.transpose(0, 2, 1), decay.transpose(0, 2, 1))
    with jax.named_scope("heads_exchange"):
        arrived = [packed[0]] + [
            lax.ppermute(packed[s], "ctx", [(i, (i + s) % n) for i in range(n)]) for s in range(1, n)
        ]
    with jax.named_scope("mixer"):
        vmem = pl.BlockSpec(memory_space=pltpu.VMEM)
        local = vw // DK
        outs = pl.pallas_call(
            functools.partial(mixer_kernel, n, heads, kw, vw),
            in_specs=[pl.BlockSpec(memory_space=pl.ANY)] * n + [vmem] * 2,
            out_shape=[shape((tokens, width), f32)] * chips + [shape((tokens, width), bf16)] * chips,
            scratch_shapes=[
                pltpu.VMEM((n, tokens, payload), bf16),
                pltpu.VMEM((n, local, 2, tokens, tokens), bf16),
                pltpu.VMEM((n, local, tokens, tokens), f32),
                pltpu.VMEM((local, DK, DK), f32),
                pltpu.VMEM((n * tokens, vw), bf16),
                pltpu.SemaphoreType.DMA((n,)),
            ],
            compiler_params=compiler_params(40),
        )(*arrived, head_gain.reshape(1, -1), out_proj)
    keeps, gives = outs[:chips], outs[chips:]
    with jax.named_scope("projection_sum"):
        sibling = [(i, i ^ 1) for i in range(n)]
        parts = []
        for j in range(chips - 1, 0, -1):
            pair = keeps[j] + lax.ppermute(gives[j], "ctx", sibling).astype(f32)
            parts.append(lax.ppermute(pair.astype(bf16), "ctx", [(i, (i + 2 * j) % n) for i in range(n)]))
        parts = [keeps[0], lax.ppermute(gives[0], "ctx", sibling)] + parts
    with jax.named_scope("dispatch"):
        hidden, rows, table = pl.pallas_call(
            functools.partial(dispatch_kernel, len(parts)),
            out_shape=[
                shape((tokens, width), f32),
                shape((devices, CAP * chunks, LANES), bf16),
                shape((slots, tokens), f32),
            ],
            scratch_shapes=[pltpu.VMEM((slots * chunks, LANES), f32)],
            compiler_params=compiler_params(48),
        )(
            residual,
            ffn_gain.reshape(1, -1),
            expert_ids.transpose(2, 0, 1),
            route_weight.transpose(2, 0, 1),
            *parts,
        )
    with jax.named_scope("to_experts"):
        came = lax.all_to_all(rows, ("ctx", "exp"), 0, 0, tiled=True)
    with jax.named_scope("experts"):
        done = pl.pallas_call(
            expert_kernel,
            out_shape=shape((devices, CAP * chunks, LANES), bf16),
            scratch_shapes=[pltpu.VMEM((slots * chunks, LANES), f32), pltpu.VMEM((slots, width), bf16)],
            compiler_params=compiler_params(48),
        )(came, w_gate, w_up, w_down)
    with jax.named_scope("from_experts"):
        back = lax.all_to_all(done, ("ctx", "exp"), 0, 0, tiled=True)
    with jax.named_scope("combine"):
        return pl.pallas_call(
            combine_kernel,
            out_shape=shape((1, tokens, width), bf16),
            scratch_shapes=[
                pltpu.VMEM((slots * chunks, LANES), f32),
                pltpu.VMEM((2 * slots, width), bf16),
            ],
            compiler_params=compiler_params(48),
        )(hidden, table, back, ablate_mask, direction.reshape(1, -1))


def solution(mesh):
    seq = P("exp", "ctx", None)
    owned = P(("ctx", "exp"), None, None)
    placed = (
        (seq,) * 6 + (P(), seq, P("ctx", None), P(), seq, seq) + (owned,) * 3 + (P("exp", "ctx"), P())
    )
    n = mesh.shape["ctx"]
    return jax.shard_map(
        functools.partial(local_part, n, n * mesh.shape["exp"]),
        mesh=mesh,
        in_specs=placed,
        out_specs=seq,
        check_vma=False,
    )
```

```python
import functools

import jax
import jax.numpy as jnp
from jax import lax
from jax.experimental import pallas as pl
from jax.experimental.pallas import tpu as pltpu
from jax.sharding import PartitionSpec as P

DK = 128
CAP = 4
EPS = 1e-06
LANES = 128

bf16 = jnp.bfloat16
f32 = jnp.float32


def mm(a, b):
    return jnp.dot(a, b, preferred_element_type=f32)


def mm_nt(a, b):
    return lax.dot_general(a, b, (((1,), (1,)), ((), ())), preferred_element_type=f32)


def mm_tn(a, b):
    return lax.dot_general(a, b, (((0,), (0,)), ((), ())), preferred_element_type=f32)


def split2(x):
    hi = x.astype(bf16)
    return hi, (x - hi.astype(f32)).astype(bf16)


def split3(x):
    hi = x.astype(bf16)
    rest = x - hi.astype(f32)
    mid = rest.astype(bf16)
    return hi, mid, (rest - mid.astype(f32)).astype(bf16)


def mm3(a, b):
    (ah, al), (bh, bl) = a, b
    return mm(jnp.concatenate([ah, al, ah], axis=1), jnp.concatenate([bh, bh, bl], axis=0))


def iota(shape, dim):
    return lax.broadcasted_iota(jnp.int32, shape, dim)


def in_hbm(*arrays):
    return [pltpu.with_memory_space_constraint(a, pltpu.HBM) for a in arrays]


def compiler_params(mib):
    return pltpu.CompilerParams(vmem_limit_bytes=mib * 1024 * 1024)


def pack_kernel(n, kw, vw, k_ref, q_ref, v_ref, g_ref, w_ref, d_ref, *refs):
    keyed, asked, gated = refs[:n], refs[n : 2 * n], refs[2 * n : 3 * n]
    w_in, d_in, small_sems, sems = refs[3 * n :]
    me = lax.axis_index("ctx")
    tokens = k_ref.shape[1]
    heads = d_ref.shape[1]
    small = [
        pltpu.make_async_copy(d_ref.at[0], d_in, small_sems.at[0]),
        pltpu.make_async_copy(w_ref.at[0], w_in, small_sems.at[1]),
    ]
    for copy in small:
        copy.start()
    copies = []
    for step in range(n):
        to = lax.rem(me + step, n)
        kat = pl.ds(pl.multiple_of(to * kw, LANES), kw)
        vat = pl.ds(pl.multiple_of(to * vw, LANES), vw)
        for i, (source, target) in enumerate(
            (
                (k_ref.at[0, :, kat], keyed[step].at[:, 0:kw]),
                (q_ref.at[0, :, kat], asked[step].at[:, 0:kw]),
                (v_ref.at[0, :, vat], asked[step].at[:, kw : kw + vw]),
                (g_ref.at[0, :, vat], gated[step]),
            )
        ):
            copy = pltpu.make_async_copy(source, target, sems.at[step, i])
            copy.start()
            copies.append(copy)
    for copy in small:
        copy.wait()
    ones = (iota((tokens, tokens), 0) <= iota((tokens, tokens), 1)).astype(bf16)
    logs = jnp.log(d_in[...])
    sums = sum(mm(piece, ones) for piece in reversed(split3(logs)))
    pieces = [*split3(sums), *split3(w_in[...])]
    aux = jnp.concatenate([p.astype(f32) for p in pieces], axis=0)
    aux = jnp.concatenate([aux, jnp.zeros((LANES - 6 * heads, tokens), f32)], axis=0).astype(bf16)
    for step in range(n):
        keyed[step][:, kw:] = aux
    for copy in copies:
        copy.wait()


def head_rates(heads, local, me, aux):
    r, l = iota((LANES, LANES), 0), iota((LANES, LANES), 1)
    wanted = me * local + lax.rem(l, local)
    pick = ((lax.rem(r, heads) == wanted) & (l < 2 * local) & (r // heads // 3 == l // local)).astype(bf16)
    return mm_tn(aux, pick), mm_tn(pick, aux)


def inverse_scale(raw):
    raw_f = raw.astype(f32)
    return lax.rsqrt(jnp.sum(raw_f * raw_f, axis=1, keepdims=True) + EPS)


def inverse_kernel(n, heads, kw, local, *refs):
    keyed, inv_ref = refs[:n], refs[n]
    me = lax.axis_index("ctx")
    tokens = keyed[0].shape[0]
    group = local * DK // kw
    row, col = iota((tokens, tokens), 0), iota((tokens, tokens), 1)
    apart = lax.bitwise_xor(row, col)
    eye = (row == col).astype(f32)
    for step in range(n):
        block = lax.rem(me - step + n, n)
        as_cols, as_rows = head_rates(heads, local, me, keyed[step][:, kw:])
        systems = []
        for g in range(local // group):
            k = keyed[step][:, g * DK : (g + 1) * DK]
            dots = mm_nt(k, k)
            diag = dots * eye
            k_row = lax.rsqrt(jnp.sum(diag, axis=0, keepdims=True) + EPS)
            k_col = lax.rsqrt(jnp.sum(diag, axis=1, keepdims=True) + EPS)
            dots = dots * k_row * k_col
            for h in range(g * group, (g + 1) * group):
                gap = as_cols[:, h : h + 1] - as_rows[h : h + 1, :]
                ratios = jnp.exp(jnp.minimum(gap, 0.0))
                write = as_cols[:, local + h : local + h + 1]
                systems.append(jnp.where(row > col, write * ratios * dots, 0.0))
        near = [jnp.where(apart < 16, s, 0.0) for s in systems]
        inverse = [eye - s for s in near]
        power = [split2(s) for s in near]
        for _ in range(3):
            power = [split2(mm3(p, p)) for p in power]
            inverse = [x + mm3(split2(x), p) for x, p in zip(inverse, power)]
        size = 16
        while size < tokens:
            off = [split2(jnp.where((apart >= size) & (apart < 2 * size), s, 0.0)) for s in systems]
            halves = [split2(x) for x in inverse]
            left = [split2(mm3(x, o)) for x, o in zip(halves, off)]
            inverse = [x - mm3(a, xs) for x, a, xs in zip(inverse, left, halves)]
            size *= 2
        for h in range(local):
            hi, lo = split2(inverse[h])
            inv_ref[block, h, 0] = hi
            inv_ref[block, h, 1] = lo


def state_kernel(n, heads, kw, vw, *refs):
    keyed, asked = refs[:n], refs[n : 2 * n]
    inv_ref, gain_ref, out_ref, kx_ref, qv_ref = refs[2 * n :]
    me = lax.axis_index("ctx")
    tokens = keyed[0].shape[0]
    local = vw // DK
    group = vw // kw
    for step in range(n):
        block = lax.rem(me - step + n, n)
        kx_ref[block] = keyed[step][...]
        qv_ref[block] = asked[step][...]
    row, col = iota((tokens, tokens), 0), iota((tokens, tokens), 1)
    gain = gain_ref[...]
    states = [jnp.zeros((DK, DK), f32) for _ in range(local)]
    for block in range(n):
        as_cols, as_rows = head_rates(heads, local, me, kx_ref[block, :, kw:])
        cumulative = jnp.exp(as_cols)
        for g in range(local // group):
            k = kx_ref[block, :, g * DK : (g + 1) * DK]
            q = qv_ref[block, :, g * DK : (g + 1) * DK]
            k_col = inverse_scale(k)
            q_col = inverse_scale(q) * DK ** (-0.5)
            eye = (row == col).astype(f32)
            k_row = jnp.sum(eye * k_col, axis=0, keepdims=True)
            dots = mm_nt(q, k) * k_row * q_col
            both = jnp.concatenate([k, q], axis=0)
            for h in range(g * group, (g + 1) * group):
                gap = as_cols[:, h : h + 1] - as_rows[h : h + 1, :]
                scores = jnp.where(row >= col, jnp.exp(jnp.minimum(gap, 0.0)) * dots, 0.0)
                v = qv_ref[block, :, kw + h * DK : kw + (h + 1) * DK].astype(f32)
                cum = cumulative[:, h : h + 1]
                write = as_cols[:, local + h : local + h + 1]
                rhs = write * v
                if block > 0:
                    high, low = split2(states[h])
                    seen = mm(jnp.concatenate([both, both], axis=1), jnp.concatenate([high, low], axis=0))
                    rhs = rhs - (write * cum * k_col) * seen[:tokens]
                delta = mm3((inv_ref[block, h, 0], inv_ref[block, h, 1]), split2(rhs))
                if block < n - 1:
                    last = as_cols[tokens - 1 : tokens, h : h + 1]
                    kept = jnp.exp(last - as_cols[:, h : h + 1]) * k_col
                    dh, dl = split2(kept * delta)
                    states[h] = jnp.exp(last) * states[h] + mm_tn(
                        jnp.concatenate([k, k], axis=0), jnp.concatenate([dh, dl], axis=0)
                    )
                out = mm3(split2(scores), split2(delta))
                if block > 0:
                    out = out + (cum * q_col) * seen[tokens:]
                mean = jnp.mean(out * out, axis=1, keepdims=True)
                out_ref[block, :, h * DK : (h + 1) * DK] = out * lax.rsqrt(mean + EPS) * gain


def gate_kernel(n, *refs):
    gated = refs[:n]
    normed_ref, proj_hbm, mixed_ref = refs[n : n + 3]
    chips = n // 2
    keeps = refs[n + 3 : n + 2 + chips]
    gives = refs[n + 2 + chips : n + 1 + 2 * chips]
    proj_ref, sem = refs[n + 1 + 2 * chips :]
    copy = pltpu.make_async_copy(proj_hbm, proj_ref, sem)
    copy.start()
    me = lax.axis_index("ctx")
    for step in range(n):
        block = lax.rem(me - step + n, n)
        gate = gated[step][...].astype(f32)
        mixed_ref[block] = (normed_ref[block] * (gate / (1.0 + jnp.exp(-gate)))).astype(bf16)
    copy.wait()
    core = lax.rem(me, 2)
    for j in range(1, chips):
        chip = lax.rem(me // 2 + j, chips)
        project(mixed_ref, chip * 2 + 1 - core, proj_ref, gives[j - 1])
        project(mixed_ref, chip * 2 + core, proj_ref, keeps[j - 1])


def project(mixed_ref, block, proj_ref, out_ref):
    mine = mixed_ref[block]
    width = 512
    for c in range(0, proj_ref.shape[1], width):
        out_ref[:, c : c + width] = mm(mine, proj_ref[:, c : c + width]).astype(out_ref.dtype)


def own_kernel(n, mixed_ref, proj_ref, keep_ref, give_ref):
    me = lax.axis_index("ctx")
    other = lax.bitwise_xor(me, 1)
    project(mixed_ref, other, proj_ref, give_ref)
    project(mixed_ref, me, proj_ref, keep_ref)


def dispatch_kernel(parts, *refs):
    residual_ref, gain_ref, ids_ref, weight_ref = refs[:4]
    part_refs = refs[4 : 4 + parts]
    hidden_ref, rows_ref, table_ref, flat_ref = refs[4 + parts :]
    tokens, width = hidden_ref.shape
    slots = table_ref.shape[0]
    chunks = width // LANES
    hidden = residual_ref[0].astype(f32)
    for part in part_refs:
        hidden = hidden + part[...].astype(f32)
    hidden_ref[...] = hidden
    mean = jnp.mean(hidden * hidden, axis=1, keepdims=True)
    normed = (hidden * lax.rsqrt(mean + EPS) * gain_ref[...]).astype(bf16)
    slot = iota((slots, tokens), 0)
    expert = slot // CAP
    named = jnp.zeros((slots, tokens), f32)
    weight = jnp.zeros((slots, tokens), f32)
    for j in range(ids_ref.shape[0]):
        hit = ids_ref[j] == expert
        named = named + hit.astype(f32)
        weight = weight + jnp.where(hit, weight_ref[j], 0.0)
    before = (iota((tokens, tokens), 0) < iota((tokens, tokens), 1)).astype(bf16)
    rank = mm(named.astype(bf16), before)
    chosen = jnp.where(rank == lax.rem(slot, CAP).astype(f32), named, 0.0)
    table_ref[...] = chosen * weight
    picker = chosen.astype(bf16)
    step = 512
    for c in range(0, width, step):
        rows = mm(picker, normed[:, c : c + step])
        for i in range(step // LANES):
            flat_ref[pl.ds(c // LANES + i, slots, stride=chunks), :] = rows[:, i * LANES : (i + 1) * LANES]
    rows_ref[...] = flat_ref[...].astype(bf16).reshape(rows_ref.shape)


def expert_kernel(rows_ref, gate_ref, up_ref, down_ref, out_ref, flat_ref, x_ref):
    slots = flat_ref.shape[0] * LANES // x_ref.shape[1]
    width = x_ref.shape[1]
    chunks = width // LANES
    flat_ref[...] = rows_ref[...].reshape(flat_ref.shape).astype(f32)
    for c in range(chunks):
        x_ref[:, c * LANES : (c + 1) * LANES] = flat_ref[pl.ds(c, slots, stride=chunks), :].astype(bf16)
    tile = 128

    def one(t, carry):
        x = x_ref[pl.ds(pl.multiple_of(t * tile, tile), tile), :]
        gate = mm(x, gate_ref[0])
        up = mm(x, up_ref[0])
        act = (gate / (1.0 + jnp.exp(-gate)) * up).astype(bf16)
        step = 512
        for c in range(0, width, step):
            y = mm(act, down_ref[0, :, c : c + step])
            for i in range(step // LANES):
                flat_ref[pl.ds(t * tile * chunks + c // LANES + i, tile, stride=chunks), :] = y[
                    :, i * LANES : (i + 1) * LANES
                ]
        return carry

    lax.fori_loop(0, slots // tile, one, 0)
    out_ref[...] = flat_ref[...].astype(bf16).reshape(out_ref.shape)


def combine_kernel(hidden_ref, table_ref, back_ref, mask_ref, dir_ref, out_ref, flat_ref, ret_ref):
    tokens, width = hidden_ref.shape
    slots = table_ref.shape[0]
    chunks = width // LANES
    flat_ref[...] = back_ref[...].reshape(flat_ref.shape).astype(f32)
    for c in range(chunks):
        got = flat_ref[pl.ds(c, slots, stride=chunks), :].astype(bf16)
        ret_ref[0:slots, c * LANES : (c + 1) * LANES] = got
        ret_ref[slots : 2 * slots, c * LANES : (c + 1) * LANES] = got
    high, low = split2(table_ref[...])
    moe = mm_tn(jnp.concatenate([high, low], axis=0), ret_ref[...])
    combined = hidden_ref[...] + moe
    direction = dir_ref[...]
    unit = direction / jnp.sqrt(jnp.sum(direction * direction, axis=1, keepdims=True) + EPS)
    along = jnp.sum(combined * unit, axis=1, keepdims=True)
    eye = iota((tokens, tokens), 0) == iota((tokens, tokens), 1)
    mask = jnp.sum(jnp.where(eye, mask_ref[...].astype(f32), 0.0), axis=1, keepdims=True)
    out_ref[0] = (combined - (mask * along) * unit).astype(bf16)


def local_part(
    n,
    devices,
    queries,
    keys,
    values,
    out_gate,
    write_rate,
    decay,
    head_gain,
    residual,
    out_proj,
    ffn_gain,
    expert_ids,
    route_weight,
    w_gate,
    w_up,
    w_down,
    ablate_mask,
    direction,
):
    tokens = queries.shape[1]
    heads = write_rate.shape[2]
    width = residual.shape[2]
    kw, vw = keys.shape[2] // n, values.shape[2] // n
    chips = n // 2
    slots = devices * CAP
    chunks = width // LANES
    shape = jax.ShapeDtypeStruct

    hbm = pl.BlockSpec(memory_space=pltpu.HBM)
    vmem = pl.BlockSpec(memory_space=pltpu.VMEM)
    local = vw // DK
    with jax.named_scope("pack"):
        packed = pl.pallas_call(
            functools.partial(pack_kernel, n, kw, vw),
            in_specs=[hbm] * 6,
            out_shape=[shape((tokens, kw + LANES), bf16)] * n
            + [shape((tokens, kw + vw), bf16)] * n
            + [shape((tokens, vw), bf16)] * n,
            scratch_shapes=[
                pltpu.VMEM((heads, tokens), f32),
                pltpu.VMEM((heads, tokens), f32),
                pltpu.SemaphoreType.DMA((2,)),
                pltpu.SemaphoreType.DMA((n, 4)),
            ],
            compiler_params=compiler_params(16),
        )(*in_hbm(keys, queries, values, out_gate, write_rate.transpose(0, 2, 1), decay.transpose(0, 2, 1)))
    with jax.named_scope("heads_exchange"):
        far_first = sorted(range(1, n), key=lambda s: (s == 1, s))
        came = {0: packed[:n][0], n: packed[n], 2 * n: packed[2 * n]}
        for first in (0, n, 2 * n):
            for s in far_first:
                route = [(i, (i + s) % n) for i in range(n)]
                came[first + s] = lax.ppermute(packed[first + s], "ctx", route)
        keyed = [came[s] for s in range(n)]
        asked = [came[n + s] for s in range(n)]
        gated = [came[2 * n + s] for s in range(n)]
    with jax.named_scope("block_inverses"):
        inverses = pl.pallas_call(
            functools.partial(inverse_kernel, n, heads, kw, local),
            out_shape=shape((n, local, 2, tokens, tokens), bf16),
            compiler_params=compiler_params(16),
            cost_estimate=pl.CostEstimate(flops=8 * 10**9, bytes_accessed=10**6, transcendentals=0),
        )(*keyed)
    with jax.named_scope("states"):
        normed = pl.pallas_call(
            functools.partial(state_kernel, n, heads, kw, vw),
            out_shape=shape((n, tokens, vw), f32),
            scratch_shapes=[
                pltpu.VMEM((n, tokens, kw + LANES), bf16),
                pltpu.VMEM((n, tokens, kw + vw), bf16),
            ],
            compiler_params=compiler_params(24),
            cost_estimate=pl.CostEstimate(flops=4 * 10**9, bytes_accessed=10**6, transcendentals=0),
        )(*keyed, *asked, inverses, head_gain.reshape(1, -1))
    with jax.named_scope("gates"):
        outs = pl.pallas_call(
            functools.partial(gate_kernel, n),
            in_specs=[vmem] * (n + 1) + [hbm],
            out_shape=[shape((n, tokens, vw), bf16)]
            + [shape((tokens, width), f32)] * (chips - 1)
            + [shape((tokens, width), bf16)] * (chips - 1),
            scratch_shapes=[pltpu.VMEM(out_proj.shape, bf16), pltpu.SemaphoreType.DMA],
            compiler_params=compiler_params(24),
        )(*gated, normed, *in_hbm(out_proj))
    mixed, keeps, gives = outs[0], outs[1:chips], outs[chips:]
    with jax.named_scope("own_projection"):
        keep, give = pl.pallas_call(
            functools.partial(own_kernel, n),
            out_shape=[shape((tokens, width), f32), shape((tokens, width), bf16)],
            compiler_params=compiler_params(24),
            cost_estimate=pl.CostEstimate(flops=2 * 10**9, bytes_accessed=10**6, transcendentals=0),
        )(mixed, out_proj)
    with jax.named_scope("projection_sum"):
        sibling = [(i, i ^ 1) for i in range(n)]
        parts = []
        for j in range(chips - 1, 0, -1):
            pair = keeps[j - 1] + lax.ppermute(gives[j - 1], "ctx", sibling).astype(f32)
            parts.append(lax.ppermute(pair.astype(bf16), "ctx", [(i, (i + 2 * j) % n) for i in range(n)]))
        parts = [keep, lax.ppermute(give, "ctx", sibling)] + parts
    with jax.named_scope("dispatch"):
        hidden, rows, table = pl.pallas_call(
            functools.partial(dispatch_kernel, len(parts)),
            out_shape=[
                shape((tokens, width), f32),
                shape((devices, CAP * chunks, LANES), bf16),
                shape((slots, tokens), f32),
            ],
            scratch_shapes=[pltpu.VMEM((slots * chunks, LANES), f32)],
            compiler_params=compiler_params(48),
        )(
            residual,
            ffn_gain.reshape(1, -1),
            expert_ids.transpose(2, 0, 1),
            route_weight.transpose(2, 0, 1),
            *parts,
        )
    with jax.named_scope("to_experts"):
        came = lax.all_to_all(rows, ("ctx", "exp"), 0, 0, tiled=True)
    with jax.named_scope("experts"):
        done = pl.pallas_call(
            expert_kernel,
            out_shape=shape((devices, CAP * chunks, LANES), bf16),
            scratch_shapes=[pltpu.VMEM((slots * chunks, LANES), f32), pltpu.VMEM((slots, width), bf16)],
            compiler_params=compiler_params(48),
        )(came, w_gate, w_up, w_down)
    with jax.named_scope("from_experts"):
        back = lax.all_to_all(done, ("ctx", "exp"), 0, 0, tiled=True)
    with jax.named_scope("combine"):
        return pl.pallas_call(
            combine_kernel,
            out_shape=shape((1, tokens, width), bf16),
            scratch_shapes=[
                pltpu.VMEM((slots * chunks, LANES), f32),
                pltpu.VMEM((2 * slots, width), bf16),
            ],
            compiler_params=compiler_params(48),
        )(hidden, table, back, ablate_mask, direction.reshape(1, -1))


def solution(mesh):
    seq = P("exp", "ctx", None)
    owned = P(("ctx", "exp"), None, None)
    placed = (
        (seq,) * 6 + (P(), seq, P("ctx", None), P(), seq, seq) + (owned,) * 3 + (P("exp", "ctx"), P())
    )
    n = mesh.shape["ctx"]
    return jax.shard_map(
        functools.partial(local_part, n, n * mesh.shape["exp"]),
        mesh=mesh,
        in_specs=placed,
        out_specs=seq,
        check_vma=False,
    )
```

```python
import functools

import jax
import jax.numpy as jnp
from jax import lax
from jax.experimental import pallas as pl
from jax.experimental.pallas import tpu as pltpu
from jax.sharding import PartitionSpec as P

DK = 128
CAP = 4
EPS = 1e-06
AUX = 16
LANES = 128

bf16 = jnp.bfloat16
f32 = jnp.float32


def mm(a, b):
    return jnp.dot(a, b, preferred_element_type=f32)


def mm_nt(a, b):
    return lax.dot_general(a, b, (((1,), (1,)), ((), ())), preferred_element_type=f32)


def mm_tn(a, b):
    return lax.dot_general(a, b, (((0,), (0,)), ((), ())), preferred_element_type=f32)


def split2(x):
    hi = x.astype(bf16)
    return hi, (x - hi.astype(f32)).astype(bf16)


def split3(x):
    hi = x.astype(bf16)
    rest = x - hi.astype(f32)
    mid = rest.astype(bf16)
    return hi, mid, (rest - mid.astype(f32)).astype(bf16)


def mm3(a, b):
    (ah, al), (bh, bl) = a, b
    return mm(jnp.concatenate([ah, al, ah], axis=1), jnp.concatenate([bh, bh, bl], axis=0))


def iota(shape, dim):
    return lax.broadcasted_iota(jnp.int32, shape, dim)


def in_hbm(*arrays):
    return [pltpu.with_memory_space_constraint(a, pltpu.HBM) for a in arrays]


def compiler_params(mib):
    return pltpu.CompilerParams(vmem_limit_bytes=mib * 1024 * 1024)


def routes(n):
    return [(chips, flip) for chips in range(n // 2) for flip in (0, 1)]


def moved(index, route, n, back=False):
    chips, flip = route
    chip = lax.rem(index // 2 + (n // 2 - chips if back else chips), n // 2)
    return chip * 2 + lax.rem(lax.rem(index, 2) + flip, 2)


def send(x, route, n):
    chips, flip = route
    pairs = [(i, (i // 2 + chips) % (n // 2) * 2 + (i % 2 + flip) % 2) for i in range(n)]
    return lax.ppermute(x, "ctx", pairs)


def pack_kernel(n, kw, vw, k_ref, q_ref, v_ref, g_ref, w_ref, d_ref, *outs):
    me = lax.axis_index("ctx")
    tokens = k_ref.shape[1]
    heads = d_ref.shape[1]
    local = vw // DK
    ones = (iota((tokens, tokens), 0) <= iota((tokens, tokens), 1)).astype(bf16)
    logs = jnp.log(d_ref[0])
    sums = sum(mm(piece, ones) for piece in reversed(split3(logs)))
    pieces = [p.astype(f32) for p in (*split3(sums), *split3(w_ref[0]))]
    rates = jnp.concatenate(pieces, axis=0).astype(bf16)
    rows = AUX * kw // LANES
    row, entry = iota((rows, 6 * heads), 0), iota((rows, 6 * heads), 1)
    outs = list(outs)
    for route in routes(n):
        to = moved(me, route, n)
        kat = pl.ds(pl.multiple_of(to * kw, LANES), kw)
        vat = pl.ds(pl.multiple_of(to * vw, LANES), vw)
        keyed = outs.pop(0)
        keyed[0:tokens] = k_ref[0, :, kat]
        wanted = row // local * heads + to * local + lax.rem(row, local)
        aux = mm(((row < 6 * local) & (entry == wanted)).astype(bf16), rates)
        for i in range(kw // LANES):
            keyed[tokens:, i * LANES : (i + 1) * LANES] = aux[i * AUX : (i + 1) * AUX].astype(bf16)
        asked = outs.pop(0)
        asked[:, 0:kw] = q_ref[0, :, kat]
        asked[:, kw : kw + vw] = v_ref[0, :, vat]
        if route[0] == 0:
            asked[:, kw + vw :] = g_ref[0, :, vat]
        else:
            outs.pop(0)[...] = g_ref[0, :, vat]


def head_rates(local, keyed, tokens):
    aux = jnp.concatenate(
        [keyed[tokens:, i * LANES : (i + 1) * LANES] for i in range(keyed.shape[1] // LANES)], axis=0
    )
    row, col = iota((aux.shape[0], LANES), 0), iota((aux.shape[0], LANES), 1)
    total = (
        (row < 6 * local) & (col < 2 * local) & (lax.rem(row, local) == lax.rem(col, local)) & (row // (3 * local) == col // local)
    ).astype(bf16)
    return mm_tn(aux, total), mm_tn(total, aux)


def inverse_scale(raw):
    raw_f = raw.astype(f32)
    return lax.rsqrt(jnp.sum(raw_f * raw_f, axis=1, keepdims=True) + EPS)


def inverse_kernel(n, local, *refs):
    keyed, inv_ref = refs[:n], refs[n]
    me = lax.axis_index("ctx")
    tokens = inv_ref.shape[-1]
    group = local * DK // keyed[0].shape[1]
    row, col = iota((tokens, tokens), 0), iota((tokens, tokens), 1)
    apart = lax.bitwise_xor(row, col)
    eye = (row == col).astype(f32)
    systems = []
    for piece in keyed:
        as_cols, as_rows = head_rates(local, piece, tokens)
        for g in range(local // group):
            k = piece[0:tokens, g * DK : (g + 1) * DK]
            dots = mm_nt(k, k)
            diag = dots * eye
            k_row = lax.rsqrt(jnp.sum(diag, axis=0, keepdims=True) + EPS)
            k_col = lax.rsqrt(jnp.sum(diag, axis=1, keepdims=True) + EPS)
            dots = jnp.where(row > col, dots * k_row * k_col, 0.0)
            for h in range(g * group, (g + 1) * group):
                gap = as_cols[:, h : h + 1] - as_rows[h : h + 1, :]
                write = as_cols[:, local + h : local + h + 1]
                systems.append(write * jnp.exp(jnp.minimum(gap, 0.0)) * dots)
    near = [jnp.where(apart < 16, s, 0.0) for s in systems]
    power = [split2(s) for s in near]
    inverse = [eye - s for s in near]
    power = [mm3(p, p) for p in power]
    for _ in range(2):
        halves = [split2(p) for p in power]
        both = [mm3(split2(jnp.concatenate([p, x], axis=0)), ps) for p, x, ps in zip(power, inverse, halves)]
        power = [b[:tokens] for b in both]
        inverse = [x + b[tokens:] for x, b in zip(inverse, both)]
    inverse = [x + mm3(split2(x), split2(p)) for x, p in zip(inverse, power)]
    size = 16
    while size < tokens:
        odd = [slice(at, at + size) for at in range(size, tokens, 2 * size)]
        beside = (apart >= size) & (apart < 2 * size)
        below = [jnp.where(beside, s, 0.0) for s in systems]
        below = [split2(jnp.concatenate([b[o] for o in odd], axis=0)) for b in below]
        halves = [split2(x) for x in inverse]
        first = [mm3(b, x) for b, x in zip(below, halves)]
        first = [split2(widen(f, size)) for f in first]
        lower = [tuple(jnp.concatenate([part[o] for o in odd], axis=0) for part in x) for x in halves]
        inverse = [x - widen(mm3(a, b), size) for x, a, b in zip(inverse, lower, first)]
        size *= 2
    for i, route in enumerate(routes(n)):
        block = moved(me, route, n, back=True)
        for h in range(local):
            hi, lo = split2(inverse[i * local + h])
            inv_ref[block, h, 0] = hi
            inv_ref[block, h, 1] = lo


def widen(x, size):
    none = jnp.zeros((size, x.shape[1]), x.dtype)
    return jnp.concatenate(
        [part for at in range(0, x.shape[0], size) for part in (none, x[at : at + size])], axis=0
    )


def state_kernel(n, kw, vw, *refs):
    keyed, asked = refs[:n], refs[n : 2 * n]
    inv_ref, gain_ref, out_ref, kx_ref, qv_ref = refs[2 * n :]
    me = lax.axis_index("ctx")
    tokens = inv_ref.shape[-1]
    local = vw // DK
    group = vw // kw
    all_heads = range(local)
    for i, route in enumerate(routes(n)):
        block = moved(me, route, n, back=True)
        kx_ref[block] = keyed[i][...]
        qv_ref[block] = asked[i][:, 0 : kw + vw]
    row, col = iota((tokens, tokens), 0), iota((tokens, tokens), 1)
    eye = (row == col).astype(f32)
    gain = gain_ref[...]

    def prepare(block):
        as_cols, as_rows = head_rates(local, kx_ref.at[block], tokens)
        cumulative = jnp.exp(as_cols)
        last = as_cols[tokens - 1 : tokens]
        ends = jnp.exp(last)
        kept = jnp.exp(last - as_cols)
        made = []
        for g in range(local // group):
            k = kx_ref[block, 0:tokens, g * DK : (g + 1) * DK]
            q = qv_ref[block, :, g * DK : (g + 1) * DK]
            k_col = inverse_scale(k)
            q_col = inverse_scale(q) * DK ** (-0.5)
            k_row = jnp.sum(eye * k_col, axis=0, keepdims=True)
            dots = jnp.where(row >= col, mm_nt(q, k) * k_row * q_col, 0.0)
            for h in range(g * group, (g + 1) * group):
                gap = as_cols[:, h : h + 1] - as_rows[h : h + 1, :]
                scores = split2(jnp.exp(jnp.minimum(gap, 0.0)) * dots)
                write = as_cols[:, local + h : local + h + 1]
                cum = cumulative[:, h : h + 1]
                made.append(
                    dict(
                        k=k,
                        q=q,
                        scores=scores,
                        write=write,
                        erase=write * cum * k_col,
                        ask=cum * q_col,
                        kept=kept[:, h : h + 1] * k_col,
                        end=ends[:, h : h + 1],
                    )
                )
        return made

    def finish(block, made, seen, delta):
        for h in all_heads:
            out = mm3(made[h]["scores"], delta[h])
            if block > 0:
                out = out + made[h]["ask"] * seen[h][tokens:]
            mean = jnp.mean(out * out, axis=1, keepdims=True)
            out_ref[block, :, h * DK : (h + 1) * DK] = out * lax.rsqrt(mean + EPS) * gain

    states, before, made = None, None, prepare(0)
    for block in range(n):
        rhs = [
            m["write"] * qv_ref[block, :, kw + h * DK : kw + (h + 1) * DK].astype(f32) for h, m in enumerate(made)
        ]
        seen = None
        if block > 0:
            both = [jnp.concatenate([m["k"], m["q"]], axis=0) for m in made]
            seen = [
                mm(jnp.concatenate([b, b], axis=1), jnp.concatenate(split2(s), axis=0)) for b, s in zip(both, states)
            ]
        if before is not None:
            finish(*before)
        if block > 0:
            rhs = [r - m["erase"] * s[:tokens] for r, m, s in zip(rhs, made, seen)]
        delta = [mm3((inv_ref[block, h, 0], inv_ref[block, h, 1]), split2(rhs[h])) for h in all_heads]
        later = prepare(block + 1) if block < n - 1 else None
        if block < n - 1:
            grown = [
                mm_tn(jnp.concatenate([m["k"], m["k"]], axis=0), jnp.concatenate(split2(m["kept"] * d), axis=0))
                for m, d in zip(made, delta)
            ]
            states = grown if block == 0 else [m["end"] * s + g for m, s, g in zip(made, states, grown)]
        before = (block, made, seen, [split2(d) for d in delta])
        made = later
    finish(*before)


def gate_kernel(n, *refs):
    gated = refs[:n]
    normed_ref, proj_ref, mixed_ref = refs[n : n + 3]
    chips = n // 2
    keeps = refs[n + 3 : n + 2 + chips]
    gives = refs[n + 2 + chips :]
    me = lax.axis_index("ctx")
    vw = mixed_ref.shape[2]
    for i, route in enumerate(routes(n)):
        block = moved(me, route, n, back=True)
        gate = gated[i][:, gated[i].shape[1] - vw :].astype(f32)
        mixed_ref[block] = (normed_ref[block] * (gate / (1.0 + jnp.exp(-gate)))).astype(bf16)
    for j in range(1, chips):
        project(mixed_ref, moved(me, (j, 1), n), proj_ref, gives[j - 1])
        project(mixed_ref, moved(me, (j, 0), n), proj_ref, keeps[j - 1])


def project(mixed_ref, block, proj_ref, out_ref):
    mine = mixed_ref[block]
    width = 512
    for c in range(0, proj_ref.shape[1], width):
        out_ref[:, c : c + width] = mm(mine, proj_ref[:, c : c + width]).astype(out_ref.dtype)


def own_kernel(n, mixed_ref, proj_ref, keep_ref, give_ref):
    me = lax.axis_index("ctx")
    project(mixed_ref, moved(me, (0, 1), n), proj_ref, give_ref)
    project(mixed_ref, me, proj_ref, keep_ref)


def dispatch_kernel(parts, *refs):
    residual_ref, gain_ref, ids_ref, weight_ref = refs[:4]
    part_refs = refs[4 : 4 + parts]
    hidden_ref, rows_ref, table_ref, flat_ref = refs[4 + parts :]
    tokens, width = hidden_ref.shape
    slots = table_ref.shape[0]
    chunks = width // LANES
    hidden = residual_ref[0].astype(f32)
    for part in part_refs:
        hidden = hidden + part[...].astype(f32)
    hidden_ref[...] = hidden
    mean = jnp.mean(hidden * hidden, axis=1, keepdims=True)
    normed = (hidden * lax.rsqrt(mean + EPS) * gain_ref[...]).astype(bf16)
    slot = iota((slots, tokens), 0)
    expert = slot // CAP
    named = jnp.zeros((slots, tokens), f32)
    weight = jnp.zeros((slots, tokens), f32)
    for j in range(ids_ref.shape[0]):
        hit = ids_ref[j] == expert
        named = named + hit.astype(f32)
        weight = weight + jnp.where(hit, weight_ref[j], 0.0)
    before = (iota((tokens, tokens), 0) < iota((tokens, tokens), 1)).astype(bf16)
    rank = mm(named.astype(bf16), before)
    chosen = jnp.where(rank == lax.rem(slot, CAP).astype(f32), named, 0.0)
    table_ref[...] = chosen * weight
    picker = chosen.astype(bf16)
    step = 512
    for c in range(0, width, step):
        rows = mm(picker, normed[:, c : c + step])
        for i in range(step // LANES):
            flat_ref[pl.ds(c // LANES + i, slots, stride=chunks), :] = rows[:, i * LANES : (i + 1) * LANES]
    rows_ref[...] = flat_ref[...].astype(bf16).reshape(rows_ref.shape)


def expert_kernel(rows_ref, gate_ref, up_ref, down_ref, out_ref, flat_ref, x_ref):
    slots = flat_ref.shape[0] * LANES // x_ref.shape[1]
    width = x_ref.shape[1]
    chunks = width // LANES
    flat_ref[...] = rows_ref[...].reshape(flat_ref.shape).astype(f32)
    for c in range(chunks):
        x_ref[:, c * LANES : (c + 1) * LANES] = flat_ref[pl.ds(c, slots, stride=chunks), :].astype(bf16)
    tile = 128

    def one(t, carry):
        x = x_ref[pl.ds(pl.multiple_of(t * tile, tile), tile), :]
        gate = mm(x, gate_ref[0])
        up = mm(x, up_ref[0])
        act = (gate / (1.0 + jnp.exp(-gate)) * up).astype(bf16)
        step = 512
        for c in range(0, width, step):
            y = mm(act, down_ref[0, :, c : c + step])
            for i in range(step // LANES):
                flat_ref[pl.ds(t * tile * chunks + c // LANES + i, tile, stride=chunks), :] = y[
                    :, i * LANES : (i + 1) * LANES
                ]
        return carry

    lax.fori_loop(0, slots // tile, one, 0)
    out_ref[...] = flat_ref[...].astype(bf16).reshape(out_ref.shape)


def combine_kernel(hidden_ref, table_ref, back_ref, mask_ref, dir_ref, out_ref, flat_ref, ret_ref):
    tokens, width = hidden_ref.shape
    slots = table_ref.shape[0]
    chunks = width // LANES
    flat_ref[...] = back_ref[...].reshape(flat_ref.shape).astype(f32)
    for c in range(chunks):
        got = flat_ref[pl.ds(c, slots, stride=chunks), :].astype(bf16)
        ret_ref[0:slots, c * LANES : (c + 1) * LANES] = got
        ret_ref[slots : 2 * slots, c * LANES : (c + 1) * LANES] = got
    high, low = split2(table_ref[...])
    moe = mm_tn(jnp.concatenate([high, low], axis=0), ret_ref[...])
    combined = hidden_ref[...] + moe
    direction = dir_ref[...]
    unit = direction / jnp.sqrt(jnp.sum(direction * direction, axis=1, keepdims=True) + EPS)
    along = jnp.sum(combined * unit, axis=1, keepdims=True)
    eye = iota((tokens, tokens), 0) == iota((tokens, tokens), 1)
    mask = jnp.sum(jnp.where(eye, mask_ref[...].astype(f32), 0.0), axis=1, keepdims=True)
    out_ref[0] = (combined - (mask * along) * unit).astype(bf16)


def local_part(
    n,
    devices,
    queries,
    keys,
    values,
    out_gate,
    write_rate,
    decay,
    head_gain,
    residual,
    out_proj,
    ffn_gain,
    expert_ids,
    route_weight,
    w_gate,
    w_up,
    w_down,
    ablate_mask,
    direction,
):
    tokens = queries.shape[1]
    width = residual.shape[2]
    kw, vw = keys.shape[2] // n, values.shape[2] // n
    chips = n // 2
    slots = devices * CAP
    chunks = width // LANES
    shape = jax.ShapeDtypeStruct

    local = vw // DK
    ways = routes(n)
    keyed_shape = shape((tokens + AUX, kw), bf16)
    with jax.named_scope("pack"):
        packed = pl.pallas_call(
            functools.partial(pack_kernel, n, kw, vw),
            out_shape=[
                out
                for route in ways
                for out in (
                    [keyed_shape, shape((tokens, kw + 2 * vw), bf16)]
                    if route[0] == 0
                    else [keyed_shape, shape((tokens, kw + vw), bf16), shape((tokens, vw), bf16)]
                )
            ],
            compiler_params=compiler_params(16),
        )(*in_hbm(keys, queries, values, out_gate, write_rate.transpose(0, 2, 1), decay.transpose(0, 2, 1)))
    with jax.named_scope("heads_exchange"):
        packed = list(packed)
        keyed, asked, gated = [], [], []
        for route in ways:
            keyed.append(packed.pop(0))
            asked.append(packed.pop(0))
            gated.append(packed.pop(0) if route[0] else None)
        order = [i for i, route in enumerate(ways) if route[0]] + [1]
        for i in order:
            keyed[i] = send(keyed[i], ways[i], n)
        for i in order[:-1]:
            asked[i] = send(asked[i], ways[i], n)
        keyed, late = lax.optimization_barrier((keyed, [asked[1]] + [gated[i] for i in order[:-1]]))
        asked[1] = send(late[0], ways[1], n)
        for i, gate in zip(order[:-1], late[1:]):
            gated[i] = send(gate, ways[i], n)
        gated[:2] = asked[:2]
    with jax.named_scope("block_inverses"):
        inverses = pl.pallas_call(
            functools.partial(inverse_kernel, n, local),
            out_shape=shape((n, local, 2, tokens, tokens), bf16),
            compiler_params=compiler_params(16),
            cost_estimate=pl.CostEstimate(flops=6 * 10**9, bytes_accessed=10**6, transcendentals=0),
        )(*keyed)
    with jax.named_scope("states"):
        normed = pl.pallas_call(
            functools.partial(state_kernel, n, kw, vw),
            out_shape=shape((n, tokens, vw), f32),
            scratch_shapes=[
                pltpu.VMEM((n, tokens + AUX, kw), bf16),
                pltpu.VMEM((n, tokens, kw + vw), bf16),
            ],
            compiler_params=compiler_params(16),
            cost_estimate=pl.CostEstimate(flops=4 * 10**9, bytes_accessed=10**6, transcendentals=0),
        )(*keyed, *asked, inverses, head_gain.reshape(1, -1))
    with jax.named_scope("gates"):
        outs = pl.pallas_call(
            functools.partial(gate_kernel, n),
            out_shape=[shape((n, tokens, vw), bf16)]
            + [shape((tokens, width), f32)] * (chips - 1)
            + [shape((tokens, width), bf16)] * (chips - 1),
            compiler_params=compiler_params(16),
        )(*gated, normed, out_proj)
    mixed, keeps, gives = outs[0], outs[1:chips], outs[chips:]
    with jax.named_scope("own_projection"):
        keep, give = pl.pallas_call(
            functools.partial(own_kernel, n),
            out_shape=[shape((tokens, width), f32), shape((tokens, width), bf16)],
            compiler_params=compiler_params(16),
            cost_estimate=pl.CostEstimate(flops=2 * 10**9, bytes_accessed=10**6, transcendentals=0),
        )(mixed, out_proj)
    with jax.named_scope("projection_sum"):
        parts = []
        for j in range(chips - 1, 0, -1):
            pair = keeps[j - 1] + send(gives[j - 1], (0, 1), n).astype(f32)
            parts.append(send(pair.astype(bf16), (j, 0), n))
        parts = [keep, send(give, (0, 1), n)] + parts
    with jax.named_scope("dispatch"):
        hidden, rows, table = pl.pallas_call(
            functools.partial(dispatch_kernel, len(parts)),
            out_shape=[
                shape((tokens, width), f32),
                shape((devices, CAP * chunks, LANES), bf16),
                shape((slots, tokens), f32),
            ],
            scratch_shapes=[pltpu.VMEM((slots * chunks, LANES), f32)],
            compiler_params=compiler_params(24),
        )(
            residual,
            ffn_gain.reshape(1, -1),
            expert_ids.transpose(2, 0, 1),
            route_weight.transpose(2, 0, 1),
            *parts,
        )
    with jax.named_scope("to_experts"):
        came = lax.all_to_all(rows, ("ctx", "exp"), 0, 0, tiled=True)
    with jax.named_scope("experts"):
        done = pl.pallas_call(
            expert_kernel,
            out_shape=shape((devices, CAP * chunks, LANES), bf16),
            scratch_shapes=[pltpu.VMEM((slots * chunks, LANES), f32), pltpu.VMEM((slots, width), bf16)],
            compiler_params=compiler_params(24),
        )(came, w_gate, w_up, w_down)
    with jax.named_scope("from_experts"):
        back = lax.all_to_all(done, ("ctx", "exp"), 0, 0, tiled=True)
    with jax.named_scope("combine"):
        return pl.pallas_call(
            combine_kernel,
            out_shape=shape((1, tokens, width), bf16),
            scratch_shapes=[
                pltpu.VMEM((slots * chunks, LANES), f32),
                pltpu.VMEM((2 * slots, width), bf16),
            ],
            compiler_params=compiler_params(24),
        )(hidden, table, back, ablate_mask, direction.reshape(1, -1))


def solution(mesh):
    seq = P("exp", "ctx", None)
    owned = P(("ctx", "exp"), None, None)
    placed = (
        (seq,) * 6 + (P(), seq, P("ctx", None), P(), seq, seq) + (owned,) * 3 + (P("exp", "ctx"), P())
    )
    n = mesh.shape["ctx"]
    return jax.shard_map(
        functools.partial(local_part, n, n * mesh.shape["exp"]),
        mesh=mesh,
        in_specs=placed,
        out_specs=seq,
        check_vma=False,
    )
```

```python
import functools

import jax
import jax.numpy as jnp
from jax import lax
from jax.experimental import pallas as pl
from jax.experimental.pallas import tpu as pltpu
from jax.sharding import PartitionSpec as P

DK = 128
CAP = 4
EPS = 1e-06
AUX = 16
LANES = 128

bf16 = jnp.bfloat16
f32 = jnp.float32


def mm(a, b):
    return jnp.dot(a, b, preferred_element_type=f32)


def mm_nt(a, b):
    return lax.dot_general(a, b, (((1,), (1,)), ((), ())), preferred_element_type=f32)


def mm_tn(a, b):
    return lax.dot_general(a, b, (((0,), (0,)), ((), ())), preferred_element_type=f32)


def split2(x):
    hi = x.astype(bf16)
    return hi, (x - hi.astype(f32)).astype(bf16)


def split3(x):
    hi = x.astype(bf16)
    rest = x - hi.astype(f32)
    mid = rest.astype(bf16)
    return hi, mid, (rest - mid.astype(f32)).astype(bf16)


def mm3(a, b):
    (ah, al), (bh, bl) = a, b
    return mm(jnp.concatenate([ah, al, ah], axis=1), jnp.concatenate([bh, bh, bl], axis=0))


def iota(shape, dim):
    return lax.broadcasted_iota(jnp.int32, shape, dim)


def in_hbm(*arrays):
    return [pltpu.with_memory_space_constraint(a, pltpu.HBM) for a in arrays]


def compiler_params(mib):
    return pltpu.CompilerParams(vmem_limit_bytes=mib * 1024 * 1024)


def routes(n):
    return [(chips, flip) for chips in range(n // 2) for flip in (0, 1)]


def moved(index, route, n, back=False):
    chips, flip = route
    chip = lax.rem(index // 2 + (n // 2 - chips if back else chips), n // 2)
    return chip * 2 + lax.rem(lax.rem(index, 2) + flip, 2)


def send(x, route, n):
    chips, flip = route
    pairs = [(i, (i // 2 + chips) % (n // 2) * 2 + (i % 2 + flip) % 2) for i in range(n)]
    return lax.ppermute(x, "ctx", pairs)


def pack_kernel(n, kw, vw, k_ref, w_ref, d_ref, q_ref, v_ref, g_ref, *outs):
    local = vw // DK
    keyed, asked, gated = outs[:n], outs[n : 2 * n], outs[2 * n :]
    me = lax.axis_index("ctx")
    tokens = k_ref.shape[1]
    heads = d_ref.shape[1]
    ones = (iota((tokens, tokens), 0) <= iota((tokens, tokens), 1)).astype(bf16)
    logs = jnp.log(d_ref[0])
    sums = sum(mm(piece, ones) for piece in reversed(split3(logs)))
    pieces = [p.astype(f32) for p in (*split3(sums), *split3(w_ref[0]))]
    rates = jnp.concatenate(pieces, axis=0).astype(bf16)
    rows = AUX * kw // LANES
    row, entry = iota((rows, 6 * heads), 0), iota((rows, 6 * heads), 1)
    for i, route in enumerate(routes(n)):
        to = moved(me, route, n)
        kat = pl.ds(pl.multiple_of(to * kw, LANES), kw)
        keyed[i][0:tokens] = k_ref[0, :, kat]
        wanted = row // local * heads + to * local + lax.rem(row, local)
        aux = mm(((row < 6 * local) & (entry == wanted)).astype(bf16), rates)
        for at in range(kw // LANES):
            keyed[i][tokens:, at * LANES : (at + 1) * LANES] = aux[at * AUX : (at + 1) * AUX].astype(bf16)
        asked[i][:, 0:kw] = q_ref[0, :, kat]
        asked[i][:, kw:] = v_ref[0, :, pl.ds(pl.multiple_of(to * vw, LANES), vw)]
    for j, out in enumerate(gated):
        chip = lax.rem(me // 2 + j + 1, n // 2)
        out[...] = g_ref[0, :, pl.ds(pl.multiple_of(chip * 2 * vw, LANES), 2 * vw)]


def head_rates(local, keyed, tokens):
    aux = jnp.concatenate(
        [keyed[tokens:, i * LANES : (i + 1) * LANES] for i in range(keyed.shape[1] // LANES)], axis=0
    )
    row, col = iota((aux.shape[0], LANES), 0), iota((aux.shape[0], LANES), 1)
    total = (
        (row < 6 * local) & (col < 2 * local) & (lax.rem(row, local) == lax.rem(col, local)) & (row // (3 * local) == col // local)
    ).astype(bf16)
    return mm_tn(aux, total), mm_tn(total, aux)


def inverse_scale(raw):
    raw_f = raw.astype(f32)
    return lax.rsqrt(jnp.sum(raw_f * raw_f, axis=1, keepdims=True) + EPS)


def inverse_kernel(n, local, *refs):
    keyed, inv_ref = refs[:n], refs[n]
    me = lax.axis_index("ctx")
    tokens = inv_ref.shape[-1]
    group = local * DK // keyed[0].shape[1]
    row, col = iota((tokens, tokens), 0), iota((tokens, tokens), 1)
    apart = lax.bitwise_xor(row, col)
    eye = (row == col).astype(f32)
    systems = []
    for piece in keyed:
        as_cols, as_rows = head_rates(local, piece, tokens)
        for g in range(local // group):
            k = piece[0:tokens, g * DK : (g + 1) * DK]
            dots = mm_nt(k, k)
            diag = dots * eye
            k_row = lax.rsqrt(jnp.sum(diag, axis=0, keepdims=True) + EPS)
            k_col = lax.rsqrt(jnp.sum(diag, axis=1, keepdims=True) + EPS)
            dots = jnp.where(row > col, dots * k_row * k_col, 0.0)
            for h in range(g * group, (g + 1) * group):
                gap = as_cols[:, h : h + 1] - as_rows[h : h + 1, :]
                write = as_cols[:, local + h : local + h + 1]
                systems.append(write * jnp.exp(jnp.minimum(gap, 0.0)) * dots)
    near = [jnp.where(apart < 16, s, 0.0) for s in systems]
    power = [split2(s) for s in near]
    inverse = [eye - s for s in near]
    power = [mm3(p, p) for p in power]
    for _ in range(2):
        halves = [split2(p) for p in power]
        both = [mm3(split2(jnp.concatenate([p, x], axis=0)), ps) for p, x, ps in zip(power, inverse, halves)]
        power = [b[:tokens] for b in both]
        inverse = [x + b[tokens:] for x, b in zip(inverse, both)]
    inverse = [x + mm3(split2(x), split2(p)) for x, p in zip(inverse, power)]
    size = 16
    while size < tokens:
        odd = [slice(at, at + size) for at in range(size, tokens, 2 * size)]
        beside = (apart >= size) & (apart < 2 * size)
        below = [jnp.where(beside, s, 0.0) for s in systems]
        below = [split2(jnp.concatenate([b[o] for o in odd], axis=0)) for b in below]
        halves = [split2(x) for x in inverse]
        first = [mm3(b, x) for b, x in zip(below, halves)]
        first = [split2(widen(f, size)) for f in first]
        lower = [tuple(jnp.concatenate([part[o] for o in odd], axis=0) for part in x) for x in halves]
        inverse = [x - widen(mm3(a, b), size) for x, a, b in zip(inverse, lower, first)]
        size *= 2
    for i, route in enumerate(routes(n)):
        block = moved(me, route, n, back=True)
        for h in range(local):
            hi, lo = split2(inverse[i * local + h])
            inv_ref[block, h, 0] = hi
            inv_ref[block, h, 1] = lo


def widen(x, size):
    none = jnp.zeros((size, x.shape[1]), x.dtype)
    return jnp.concatenate(
        [part for at in range(0, x.shape[0], size) for part in (none, x[at : at + size])], axis=0
    )


def state_kernel(n, kw, vw, *refs):
    keyed, asked = refs[:n], refs[n : 2 * n]
    inv_ref, gain_ref, keep_ref, give_ref, out_ref, kx_ref, qv_ref = refs[2 * n :]
    me = lax.axis_index("ctx")
    tokens = inv_ref.shape[-1]
    local = vw // DK
    group = vw // kw
    all_heads = range(local)
    for i, route in enumerate(routes(n)):
        block = moved(me, route, n, back=True)
        kx_ref[block] = keyed[i][...]
        qv_ref[block] = asked[i][...]
    row, col = iota((tokens, tokens), 0), iota((tokens, tokens), 1)
    eye = (row == col).astype(f32)
    gain = gain_ref[...]

    def prepare(block):
        as_cols, as_rows = head_rates(local, kx_ref.at[block], tokens)
        cumulative = jnp.exp(as_cols)
        last = as_cols[tokens - 1 : tokens]
        ends = jnp.exp(last)
        kept = jnp.exp(last - as_cols)
        made = []
        for g in range(local // group):
            k = kx_ref[block, 0:tokens, g * DK : (g + 1) * DK]
            q = qv_ref[block, :, g * DK : (g + 1) * DK]
            k_col = inverse_scale(k)
            q_col = inverse_scale(q) * DK ** (-0.5)
            k_row = jnp.sum(eye * k_col, axis=0, keepdims=True)
            dots = jnp.where(row >= col, mm_nt(q, k) * k_row * q_col, 0.0)
            for h in range(g * group, (g + 1) * group):
                gap = as_cols[:, h : h + 1] - as_rows[h : h + 1, :]
                scores = split2(jnp.exp(jnp.minimum(gap, 0.0)) * dots)
                write = as_cols[:, local + h : local + h + 1]
                cum = cumulative[:, h : h + 1]
                made.append(
                    dict(
                        k=k,
                        q=q,
                        scores=scores,
                        write=write,
                        erase=write * cum * k_col,
                        ask=cum * q_col,
                        kept=kept[:, h : h + 1] * k_col,
                        end=ends[:, h : h + 1],
                    )
                )
        return made

    def finish(block, made, seen, delta):
        for h in all_heads:
            out = mm3(made[h]["scores"], delta[h])
            if block > 0:
                out = out + made[h]["ask"] * seen[h][tokens:]
            mean = jnp.mean(out * out, axis=1, keepdims=True)
            out_ref[block, :, h * DK : (h + 1) * DK] = out * lax.rsqrt(mean + EPS) * gain

    states, before, made = None, None, prepare(0)
    for block in range(n):
        rhs = [
            m["write"] * qv_ref[block, :, kw + h * DK : kw + (h + 1) * DK].astype(f32) for h, m in enumerate(made)
        ]
        seen = None
        if block > 0:
            both = [jnp.concatenate([m["k"], m["q"]], axis=0) for m in made]
            seen = [
                mm(jnp.concatenate([b, b], axis=1), jnp.concatenate(split2(s), axis=0)) for b, s in zip(both, states)
            ]
        if before is not None:
            finish(*before)
        if block > 0:
            rhs = [r - m["erase"] * s[:tokens] for r, m, s in zip(rhs, made, seen)]
        delta = [mm3((inv_ref[block, h, 0], inv_ref[block, h, 1]), split2(rhs[h])) for h in all_heads]
        later = prepare(block + 1) if block < n - 1 else None
        if block < n - 1:
            grown = [
                mm_tn(jnp.concatenate([m["k"], m["k"]], axis=0), jnp.concatenate(split2(m["kept"] * d), axis=0))
                for m, d in zip(made, delta)
            ]
            states = grown if block == 0 else [m["end"] * s + g for m, s, g in zip(made, states, grown)]
        before = (block, made, seen, [split2(d) for d in delta])
        made = later
    finish(*before)
    for j in range(n // 2):
        keep_ref[j] = out_ref[moved(me, (j, 0), n)]
        give_ref[j] = out_ref[moved(me, (j, 1), n)].astype(bf16)


def chip_projection(me, keep, other, gate_ref, start, proj_ref, proj_other_ref, columns):
    vw = keep.shape[1]
    mixed = []
    for heads, core in ((keep, lax.rem(me, 2)), (other, 1 - lax.rem(me, 2))):
        gate = gate_ref[:, pl.ds(pl.multiple_of(start + core * vw, LANES), vw)].astype(f32)
        mixed.append((heads.astype(f32) * (gate / (1.0 + jnp.exp(-gate)))).astype(bf16))
    for at in range(0, proj_ref.shape[1], columns):
        here = slice(at, at + columns)
        yield here, mm(mixed[0], proj_ref[:, here]) + mm(mixed[1], proj_other_ref[:, here])


def far_kernel(n, *refs):
    gated = refs[: n // 2 - 1]
    keep_ref, other_ref, proj_ref, proj_other_ref, *sums = refs[n // 2 - 1 :]
    me = lax.axis_index("ctx")
    for j, (gate_ref, out) in enumerate(zip(gated, sums), 1):
        for here, part in chip_projection(me, keep_ref[j], other_ref[j], gate_ref, 0, proj_ref, proj_other_ref, 512):
            out[:, here] = part.astype(bf16)


def home_kernel(
    residual_ref,
    gate_ref,
    keep_ref,
    other_ref,
    proj_ref,
    proj_other_ref,
    ids_ref,
    weight_ref,
    base_ref,
    picker_ref,
    table_ref,
):
    me = lax.axis_index("ctx")
    start = me // 2 * 2 * keep_ref.shape[2]
    gate_ref = gate_ref.at[0]
    for here, part in chip_projection(me, keep_ref[0], other_ref[0], gate_ref, start, proj_ref, proj_other_ref, 512):
        base_ref[:, here] = residual_ref[0, :, here].astype(f32) + part
    slots, tokens = table_ref.shape
    slot = iota((slots, tokens), 0)
    expert = slot // CAP
    named = jnp.zeros((slots, tokens), f32)
    weight = jnp.zeros((slots, tokens), f32)
    for j in range(ids_ref.shape[0]):
        hit = ids_ref[j] == expert
        named = named + hit.astype(f32)
        weight = weight + jnp.where(hit, weight_ref[j], 0.0)
    before = (iota((tokens, tokens), 0) < iota((tokens, tokens), 1)).astype(bf16)
    rank = mm(named.astype(bf16), before)
    chosen = jnp.where(rank == lax.rem(slot, CAP).astype(f32), named, 0.0)
    table_ref[...] = chosen * weight
    picker_ref[...] = chosen.astype(bf16)


def dispatch_kernel(base_ref, gain_ref, picker_ref, *refs):
    part_refs = refs[:-3]
    hidden_ref, rows_ref, flat_ref = refs[-3:]
    width = hidden_ref.shape[1]
    slots = picker_ref.shape[0]
    chunks = width // LANES
    squares = 0.0
    step = 512
    for c in range(0, width, step):
        total = base_ref[:, c : c + step]
        for part in part_refs:
            total = total + part[:, c : c + step].astype(f32)
        hidden_ref[:, c : c + step] = total
        squares = squares + jnp.sum(total * total, axis=1, keepdims=True)
    scale = lax.rsqrt(squares * (1.0 / width) + EPS)
    picker = picker_ref[...]
    for c in range(0, width, step):
        normed = (hidden_ref[:, c : c + step] * scale * gain_ref[:, c : c + step]).astype(bf16)
        rows = mm(picker, normed)
        for i in range(step // LANES):
            flat_ref[pl.ds(c // LANES + i, slots, stride=chunks), :] = rows[:, i * LANES : (i + 1) * LANES]
    rows_ref[...] = flat_ref[...].astype(bf16).reshape(rows_ref.shape)


def expert_kernel(rows_ref, gate_ref, up_ref, down_ref, out_ref, flat_ref, x_ref):
    slots = flat_ref.shape[0] * LANES // x_ref.shape[1]
    width = x_ref.shape[1]
    chunks = width // LANES
    flat_ref[...] = rows_ref[...].reshape(flat_ref.shape).astype(f32)
    for c in range(chunks):
        x_ref[:, c * LANES : (c + 1) * LANES] = flat_ref[pl.ds(c, slots, stride=chunks), :].astype(bf16)
    tile = 128

    def one(t, carry):
        x = x_ref[pl.ds(pl.multiple_of(t * tile, tile), tile), :]
        gate = mm(x, gate_ref[0])
        up = mm(x, up_ref[0])
        act = (gate / (1.0 + jnp.exp(-gate)) * up).astype(bf16)
        step = 512
        for c in range(0, width, step):
            y = mm(act, down_ref[0, :, c : c + step])
            for i in range(step // LANES):
                flat_ref[pl.ds(t * tile * chunks + c // LANES + i, tile, stride=chunks), :] = y[
                    :, i * LANES : (i + 1) * LANES
                ]
        return carry

    lax.fori_loop(0, slots // tile, one, 0)
    out_ref[...] = flat_ref[...].astype(bf16).reshape(out_ref.shape)


def combine_kernel(hidden_ref, table_ref, back_ref, mask_ref, dir_ref, out_ref, flat_ref, sum_ref):
    tokens, width = hidden_ref.shape
    slots = table_ref.shape[0]
    chunks = width // LANES
    flat_ref[...] = back_ref[...].reshape(flat_ref.shape).astype(f32)
    table = jnp.concatenate(split2(table_ref[...]), axis=0)
    direction = dir_ref[...]
    unit = direction / jnp.sqrt(jnp.sum(direction * direction, axis=1, keepdims=True) + EPS)
    eye = iota((tokens, tokens), 0) == iota((tokens, tokens), 1)
    mask = jnp.sum(jnp.where(eye, mask_ref[...].astype(f32), 0.0), axis=1, keepdims=True)
    along = 0.0
    step = 256
    for c in range(0, width, step):
        back = jnp.concatenate(
            [flat_ref[pl.ds(c // LANES + i, slots, stride=chunks), :].astype(bf16) for i in range(step // LANES)], axis=1
        )
        total = hidden_ref[:, c : c + step] + mm_tn(table, jnp.concatenate([back, back], axis=0))
        sum_ref[:, c : c + step] = total
        along = along + jnp.sum(total * unit[:, c : c + step], axis=1, keepdims=True)
    out_ref[0] = (sum_ref[...] - (mask * along) * unit).astype(bf16)


def local_part(
    n,
    devices,
    queries,
    keys,
    values,
    out_gate,
    write_rate,
    decay,
    head_gain,
    residual,
    out_proj,
    ffn_gain,
    expert_ids,
    route_weight,
    w_gate,
    w_up,
    w_down,
    ablate_mask,
    direction,
):
    tokens = queries.shape[1]
    width = residual.shape[2]
    kw, vw = keys.shape[2] // n, values.shape[2] // n
    chips = n // 2
    slots = devices * CAP
    chunks = width // LANES
    shape = jax.ShapeDtypeStruct

    local = vw // DK
    ways = routes(n)
    keyed_shape = shape((tokens + AUX, kw), bf16)
    with jax.named_scope("pack"):
        packed = pl.pallas_call(
            functools.partial(pack_kernel, n, kw, vw),
            out_shape=[keyed_shape] * n
            + [shape((tokens, kw + vw), bf16)] * n
            + [shape((tokens, 2 * vw), bf16)] * (chips - 1),
            compiler_params=compiler_params(16),
        )(*in_hbm(keys, write_rate.transpose(0, 2, 1), decay.transpose(0, 2, 1), queries, values, out_gate))
        keyed, asked, gated = list(packed[:n]), list(packed[n : 2 * n]), packed[2 * n :]
    with jax.named_scope("heads_exchange"):
        order = [i for i, route in enumerate(ways) if route[0]] + [1]
        for i in order:
            keyed[i] = send(keyed[i], ways[i], n)
        for i in order[:-1]:
            asked[i] = send(asked[i], ways[i], n)
    with jax.named_scope("block_inverses"):
        inverses = pl.pallas_call(
            functools.partial(inverse_kernel, n, local),
            out_shape=shape((n, local, 2, tokens, tokens), bf16),
            compiler_params=compiler_params(16),
            cost_estimate=pl.CostEstimate(flops=6 * 10**9, bytes_accessed=10**6, transcendentals=0),
        )(*keyed)
    with jax.named_scope("late_exchange"):
        proj = out_proj
        inverses, asked[1], gated = lax.optimization_barrier((inverses, asked[1], gated))
        asked[1] = send(asked[1], ways[1], n)
        gated = [send(gate, (j, 0), n) for j, gate in enumerate(gated, 1)]
        proj_other = send(proj, (0, 1), n)
    with jax.named_scope("states"):
        keep, give = pl.pallas_call(
            functools.partial(state_kernel, n, kw, vw),
            out_shape=[shape((chips, tokens, vw), f32), shape((chips, tokens, vw), bf16)],
            scratch_shapes=[
                pltpu.VMEM((n, tokens, vw), f32),
                pltpu.VMEM((n, tokens + AUX, kw), bf16),
                pltpu.VMEM((n, tokens, kw + vw), bf16),
            ],
            compiler_params=compiler_params(16),
            cost_estimate=pl.CostEstimate(flops=4 * 10**9, bytes_accessed=10**6, transcendentals=0),
        )(*keyed, *asked, inverses, head_gain.reshape(1, -1))
    with jax.named_scope("far_projection"):
        other = send(give, (0, 1), n)
        sums = pl.pallas_call(
            functools.partial(far_kernel, n),
            out_shape=[shape((tokens, width), bf16)] * (chips - 1),
            compiler_params=compiler_params(16),
        )(*gated, keep, other, out_proj, proj_other)
    with jax.named_scope("projection_sum"):
        parts = [send(part, (j, 0), n) for j, part in enumerate(sums, 1)]
    with jax.named_scope("home"):
        base, picker, table = pl.pallas_call(
            home_kernel,
            out_shape=[shape((tokens, width), f32), shape((slots, tokens), bf16), shape((slots, tokens), f32)],
            compiler_params=compiler_params(16),
            cost_estimate=pl.CostEstimate(flops=1000, bytes_accessed=1000, transcendentals=0),
        )(
            residual,
            out_gate,
            keep,
            other,
            out_proj,
            proj_other,
            expert_ids.transpose(2, 0, 1),
            route_weight.transpose(2, 0, 1),
        )
    with jax.named_scope("dispatch"):
        hidden, rows = pl.pallas_call(
            dispatch_kernel,
            out_shape=[shape((tokens, width), f32), shape((devices, CAP * chunks, LANES), bf16)],
            scratch_shapes=[pltpu.VMEM((slots * chunks, LANES), f32)],
            compiler_params=compiler_params(24),
        )(base, ffn_gain.reshape(1, -1), picker, *parts)
    with jax.named_scope("to_experts"):
        came = lax.all_to_all(rows, ("ctx", "exp"), 0, 0, tiled=True)
    with jax.named_scope("experts"):
        done = pl.pallas_call(
            expert_kernel,
            out_shape=shape((devices, CAP * chunks, LANES), bf16),
            scratch_shapes=[pltpu.VMEM((slots * chunks, LANES), f32), pltpu.VMEM((slots, width), bf16)],
            compiler_params=compiler_params(24),
        )(came, w_gate, w_up, w_down)
    with jax.named_scope("from_experts"):
        back = lax.all_to_all(done, ("ctx", "exp"), 0, 0, tiled=True)
    with jax.named_scope("combine"):
        return pl.pallas_call(
            combine_kernel,
            out_shape=shape((1, tokens, width), bf16),
            scratch_shapes=[
                pltpu.VMEM((slots * chunks, LANES), f32),
                pltpu.VMEM((tokens, width), f32),
            ],
            compiler_params=compiler_params(24),
        )(hidden, table, back, ablate_mask, direction.reshape(1, -1))


def solution(mesh):
    seq = P("exp", "ctx", None)
    owned = P(("ctx", "exp"), None, None)
    placed = (
        (seq,) * 6 + (P(), seq, P("ctx", None), P(), seq, seq) + (owned,) * 3 + (P("exp", "ctx"), P())
    )
    n = mesh.shape["ctx"]
    return jax.shard_map(
        functools.partial(local_part, n, n * mesh.shape["exp"]),
        mesh=mesh,
        in_specs=placed,
        out_specs=seq,
        check_vma=False,
    )
```

```python
import functools

import jax
import jax.numpy as jnp
from jax import lax
from jax.experimental import pallas as pl
from jax.experimental.pallas import tpu as pltpu
from jax.sharding import PartitionSpec as P

DK = 128
CAP = 4
EPS = 1e-06
AUX = 16
LANES = 128

bf16 = jnp.bfloat16
f32 = jnp.float32


def mm(a, b):
    return jnp.dot(a, b, preferred_element_type=f32)


def mm_nt(a, b):
    return lax.dot_general(a, b, (((1,), (1,)), ((), ())), preferred_element_type=f32)


def mm_tn(a, b):
    return lax.dot_general(a, b, (((0,), (0,)), ((), ())), preferred_element_type=f32)


def split2(x):
    hi = x.astype(bf16)
    return hi, (x - hi.astype(f32)).astype(bf16)


def split3(x):
    hi = x.astype(bf16)
    rest = x - hi.astype(f32)
    mid = rest.astype(bf16)
    return hi, mid, (rest - mid.astype(f32)).astype(bf16)


def mm3(a, b):
    (ah, al), (bh, bl) = a, b
    return mm(jnp.concatenate([ah, al, ah], axis=1), jnp.concatenate([bh, bh, bl], axis=0))


def iota(shape, dim):
    return lax.broadcasted_iota(jnp.int32, shape, dim)


def in_hbm(*arrays):
    return [pltpu.with_memory_space_constraint(a, pltpu.HBM) for a in arrays]


def compiler_params(mib):
    return pltpu.CompilerParams(vmem_limit_bytes=mib * 1024 * 1024)


def routes(n):
    return [(chips, flip) for chips in range(n // 2) for flip in (0, 1)]


def moved(index, route, n, back=False):
    chips, flip = route
    chip = lax.rem(index // 2 + (n // 2 - chips if back else chips), n // 2)
    return chip * 2 + lax.rem(lax.rem(index, 2) + flip, 2)


def send(x, route, n):
    chips, flip = route
    pairs = [(i, (i // 2 + chips) % (n // 2) * 2 + (i % 2 + flip) % 2) for i in range(n)]
    return lax.ppermute(x, "ctx", pairs)


def pack_kernel(n, kw, vw, k_ref, w_ref, d_ref, q_ref, v_ref, g_ref, *outs):
    local = vw // DK
    keyed, asked, gated = outs[:n], outs[n : 2 * n], outs[2 * n :]
    me = lax.axis_index("ctx")
    tokens = k_ref.shape[1]
    heads = d_ref.shape[1]
    ones = (iota((tokens, tokens), 0) <= iota((tokens, tokens), 1)).astype(bf16)
    logs = jnp.log(d_ref[0])
    sums = sum(mm(piece, ones) for piece in reversed(split3(logs)))
    pieces = [p.astype(f32) for p in (*split3(sums), *split3(w_ref[0]))]
    rates = jnp.concatenate(pieces, axis=0).astype(bf16)
    rows = AUX * kw // LANES
    row, entry = iota((rows, 6 * heads), 0), iota((rows, 6 * heads), 1)
    for i, route in enumerate(routes(n)):
        to = moved(me, route, n)
        kat = pl.ds(pl.multiple_of(to * kw, LANES), kw)
        keyed[i][0:tokens] = k_ref[0, :, kat]
        wanted = row // local * heads + to * local + lax.rem(row, local)
        aux = mm(((row < 6 * local) & (entry == wanted)).astype(bf16), rates)
        for at in range(kw // LANES):
            keyed[i][tokens:, at * LANES : (at + 1) * LANES] = aux[at * AUX : (at + 1) * AUX].astype(bf16)
        asked[i][:, 0:kw] = q_ref[0, :, kat]
        asked[i][:, kw:] = v_ref[0, :, pl.ds(pl.multiple_of(to * vw, LANES), vw)]
    for j, out in enumerate(gated):
        chip = lax.rem(me // 2 + j + 1, n // 2)
        out[...] = g_ref[0, :, pl.ds(pl.multiple_of(chip * 2 * vw, LANES), 2 * vw)]


def head_rates(local, keyed, tokens):
    aux = jnp.concatenate(
        [keyed[tokens:, i * LANES : (i + 1) * LANES] for i in range(keyed.shape[1] // LANES)], axis=0
    )
    row, col = iota((aux.shape[0], LANES), 0), iota((aux.shape[0], LANES), 1)
    same = (row < 6 * local) & (lax.rem(row, local) == lax.rem(col, local)) & (row // (3 * local) == col // local)
    return aux, (same & (col < 2 * local)).astype(bf16)


def both_halves(x):
    return jnp.concatenate(split2(x), axis=1)


def mm3_held(held, b):
    return mm(jnp.concatenate([held, held[:, : held.shape[1] // 2]], axis=1), b)


def stacked(x):
    high, low = split2(x)
    return jnp.concatenate([high, high, low], axis=0)


def inverse_scale(raw):
    raw_f = raw.astype(f32)
    return lax.rsqrt(jnp.sum(raw_f * raw_f, axis=1, keepdims=True) + EPS)


def inverse_kernel(n, local, *refs):
    keyed = refs[:n]
    value_ref, erase_ref, key_ref, row_ref = refs[n:]
    me = lax.axis_index("ctx")
    tokens = value_ref.shape[2]
    group = local * DK // keyed[0].shape[1]
    row, col = iota((tokens, tokens), 0), iota((tokens, tokens), 1)
    apart = lax.bitwise_xor(row, col)
    eye = (row == col).astype(f32)
    systems, scales = [], []
    for i, route in enumerate(routes(n)):
        block = moved(me, route, n, back=True)
        aux, total = head_rates(local, keyed[i], tokens)
        as_cols, as_rows = mm_tn(aux, total), mm_tn(total, aux)
        down, up = jnp.exp(as_rows), jnp.exp(-as_rows)
        left = jnp.exp(as_rows[:, tokens - 1 :] - as_rows)
        down_cols = jnp.exp(as_cols)
        for g in range(local // group):
            k = keyed[i][0:tokens, g * DK : (g + 1) * DK]
            k_t = k.astype(f32).T
            dots = mm_nt(k, k)
            diag = dots * eye
            k_row = lax.rsqrt(jnp.sum(diag, axis=0, keepdims=True) + EPS)
            k_col = lax.rsqrt(jnp.sum(diag, axis=1, keepdims=True) + EPS)
            dots = jnp.where(row > col, dots * k_row, 0.0)
            for h in range(g * group, (g + 1) * group):
                write = as_rows[local + h : local + h + 1]
                scale = as_cols[:, local + h : local + h + 1] * down_cols[:, h : h + 1] * k_col
                systems.append(scale * (up[h : h + 1] * dots))
                scales.append((write, write * down[h : h + 1] * k_row))
                key_ref[block, h] = both_halves(k_t * (left[h : h + 1] * k_row))
                row_ref[block, h, 0:1] = up[h : h + 1] * k_row
                row_ref[block, h, 1:2] = jnp.broadcast_to(down[h : h + 1, tokens - 1 :], (1, tokens))
    near = [jnp.where(apart < 16, s, 0.0) for s in systems]
    power = [split2(s) for s in near]
    inverse = [eye - s for s in near]
    power = [mm3(p, p) for p in power]
    for _ in range(2):
        halves = [split2(p) for p in power]
        both = [mm3(split2(jnp.concatenate([p, x], axis=0)), ps) for p, x, ps in zip(power, inverse, halves)]
        power = [b[:tokens] for b in both]
        inverse = [x + b[tokens:] for x, b in zip(inverse, both)]
    inverse = [x + mm3(split2(x), split2(p)) for x, p in zip(inverse, power)]
    size = 16
    while size < tokens:
        odd = [slice(at, at + size) for at in range(size, tokens, 2 * size)]
        beside = (apart >= size) & (apart < 2 * size)
        below = [jnp.where(beside, s, 0.0) for s in systems]
        below = [split2(jnp.concatenate([b[o] for o in odd], axis=0)) for b in below]
        halves = [split2(x) for x in inverse]
        first = [mm3(b, x) for b, x in zip(below, halves)]
        first = [split2(widen(f, size)) for f in first]
        lower = [tuple(jnp.concatenate([part[o] for o in odd], axis=0) for part in x) for x in halves]
        inverse = [x - widen(mm3(a, b), size) for x, a, b in zip(inverse, lower, first)]
        size *= 2
    for i, route in enumerate(routes(n)):
        block = moved(me, route, n, back=True)
        for h in range(local):
            for_values, for_state = scales[i * local + h]
            value_ref[block, h] = both_halves(inverse[i * local + h] * for_values)
            erase_ref[block, h] = both_halves(inverse[i * local + h] * for_state)


def widen(x, size):
    none = jnp.zeros((size, x.shape[1]), x.dtype)
    return jnp.concatenate(
        [part for at in range(0, x.shape[0], size) for part in (none, x[at : at + size])], axis=0
    )


def state_kernel(n, kw, vw, *refs):
    keyed, asked = refs[:n], refs[n : 2 * n]
    value_ref, erase_ref, key_ref, row_ref, gain_ref, keep_ref, give_ref, out_ref, kx_ref, qv_ref = refs[2 * n :]
    me = lax.axis_index("ctx")
    tokens = value_ref.shape[2]
    local = vw // DK
    group = vw // kw
    all_heads = range(local)
    for i, route in enumerate(routes(n)):
        block = moved(me, route, n, back=True)
        kx_ref[block] = keyed[i][...]
        qv_ref[block] = asked[i][...]
    row, col = iota((tokens, tokens), 0), iota((tokens, tokens), 1)
    gain = gain_ref[...]

    def prepare(block):
        aux, total = head_rates(local, kx_ref.at[block], tokens)
        down_cols = jnp.exp(mm_tn(aux, total))
        made = []
        for g in range(local // group):
            k = kx_ref[block, 0:tokens, g * DK : (g + 1) * DK]
            q = qv_ref[block, :, g * DK : (g + 1) * DK]
            q_col = inverse_scale(q) * DK ** (-0.5)
            dots = jnp.where(row >= col, mm_nt(q, k), 0.0)
            for h in range(g * group, (g + 1) * group):
                v = qv_ref[block, :, kw + h * DK : kw + (h + 1) * DK]
                made.append(
                    dict(
                        k=jnp.concatenate([k, k], axis=1),
                        q=jnp.concatenate([q, q], axis=1),
                        scores=both_halves(dots * row_ref[block, h, 0:1]),
                        scale=down_cols[:, h : h + 1] * q_col,
                        written=mm(value_ref[block, h], jnp.concatenate([v, v], axis=0)),
                    )
                )
        return made

    def finish(block, made, held, delta):
        for h in all_heads:
            out = mm3_held(made[h]["scores"], delta[h])
            if held is not None:
                out = out + mm(made[h]["q"], held[h])
            out = made[h]["scale"] * out
            mean = jnp.mean(out * out, axis=1, keepdims=True)
            out_ref[block, :, h * DK : (h + 1) * DK] = out * lax.rsqrt(mean + EPS) * gain

    states, before, made = None, None, prepare(0)
    for block in range(n):
        held = None
        delta = [m["written"] for m in made]
        if block > 0:
            held = [jnp.concatenate(split2(s), axis=0) for s in states]
            seen = [mm(m["k"], s) for m, s in zip(made, held)]
            finish(*before)
            delta = [d - mm3_held(erase_ref[block, h], stacked(seen[h])) for h, d in enumerate(delta)]
        later = prepare(block + 1) if block < n - 1 else None
        delta = [stacked(d) for d in delta]
        if block < n - 1:
            grown = [mm3_held(key_ref[block, h], delta[h]) for h in all_heads]
            if block == 0:
                states = grown
            else:
                states = [row_ref[block, h, 1:2] * states[h] + grown[h] for h in all_heads]
        before = (block, made, held, delta)
        made = later
    finish(*before)
    for j in range(n // 2):
        keep_ref[j] = out_ref[moved(me, (j, 0), n)]
        give_ref[j] = out_ref[moved(me, (j, 1), n)].astype(bf16)


def chip_projection(me, keep, other, gate_ref, start, proj_ref, proj_other_ref, columns):
    vw = keep.shape[1]
    mixed = []
    for heads, core in ((keep, lax.rem(me, 2)), (other, 1 - lax.rem(me, 2))):
        gate = gate_ref[:, pl.ds(pl.multiple_of(start + core * vw, LANES), vw)].astype(f32)
        mixed.append((heads.astype(f32) * (gate / (1.0 + jnp.exp(-gate)))).astype(bf16))
    for at in range(0, proj_ref.shape[1], columns):
        here = slice(at, at + columns)
        yield here, mm(mixed[0], proj_ref[:, here]) + mm(mixed[1], proj_other_ref[:, here])


def far_kernel(n, *refs):
    gated = refs[: n // 2 - 1]
    keep_ref, other_ref, proj_ref, proj_other_ref, *sums = refs[n // 2 - 1 :]
    me = lax.axis_index("ctx")
    for j, (gate_ref, out) in enumerate(zip(gated, sums), 1):
        for here, part in chip_projection(me, keep_ref[j], other_ref[j], gate_ref, 0, proj_ref, proj_other_ref, 512):
            out[:, here] = part.astype(bf16)


def home_kernel(
    residual_ref,
    gate_ref,
    keep_ref,
    other_ref,
    proj_ref,
    proj_other_ref,
    ids_ref,
    weight_ref,
    base_ref,
    picker_ref,
    table_ref,
):
    me = lax.axis_index("ctx")
    start = me // 2 * 2 * keep_ref.shape[2]
    gate_ref = gate_ref.at[0]
    for here, part in chip_projection(me, keep_ref[0], other_ref[0], gate_ref, start, proj_ref, proj_other_ref, 512):
        base_ref[:, here] = residual_ref[0, :, here].astype(f32) + part
    slots, tokens = table_ref.shape
    slot = iota((slots, tokens), 0)
    expert = slot // CAP
    named = jnp.zeros((slots, tokens), f32)
    weight = jnp.zeros((slots, tokens), f32)
    for j in range(ids_ref.shape[0]):
        hit = ids_ref[j] == expert
        named = named + hit.astype(f32)
        weight = weight + jnp.where(hit, weight_ref[j], 0.0)
    before = (iota((tokens, tokens), 0) < iota((tokens, tokens), 1)).astype(bf16)
    rank = mm(named.astype(bf16), before)
    chosen = jnp.where(rank == lax.rem(slot, CAP).astype(f32), named, 0.0)
    table_ref[...] = chosen * weight
    picker_ref[...] = chosen.astype(bf16)


def dispatch_kernel(base_ref, gain_ref, picker_ref, *refs):
    part_refs = refs[:-3]
    hidden_ref, rows_ref, flat_ref = refs[-3:]
    width = hidden_ref.shape[1]
    slots = picker_ref.shape[0]
    chunks = width // LANES
    squares = 0.0
    step = 512
    for c in range(0, width, step):
        total = base_ref[:, c : c + step]
        for part in part_refs:
            total = total + part[:, c : c + step].astype(f32)
        hidden_ref[:, c : c + step] = total
        squares = squares + jnp.sum(total * total, axis=1, keepdims=True)
    scale = lax.rsqrt(squares * (1.0 / width) + EPS)
    picker = picker_ref[...]
    for c in range(0, width, step):
        normed = (hidden_ref[:, c : c + step] * scale * gain_ref[:, c : c + step]).astype(bf16)
        rows = mm(picker, normed)
        for i in range(step // LANES):
            flat_ref[pl.ds(c // LANES + i, slots, stride=chunks), :] = rows[:, i * LANES : (i + 1) * LANES]
    rows_ref[...] = flat_ref[...].astype(bf16).reshape(rows_ref.shape)


def expert_kernel(rows_ref, gate_ref, up_ref, down_ref, out_ref, flat_ref, x_ref):
    slots = flat_ref.shape[0] * LANES // x_ref.shape[1]
    width = x_ref.shape[1]
    chunks = width // LANES
    flat_ref[...] = rows_ref[...].reshape(flat_ref.shape).astype(f32)
    for c in range(chunks):
        x_ref[:, c * LANES : (c + 1) * LANES] = flat_ref[pl.ds(c, slots, stride=chunks), :].astype(bf16)
    tile = 128

    def one(t, carry):
        x = x_ref[pl.ds(pl.multiple_of(t * tile, tile), tile), :]
        gate = mm(x, gate_ref[0])
        up = mm(x, up_ref[0])
        act = (gate / (1.0 + jnp.exp(-gate)) * up).astype(bf16)
        step = 512
        for c in range(0, width, step):
            y = mm(act, down_ref[0, :, c : c + step])
            for i in range(step // LANES):
                flat_ref[pl.ds(t * tile * chunks + c // LANES + i, tile, stride=chunks), :] = y[
                    :, i * LANES : (i + 1) * LANES
                ]
        return carry

    lax.fori_loop(0, slots // tile, one, 0)
    out_ref[...] = flat_ref[...].astype(bf16).reshape(out_ref.shape)


def combine_kernel(hidden_ref, table_ref, back_ref, mask_ref, dir_ref, out_ref, flat_ref, sum_ref):
    tokens, width = hidden_ref.shape
    slots = table_ref.shape[0]
    chunks = width // LANES
    flat_ref[...] = back_ref[...].reshape(flat_ref.shape).astype(f32)
    table = jnp.concatenate(split2(table_ref[...]), axis=0)
    direction = dir_ref[...]
    unit = direction / jnp.sqrt(jnp.sum(direction * direction, axis=1, keepdims=True) + EPS)
    eye = iota((tokens, tokens), 0) == iota((tokens, tokens), 1)
    mask = jnp.sum(jnp.where(eye, mask_ref[...].astype(f32), 0.0), axis=1, keepdims=True)
    along = 0.0
    step = 256
    for c in range(0, width, step):
        back = jnp.concatenate(
            [flat_ref[pl.ds(c // LANES + i, slots, stride=chunks), :].astype(bf16) for i in range(step // LANES)], axis=1
        )
        total = hidden_ref[:, c : c + step] + mm_tn(table, jnp.concatenate([back, back], axis=0))
        sum_ref[:, c : c + step] = total
        along = along + jnp.sum(total * unit[:, c : c + step], axis=1, keepdims=True)
    out_ref[0] = (sum_ref[...] - (mask * along) * unit).astype(bf16)


def local_part(
    n,
    devices,
    queries,
    keys,
    values,
    out_gate,
    write_rate,
    decay,
    head_gain,
    residual,
    out_proj,
    ffn_gain,
    expert_ids,
    route_weight,
    w_gate,
    w_up,
    w_down,
    ablate_mask,
    direction,
):
    tokens = queries.shape[1]
    width = residual.shape[2]
    kw, vw = keys.shape[2] // n, values.shape[2] // n
    chips = n // 2
    slots = devices * CAP
    chunks = width // LANES
    shape = jax.ShapeDtypeStruct

    local = vw // DK
    ways = routes(n)
    keyed_shape = shape((tokens + AUX, kw), bf16)
    with jax.named_scope("pack"):
        packed = pl.pallas_call(
            functools.partial(pack_kernel, n, kw, vw),
            out_shape=[keyed_shape] * n
            + [shape((tokens, kw + vw), bf16)] * n
            + [shape((tokens, 2 * vw), bf16)] * (chips - 1),
            compiler_params=compiler_params(16),
        )(*in_hbm(keys, write_rate.transpose(0, 2, 1), decay.transpose(0, 2, 1), queries, values, out_gate))
        keyed, asked, gated = list(packed[:n]), list(packed[n : 2 * n]), packed[2 * n :]
    with jax.named_scope("heads_exchange"):
        order = [i for i, route in enumerate(ways) if route[0]] + [1]
        for i in order:
            keyed[i] = send(keyed[i], ways[i], n)
        for i in order[:-1]:
            asked[i] = send(asked[i], ways[i], n)
    with jax.named_scope("block_inverses"):
        wide = shape((n, local, tokens, 2 * tokens), bf16)
        inverses = pl.pallas_call(
            functools.partial(inverse_kernel, n, local),
            out_shape=[wide, wide, shape((n, local, DK, 2 * tokens), bf16), shape((n, local, 8, tokens), f32)],
            compiler_params=compiler_params(16),
            cost_estimate=pl.CostEstimate(flops=6 * 10**9, bytes_accessed=10**6, transcendentals=0),
        )(*keyed)
    with jax.named_scope("late_exchange"):
        proj = out_proj
        keyed, asked[1], gated = lax.optimization_barrier((keyed, asked[1], gated))
        asked[1] = send(asked[1], ways[1], n)
        gated = [send(gate, (j, 0), n) for j, gate in enumerate(gated, 1)]
        proj_other = send(proj, (0, 1), n)
    with jax.named_scope("states"):
        keep, give = pl.pallas_call(
            functools.partial(state_kernel, n, kw, vw),
            out_shape=[shape((chips, tokens, vw), f32), shape((chips, tokens, vw), bf16)],
            scratch_shapes=[
                pltpu.VMEM((n, tokens, vw), f32),
                pltpu.VMEM((n, tokens + AUX, kw), bf16),
                pltpu.VMEM((n, tokens, kw + vw), bf16),
            ],
            compiler_params=compiler_params(16),
            cost_estimate=pl.CostEstimate(flops=4 * 10**9, bytes_accessed=10**6, transcendentals=0),
        )(*keyed, *asked, *inverses, head_gain.reshape(1, -1))
    with jax.named_scope("far_projection"):
        other = send(give, (0, 1), n)
        sums = pl.pallas_call(
            functools.partial(far_kernel, n),
            out_shape=[shape((tokens, width), bf16)] * (chips - 1),
            compiler_params=compiler_params(16),
        )(*gated, keep, other, out_proj, proj_other)
    with jax.named_scope("projection_sum"):
        parts = [send(part, (j, 0), n) for j, part in enumerate(sums, 1)]
    with jax.named_scope("home"):
        base, picker, table = pl.pallas_call(
            home_kernel,
            out_shape=[shape((tokens, width), f32), shape((slots, tokens), bf16), shape((slots, tokens), f32)],
            compiler_params=compiler_params(16),
            cost_estimate=pl.CostEstimate(flops=1000, bytes_accessed=1000, transcendentals=0),
        )(
            residual,
            out_gate,
            keep,
            other,
            out_proj,
            proj_other,
            expert_ids.transpose(2, 0, 1),
            route_weight.transpose(2, 0, 1),
        )
    with jax.named_scope("dispatch"):
        hidden, rows = pl.pallas_call(
            dispatch_kernel,
            out_shape=[shape((tokens, width), f32), shape((devices, CAP * chunks, LANES), bf16)],
            scratch_shapes=[pltpu.VMEM((slots * chunks, LANES), f32)],
            compiler_params=compiler_params(24),
        )(base, ffn_gain.reshape(1, -1), picker, *parts)
    with jax.named_scope("to_experts"):
        came = lax.all_to_all(rows, ("ctx", "exp"), 0, 0, tiled=True)
    with jax.named_scope("experts"):
        done = pl.pallas_call(
            expert_kernel,
            out_shape=shape((devices, CAP * chunks, LANES), bf16),
            scratch_shapes=[pltpu.VMEM((slots * chunks, LANES), f32), pltpu.VMEM((slots, width), bf16)],
            compiler_params=compiler_params(24),
        )(came, w_gate, w_up, w_down)
    with jax.named_scope("from_experts"):
        back = lax.all_to_all(done, ("ctx", "exp"), 0, 0, tiled=True)
    with jax.named_scope("combine"):
        return pl.pallas_call(
            combine_kernel,
            out_shape=shape((1, tokens, width), bf16),
            scratch_shapes=[
                pltpu.VMEM((slots * chunks, LANES), f32),
                pltpu.VMEM((tokens, width), f32),
            ],
            compiler_params=compiler_params(24),
        )(hidden, table, back, ablate_mask, direction.reshape(1, -1))


def solution(mesh):
    seq = P("exp", "ctx", None)
    owned = P(("ctx", "exp"), None, None)
    placed = (
        (seq,) * 6 + (P(), seq, P("ctx", None), P(), seq, seq) + (owned,) * 3 + (P("exp", "ctx"), P())
    )
    n = mesh.shape["ctx"]
    return jax.shard_map(
        functools.partial(local_part, n, n * mesh.shape["exp"]),
        mesh=mesh,
        in_specs=placed,
        out_specs=seq,
        check_vma=False,
    )
```

```python
import functools

import jax
import jax.numpy as jnp
from jax import lax
from jax.experimental import pallas as pl
from jax.experimental.pallas import tpu as pltpu
from jax.sharding import PartitionSpec as P

DK = 128
CAP = 4
EPS = 1e-06
AUX = 16
LANES = 128

bf16 = jnp.bfloat16
f32 = jnp.float32


def mm(a, b):
    return jnp.dot(a, b, preferred_element_type=f32)


def mm_nt(a, b):
    return lax.dot_general(a, b, (((1,), (1,)), ((), ())), preferred_element_type=f32)


def mm_tn(a, b):
    return lax.dot_general(a, b, (((0,), (0,)), ((), ())), preferred_element_type=f32)


def split2(x):
    hi = x.astype(bf16)
    return hi, (x - hi.astype(f32)).astype(bf16)


def split3(x):
    hi = x.astype(bf16)
    rest = x - hi.astype(f32)
    mid = rest.astype(bf16)
    return hi, mid, (rest - mid.astype(f32)).astype(bf16)


def mm3(a, b):
    (ah, al), (bh, bl) = a, b
    return mm(jnp.concatenate([ah, al, ah], axis=1), jnp.concatenate([bh, bh, bl], axis=0))


def iota(shape, dim):
    return lax.broadcasted_iota(jnp.int32, shape, dim)


def in_hbm(*arrays):
    return [pltpu.with_memory_space_constraint(a, pltpu.HBM) for a in arrays]


def compiler_params(mib):
    return pltpu.CompilerParams(vmem_limit_bytes=mib * 1024 * 1024)


def routes(n):
    return [(chips, flip) for chips in range(n // 2) for flip in (0, 1)]


def moved(index, route, n, back=False):
    chips, flip = route
    chip = lax.rem(index // 2 + (n // 2 - chips if back else chips), n // 2)
    return chip * 2 + lax.rem(lax.rem(index, 2) + flip, 2)


def send(x, route, n):
    chips, flip = route
    pairs = [(i, (i // 2 + chips) % (n // 2) * 2 + (i % 2 + flip) % 2) for i in range(n)]
    return lax.ppermute(x, "ctx", pairs)


def pack_kernel(n, kw, vw, k_ref, w_ref, d_ref, q_ref, v_ref, g_ref, *outs):
    local = vw // DK
    keyed, asked, gated = outs[:n], outs[n : 2 * n], outs[2 * n :]
    me = lax.axis_index("ctx")
    tokens = k_ref.shape[1]
    heads = d_ref.shape[1]
    ones = (iota((tokens, tokens), 0) <= iota((tokens, tokens), 1)).astype(bf16)
    logs = jnp.log(d_ref[0])
    sums = sum(mm(piece, ones) for piece in reversed(split3(logs)))
    pieces = [p.astype(f32) for p in (*split3(sums), *split3(w_ref[0]))]
    rates = jnp.concatenate(pieces, axis=0).astype(bf16)
    rows = AUX * kw // LANES
    row, entry = iota((rows, 6 * heads), 0), iota((rows, 6 * heads), 1)
    for i, route in enumerate(routes(n)):
        to = moved(me, route, n)
        kat = pl.ds(pl.multiple_of(to * kw, LANES), kw)
        keyed[i][0:tokens] = k_ref[0, :, kat]
        wanted = row // local * heads + to * local + lax.rem(row, local)
        aux = mm(((row < 6 * local) & (entry == wanted)).astype(bf16), rates)
        for at in range(kw // LANES):
            keyed[i][tokens:, at * LANES : (at + 1) * LANES] = aux[at * AUX : (at + 1) * AUX].astype(bf16)
        asked[i][:, 0:kw] = q_ref[0, :, kat]
        asked[i][:, kw:] = v_ref[0, :, pl.ds(pl.multiple_of(to * vw, LANES), vw)]
    for j, out in enumerate(gated):
        chip = lax.rem(me // 2 + j + 1, n // 2)
        out[...] = g_ref[0, :, pl.ds(pl.multiple_of(chip * 2 * vw, LANES), 2 * vw)]


def head_rates(local, keyed, tokens):
    aux = jnp.concatenate(
        [keyed[tokens:, i * LANES : (i + 1) * LANES] for i in range(keyed.shape[1] // LANES)], axis=0
    )
    row, col = iota((aux.shape[0], LANES), 0), iota((aux.shape[0], LANES), 1)
    same = (row < 6 * local) & (lax.rem(row, local) == lax.rem(col, local)) & (row // (3 * local) == col // local)
    return aux, (same & (col < 2 * local)).astype(bf16)


def both_halves(x):
    return jnp.concatenate(split2(x), axis=1)


def mm3_held(held, b):
    return mm(jnp.concatenate([held, held[:, : held.shape[1] // 2]], axis=1), b)


def stacked(x):
    high, low = split2(x)
    return jnp.concatenate([high, high, low], axis=0)


def inverse_scale(raw):
    raw_f = raw.astype(f32)
    return lax.rsqrt(jnp.sum(raw_f * raw_f, axis=1, keepdims=True) + EPS)


def inverse_kernel(n, local, *refs):
    keyed = refs[:n]
    value_ref, erase_ref, key_ref, row_ref = refs[n:]
    me = lax.axis_index("ctx")
    tokens = value_ref.shape[2]
    group = local * DK // keyed[0].shape[1]
    row, col = iota((tokens, tokens), 0), iota((tokens, tokens), 1)
    apart = lax.bitwise_xor(row, col)
    eye = (row == col).astype(f32)
    systems, scales = [], []
    for i, route in enumerate(routes(n)):
        block = moved(me, route, n, back=True)
        aux, total = head_rates(local, keyed[i], tokens)
        as_cols, as_rows = mm_tn(aux, total), mm_tn(total, aux)
        down, up = jnp.exp(as_rows), jnp.exp(-as_rows)
        left = jnp.exp(as_rows[:, tokens - 1 :] - as_rows)
        down_cols = jnp.exp(as_cols)
        for g in range(local // group):
            k = keyed[i][0:tokens, g * DK : (g + 1) * DK]
            k_t = k.astype(f32).T
            dots = mm_nt(k, k)
            diag = dots * eye
            k_row = lax.rsqrt(jnp.sum(diag, axis=0, keepdims=True) + EPS)
            k_col = lax.rsqrt(jnp.sum(diag, axis=1, keepdims=True) + EPS)
            dots = jnp.where(row > col, dots * k_row, 0.0)
            for h in range(g * group, (g + 1) * group):
                write = as_rows[local + h : local + h + 1]
                scale = as_cols[:, local + h : local + h + 1] * down_cols[:, h : h + 1] * k_col
                systems.append(scale * (up[h : h + 1] * dots))
                scales.append((write, write * down[h : h + 1] * k_row))
                key_ref[block, h] = both_halves(k_t * (left[h : h + 1] * k_row))
                row_ref[block, h, 0:1] = up[h : h + 1] * k_row
                row_ref[block, h, 1:2] = jnp.broadcast_to(down[h : h + 1, tokens - 1 :], (1, tokens))
    near = [jnp.where(apart < 16, s, 0.0) for s in systems]
    power = [split2(s) for s in near]
    inverse = [eye - s for s in near]
    power = [mm3(p, p) for p in power]
    for _ in range(2):
        halves = [split2(p) for p in power]
        both = [mm3(split2(jnp.concatenate([p, x], axis=0)), ps) for p, x, ps in zip(power, inverse, halves)]
        power = [b[:tokens] for b in both]
        inverse = [x + b[tokens:] for x, b in zip(inverse, both)]
    inverse = [x + mm3(split2(x), split2(p)) for x, p in zip(inverse, power)]
    size = 16
    while size < tokens:
        odd = [slice(at, at + size) for at in range(size, tokens, 2 * size)]
        beside = (apart >= size) & (apart < 2 * size)
        below = [jnp.where(beside, s, 0.0) for s in systems]
        below = [split2(jnp.concatenate([b[o] for o in odd], axis=0)) for b in below]
        halves = [split2(x) for x in inverse]
        first = [mm3(b, x) for b, x in zip(below, halves)]
        first = [split2(widen(f, size)) for f in first]
        lower = [tuple(jnp.concatenate([part[o] for o in odd], axis=0) for part in x) for x in halves]
        inverse = [x - widen(mm3(a, b), size) for x, a, b in zip(inverse, lower, first)]
        size *= 2
    for i, route in enumerate(routes(n)):
        block = moved(me, route, n, back=True)
        for h in range(local):
            for_values, for_state = scales[i * local + h]
            value_ref[block, h] = both_halves(inverse[i * local + h] * for_values)
            erase_ref[block, h] = both_halves(inverse[i * local + h] * for_state)


def widen(x, size):
    none = jnp.zeros((size, x.shape[1]), x.dtype)
    return jnp.concatenate(
        [part for at in range(0, x.shape[0], size) for part in (none, x[at : at + size])], axis=0
    )


def state_kernel(n, kw, vw, *refs):
    keyed, asked = refs[:n], refs[n : 2 * n]
    value_ref, erase_ref, key_ref, row_ref, gain_ref, keep_ref, give_ref, out_ref, kx_ref, qv_ref = refs[2 * n :]
    me = lax.axis_index("ctx")
    tokens = value_ref.shape[2]
    local = vw // DK
    group = vw // kw
    all_heads = range(local)
    for i, route in enumerate(routes(n)):
        block = moved(me, route, n, back=True)
        kx_ref[block] = keyed[i][...]
        qv_ref[block] = asked[i][...]
    row, col = iota((tokens, tokens), 0), iota((tokens, tokens), 1)
    gain = gain_ref[...]

    def prepare(block):
        aux, total = head_rates(local, kx_ref.at[block], tokens)
        down_cols = jnp.exp(mm_tn(aux, total))
        made = []
        for g in range(local // group):
            k = kx_ref[block, 0:tokens, g * DK : (g + 1) * DK]
            q = qv_ref[block, :, g * DK : (g + 1) * DK]
            q_col = inverse_scale(q) * DK ** (-0.5)
            dots = jnp.where(row >= col, mm_nt(q, k), 0.0)
            for h in range(g * group, (g + 1) * group):
                v = qv_ref[block, :, kw + h * DK : kw + (h + 1) * DK]
                made.append(
                    dict(
                        k=jnp.concatenate([k, k], axis=1),
                        q=jnp.concatenate([q, q], axis=1),
                        scores=both_halves(dots * row_ref[block, h, 0:1]),
                        scale=down_cols[:, h : h + 1] * q_col,
                        written=mm(value_ref[block, h], jnp.concatenate([v, v], axis=0)),
                    )
                )
        return made

    def finish(block, made, held, delta):
        for h in all_heads:
            out = mm3_held(made[h]["scores"], delta[h])
            if held is not None:
                out = out + mm(made[h]["q"], held[h])
            out = made[h]["scale"] * out
            mean = jnp.mean(out * out, axis=1, keepdims=True)
            out_ref[block, :, h * DK : (h + 1) * DK] = out * lax.rsqrt(mean + EPS) * gain

    states, before, made = None, None, prepare(0)
    for block in range(n):
        held = None
        delta = [m["written"] for m in made]
        if block > 0:
            held = [jnp.concatenate(split2(s), axis=0) for s in states]
            seen = [mm(m["k"], s) for m, s in zip(made, held)]
            finish(*before)
            delta = [d - mm3_held(erase_ref[block, h], stacked(seen[h])) for h, d in enumerate(delta)]
        later = prepare(block + 1) if block < n - 1 else None
        delta = [stacked(d) for d in delta]
        if block < n - 1:
            grown = [mm3_held(key_ref[block, h], delta[h]) for h in all_heads]
            if block == 0:
                states = grown
            else:
                states = [row_ref[block, h, 1:2] * states[h] + grown[h] for h in all_heads]
        before = (block, made, held, delta)
        made = later
    finish(*before)
    for j in range(n // 2):
        keep_ref[j] = out_ref[moved(me, (j, 0), n)]
        give_ref[j] = out_ref[moved(me, (j, 1), n)].astype(bf16)


def chip_projection(me, keep, other, gate_ref, start, proj_ref, proj_other_ref, columns):
    vw = keep.shape[1]
    mixed = []
    for heads, core in ((keep, lax.rem(me, 2)), (other, 1 - lax.rem(me, 2))):
        gate = gate_ref[:, pl.ds(pl.multiple_of(start + core * vw, LANES), vw)].astype(f32)
        mixed.append((heads.astype(f32) * (gate / (1.0 + jnp.exp(-gate)))).astype(bf16))
    for at in range(0, proj_ref.shape[1], columns):
        here = slice(at, at + columns)
        yield here, mm(mixed[0], proj_ref[:, here]) + mm(mixed[1], proj_other_ref[:, here])


def far_kernel(n, *refs):
    gated = refs[: n // 2 - 1]
    keep_ref, other_ref, proj_ref, proj_other_ref, *sums = refs[n // 2 - 1 :]
    me = lax.axis_index("ctx")
    for j, (gate_ref, out) in enumerate(zip(gated, sums), 1):
        for here, part in chip_projection(me, keep_ref[j], other_ref[j], gate_ref, 0, proj_ref, proj_other_ref, 512):
            out[:, here] = part.astype(bf16)


def home_kernel(
    residual_ref,
    gate_ref,
    keep_ref,
    other_ref,
    proj_ref,
    proj_other_ref,
    ids_ref,
    weight_ref,
    base_ref,
    picker_ref,
    table_ref,
):
    me = lax.axis_index("ctx")
    start = me // 2 * 2 * keep_ref.shape[2]
    gate_ref = gate_ref.at[0]
    for here, part in chip_projection(me, keep_ref[0], other_ref[0], gate_ref, start, proj_ref, proj_other_ref, 512):
        base_ref[:, here] = residual_ref[0, :, here].astype(f32) + part
    slots, tokens = table_ref.shape
    slot = iota((slots, tokens), 0)
    expert = slot // CAP
    named = jnp.zeros((slots, tokens), f32)
    weight = jnp.zeros((slots, tokens), f32)
    for j in range(ids_ref.shape[0]):
        hit = ids_ref[j] == expert
        named = named + hit.astype(f32)
        weight = weight + jnp.where(hit, weight_ref[j], 0.0)
    before = (iota((tokens, tokens), 0) < iota((tokens, tokens), 1)).astype(bf16)
    rank = mm(named.astype(bf16), before)
    chosen = jnp.where(rank == lax.rem(slot, CAP).astype(f32), named, 0.0)
    table_ref[...] = chosen * weight
    picker_ref[...] = chosen.astype(bf16)


def dispatch_kernel(base_ref, gain_ref, picker_ref, *refs):
    part_refs = refs[:-2]
    hidden_ref, rows_ref = refs[-2:]
    width = hidden_ref.shape[1]
    squares = 0.0
    step = 512
    for c in range(0, width, step):
        total = base_ref[:, c : c + step]
        for part in part_refs:
            total = total + part[:, c : c + step].astype(f32)
        hidden_ref[:, c : c + step] = total
        squares = squares + jnp.sum(total * total, axis=1, keepdims=True)
    scale = lax.rsqrt(squares * (1.0 / width) + EPS)
    picker = picker_ref[...]
    for c in range(0, width, step):
        normed = (hidden_ref[:, c : c + step] * scale * gain_ref[:, c : c + step]).astype(bf16)
        rows = mm(picker, normed).astype(bf16)
        rows_ref[:, :, c : c + step] = rows.reshape(*rows_ref.shape[:2], step)


def expert_kernel(rows_ref, gate_ref, up_ref, down_ref, out_ref):
    sources, cap, width = rows_ref.shape
    tile = min(sources, 128 // cap)

    def one(t, carry):
        here = pl.ds(t * tile, tile)
        x = rows_ref[here].reshape(tile * cap, width)
        gate = mm(x, gate_ref[0])
        up = mm(x, up_ref[0])
        act = (gate / (1.0 + jnp.exp(-gate)) * up).astype(bf16)
        step = 512
        for c in range(0, width, step):
            y = mm(act, down_ref[0, :, c : c + step]).astype(bf16)
            out_ref[here, :, c : c + step] = y.reshape(tile, cap, step)
        return carry

    if sources == tile:
        one(0, 0)
    else:
        lax.fori_loop(0, sources // tile, one, 0)


def combine_kernel(hidden_ref, table_ref, back_ref, mask_ref, dir_ref, out_ref, sum_ref):
    tokens, width = hidden_ref.shape
    slots = table_ref.shape[0]
    table = jnp.concatenate(split2(table_ref[...]), axis=0)
    direction = dir_ref[...]
    unit = direction / jnp.sqrt(jnp.sum(direction * direction, axis=1, keepdims=True) + EPS)
    eye = iota((tokens, tokens), 0) == iota((tokens, tokens), 1)
    mask = jnp.sum(jnp.where(eye, mask_ref[...].astype(f32), 0.0), axis=1, keepdims=True)
    along = 0.0
    step = 256
    for c in range(0, width, step):
        back = back_ref[:, :, c : c + step].reshape(slots, step)
        total = hidden_ref[:, c : c + step] + mm_tn(table, jnp.concatenate([back, back], axis=0))
        sum_ref[:, c : c + step] = total
        along = along + jnp.sum(total * unit[:, c : c + step], axis=1, keepdims=True)
    out_ref[0] = (sum_ref[...] - (mask * along) * unit).astype(bf16)


def local_part(
    n,
    devices,
    queries,
    keys,
    values,
    out_gate,
    write_rate,
    decay,
    head_gain,
    residual,
    out_proj,
    ffn_gain,
    expert_ids,
    route_weight,
    w_gate,
    w_up,
    w_down,
    ablate_mask,
    direction,
):
    tokens = queries.shape[1]
    width = residual.shape[2]
    kw, vw = keys.shape[2] // n, values.shape[2] // n
    chips = n // 2
    slots = devices * CAP
    shape = jax.ShapeDtypeStruct

    local = vw // DK
    ways = routes(n)
    keyed_shape = shape((tokens + AUX, kw), bf16)
    with jax.named_scope("pack"):
        packed = pl.pallas_call(
            functools.partial(pack_kernel, n, kw, vw),
            out_shape=[keyed_shape] * n
            + [shape((tokens, kw + vw), bf16)] * n
            + [shape((tokens, 2 * vw), bf16)] * (chips - 1),
            compiler_params=compiler_params(16),
        )(*in_hbm(keys, write_rate.transpose(0, 2, 1), decay.transpose(0, 2, 1), queries, values, out_gate))
        keyed, asked, gated = list(packed[:n]), list(packed[n : 2 * n]), packed[2 * n :]
    with jax.named_scope("heads_exchange"):
        order = [i for i, route in enumerate(ways) if route[0]] + [1]
        for i in order:
            keyed[i] = send(keyed[i], ways[i], n)
        for i in order[:-1]:
            asked[i] = send(asked[i], ways[i], n)
    with jax.named_scope("block_inverses"):
        wide = shape((n, local, tokens, 2 * tokens), bf16)
        inverses = pl.pallas_call(
            functools.partial(inverse_kernel, n, local),
            out_shape=[wide, wide, shape((n, local, DK, 2 * tokens), bf16), shape((n, local, 8, tokens), f32)],
            compiler_params=compiler_params(16),
            cost_estimate=pl.CostEstimate(flops=6 * 10**9, bytes_accessed=10**6, transcendentals=0),
        )(*keyed)
    with jax.named_scope("late_exchange"):
        proj = out_proj
        keyed, asked[1], gated = lax.optimization_barrier((keyed, asked[1], gated))
        asked[1] = send(asked[1], ways[1], n)
        gated = [send(gate, (j, 0), n) for j, gate in enumerate(gated, 1)]
        proj_other = send(proj, (0, 1), n)
    with jax.named_scope("states"):
        keep, give = pl.pallas_call(
            functools.partial(state_kernel, n, kw, vw),
            out_shape=[shape((chips, tokens, vw), f32), shape((chips, tokens, vw), bf16)],
            scratch_shapes=[
                pltpu.VMEM((n, tokens, vw), f32),
                pltpu.VMEM((n, tokens + AUX, kw), bf16),
                pltpu.VMEM((n, tokens, kw + vw), bf16),
            ],
            compiler_params=compiler_params(16),
            cost_estimate=pl.CostEstimate(flops=4 * 10**9, bytes_accessed=10**6, transcendentals=0),
        )(*keyed, *asked, *inverses, head_gain.reshape(1, -1))
    with jax.named_scope("far_projection"):
        other = send(give, (0, 1), n)
        sums = pl.pallas_call(
            functools.partial(far_kernel, n),
            out_shape=[shape((tokens, width), bf16)] * (chips - 1),
            compiler_params=compiler_params(16),
        )(*gated, keep, other, out_proj, proj_other)
    with jax.named_scope("projection_sum"):
        parts = [send(part, (j, 0), n) for j, part in enumerate(sums, 1)]
    with jax.named_scope("home"):
        base, picker, table = pl.pallas_call(
            home_kernel,
            out_shape=[shape((tokens, width), f32), shape((slots, tokens), bf16), shape((slots, tokens), f32)],
            compiler_params=compiler_params(16),
            cost_estimate=pl.CostEstimate(flops=1000, bytes_accessed=1000, transcendentals=0),
        )(
            residual,
            out_gate,
            keep,
            other,
            out_proj,
            proj_other,
            expert_ids.transpose(2, 0, 1),
            route_weight.transpose(2, 0, 1),
        )
    with jax.named_scope("dispatch"):
        hidden, rows = pl.pallas_call(
            dispatch_kernel,
            out_shape=[shape((tokens, width), f32), shape((devices, CAP, width), bf16)],
            compiler_params=compiler_params(24),
        )(base, ffn_gain.reshape(1, -1), picker, *parts)
    with jax.named_scope("to_experts"):
        came = lax.all_to_all(rows, ("ctx", "exp"), 0, 0, tiled=True)
    with jax.named_scope("experts"):
        done = pl.pallas_call(
            expert_kernel,
            out_shape=shape((devices, CAP, width), bf16),
            compiler_params=compiler_params(24),
        )(came, w_gate, w_up, w_down)
    with jax.named_scope("from_experts"):
        back = lax.all_to_all(done, ("ctx", "exp"), 0, 0, tiled=True)
    with jax.named_scope("combine"):
        return pl.pallas_call(
            combine_kernel,
            out_shape=shape((1, tokens, width), bf16),
            scratch_shapes=[pltpu.VMEM((tokens, width), f32)],
            compiler_params=compiler_params(24),
        )(hidden, table, back, ablate_mask, direction.reshape(1, -1))


def solution(mesh):
    seq = P("exp", "ctx", None)
    owned = P(("ctx", "exp"), None, None)
    placed = (
        (seq,) * 6 + (P(), seq, P("ctx", None), P(), seq, seq) + (owned,) * 3 + (P("exp", "ctx"), P())
    )
    n = mesh.shape["ctx"]
    return jax.shard_map(
        functools.partial(local_part, n, n * mesh.shape["exp"]),
        mesh=mesh,
        in_specs=placed,
        out_specs=seq,
        check_vma=False,
    )
```

```python
import functools

import jax
import jax.numpy as jnp
from jax import lax
from jax.experimental import pallas as pl
from jax.experimental.pallas import tpu as pltpu
from jax.sharding import PartitionSpec as P

DK = 128
CAP = 4
EPS = 1e-06
AUX = 16
LANES = 128

bf16 = jnp.bfloat16
f32 = jnp.float32


def mm(a, b):
    return jnp.dot(a, b, preferred_element_type=f32)


def mm_nt(a, b):
    return lax.dot_general(a, b, (((1,), (1,)), ((), ())), preferred_element_type=f32)


def mm_tn(a, b):
    return lax.dot_general(a, b, (((0,), (0,)), ((), ())), preferred_element_type=f32)


def split2(x):
    hi = x.astype(bf16)
    return hi, (x - hi.astype(f32)).astype(bf16)


def split3(x):
    hi = x.astype(bf16)
    rest = x - hi.astype(f32)
    mid = rest.astype(bf16)
    return hi, mid, (rest - mid.astype(f32)).astype(bf16)


def mm3(a, b):
    (ah, al), (bh, bl) = a, b
    return mm(jnp.concatenate([ah, al, ah], axis=1), jnp.concatenate([bh, bh, bl], axis=0))


def iota(shape, dim):
    return lax.broadcasted_iota(jnp.int32, shape, dim)


def in_hbm(*arrays):
    return [pltpu.with_memory_space_constraint(a, pltpu.HBM) for a in arrays]


def compiler_params(mib):
    return pltpu.CompilerParams(vmem_limit_bytes=mib * 1024 * 1024)


def routes(n):
    return [(chips, flip) for chips in range(n // 2) for flip in (0, 1)]


def moved(index, route, n, back=False):
    chips, flip = route
    chip = lax.rem(index // 2 + (n // 2 - chips if back else chips), n // 2)
    return chip * 2 + lax.rem(lax.rem(index, 2) + flip, 2)


def send(x, route, n):
    chips, flip = route
    pairs = [(i, (i // 2 + chips) % (n // 2) * 2 + (i % 2 + flip) % 2) for i in range(n)]
    return lax.ppermute(x, "ctx", pairs)


def pack_kernel(n, kw, vw, k_ref, w_ref, d_ref, q_ref, v_ref, g_ref, *outs):
    local = vw // DK
    keyed, asked, gated = outs[:n], outs[n : 2 * n], outs[2 * n :]
    me = lax.axis_index("ctx")
    tokens = k_ref.shape[1]
    heads = d_ref.shape[1]
    pieces = [p.astype(f32) for p in (*split3(d_ref[0]), *split3(w_ref[0]))]
    rates = jnp.concatenate(pieces, axis=0).astype(bf16)
    rows = AUX * kw // LANES
    row, entry = iota((rows, 6 * heads), 0), iota((rows, 6 * heads), 1)
    for i, route in enumerate(routes(n)):
        to = moved(me, route, n)
        kat = pl.ds(pl.multiple_of(to * kw, LANES), kw)
        keyed[i][0:tokens] = k_ref[0, :, kat]
        wanted = row // local * heads + to * local + lax.rem(row, local)
        aux = mm(((row < 6 * local) & (entry == wanted)).astype(bf16), rates)
        for at in range(kw // LANES):
            keyed[i][tokens:, at * LANES : (at + 1) * LANES] = aux[at * AUX : (at + 1) * AUX].astype(bf16)
        asked[i][:, 0:kw] = q_ref[0, :, kat]
        asked[i][:, kw:] = v_ref[0, :, pl.ds(pl.multiple_of(to * vw, LANES), vw)]
    for j, out in enumerate(gated):
        chip = lax.rem(me // 2 + j + 1, n // 2)
        out[...] = g_ref[0, :, pl.ds(pl.multiple_of(chip * 2 * vw, LANES), 2 * vw)]


def head_rates(local, keyed, tokens):
    aux = jnp.concatenate(
        [keyed[tokens:, i * LANES : (i + 1) * LANES] for i in range(keyed.shape[1] // LANES)], axis=0
    )
    row, col = iota((aux.shape[0], LANES), 0), iota((aux.shape[0], LANES), 1)
    same = (row < 6 * local) & (lax.rem(row, local) == lax.rem(col, local)) & (row // (3 * local) == col // local)
    return aux, (same & (col < 2 * local)).astype(bf16)


def both_halves(x):
    return jnp.concatenate(split2(x), axis=1)


def mm3_held(held, b):
    return mm(jnp.concatenate([held, held[:, : held.shape[1] // 2]], axis=1), b)


def stacked(x):
    high, low = split2(x)
    return jnp.concatenate([high, high, low], axis=0)


def inverse_scale(raw):
    raw_f = raw.astype(f32)
    return lax.rsqrt(jnp.sum(raw_f * raw_f, axis=1, keepdims=True) + EPS)


def inverse_kernel(n, local, *refs):
    keyed = refs[:n]
    value_ref, erase_ref, key_ref, row_ref, down_ref = refs[n:]
    me = lax.axis_index("ctx")
    tokens = value_ref.shape[2]
    group = local * DK // keyed[0].shape[1]
    row, col = iota((tokens, tokens), 0), iota((tokens, tokens), 1)
    apart = lax.bitwise_xor(row, col)
    eye = (row == col).astype(f32)
    ones = (row >= col).astype(bf16)
    systems, scales = [], []
    for i, route in enumerate(routes(n)):
        block = moved(me, route, n, back=True)
        aux, total = head_rates(local, keyed[i], tokens)
        as_cols, as_rows = mm_tn(aux, total), mm_tn(total, aux)
        decays = jnp.where(iota((8, tokens), 0) < local, as_rows[0:8], 1.0)
        logs = [piece.astype(f32) for piece in split3(jnp.log(decays))]
        logs = jnp.concatenate(logs, axis=0).astype(bf16)
        sums = mm_nt(logs, ones)
        sums = sums[16:24] + sums[8:16] + sums[0:8]
        sum_cols = mm_nt(ones, logs)
        down, up = jnp.exp(sums), jnp.exp(-sums)
        left = jnp.exp(sums[:, tokens - 1 :] - sums)
        down_cols = jnp.exp(sum_cols[:, 16:24] + sum_cols[:, 8:16] + sum_cols[:, 0:8])
        down_ref[block] = jnp.concatenate([down_cols, jnp.zeros((tokens, LANES - 8), f32)], axis=1)
        for g in range(local // group):
            k = keyed[i][0:tokens, g * DK : (g + 1) * DK]
            k_t = k.astype(f32).T
            dots = mm_nt(k, k)
            diag = dots * eye
            k_row = lax.rsqrt(jnp.sum(diag, axis=0, keepdims=True) + EPS)
            k_col = lax.rsqrt(jnp.sum(diag, axis=1, keepdims=True) + EPS)
            dots = jnp.where(row > col, dots * k_row, 0.0)
            for h in range(g * group, (g + 1) * group):
                write = as_rows[local + h : local + h + 1]
                scale = as_cols[:, local + h : local + h + 1] * down_cols[:, h : h + 1] * k_col
                systems.append(scale * (up[h : h + 1] * dots))
                scales.append((write, write * down[h : h + 1] * k_row))
                key_ref[block, h] = both_halves(k_t * (left[h : h + 1] * k_row))
                row_ref[block, h, 0:1] = up[h : h + 1] * k_row
                row_ref[block, h, 1:2] = jnp.broadcast_to(down[h : h + 1, tokens - 1 :], (1, tokens))
    near = [jnp.where(apart < 16, s, 0.0) for s in systems]
    power = [split2(s) for s in near]
    inverse = [eye - s for s in near]
    power = [mm3(p, p) for p in power]
    for _ in range(2):
        halves = [split2(p) for p in power]
        both = [mm3(split2(jnp.concatenate([p, x], axis=0)), ps) for p, x, ps in zip(power, inverse, halves)]
        power = [b[:tokens] for b in both]
        inverse = [x + b[tokens:] for x, b in zip(inverse, both)]
    inverse = [x + mm3(split2(x), split2(p)) for x, p in zip(inverse, power)]
    size = 16
    while size < tokens:
        odd = [slice(at, at + size) for at in range(size, tokens, 2 * size)]
        beside = (apart >= size) & (apart < 2 * size)
        below = [jnp.where(beside, s, 0.0) for s in systems]
        below = [split2(jnp.concatenate([b[o] for o in odd], axis=0)) for b in below]
        halves = [split2(x) for x in inverse]
        first = [mm3(b, x) for b, x in zip(below, halves)]
        first = [split2(widen(f, size)) for f in first]
        lower = [tuple(jnp.concatenate([part[o] for o in odd], axis=0) for part in x) for x in halves]
        inverse = [x - widen(mm3(a, b), size) for x, a, b in zip(inverse, lower, first)]
        size *= 2
    for i, route in enumerate(routes(n)):
        block = moved(me, route, n, back=True)
        for h in range(local):
            for_values, for_state = scales[i * local + h]
            value_ref[block, h] = both_halves(inverse[i * local + h] * for_values)
            erase_ref[block, h] = both_halves(inverse[i * local + h] * for_state)


def widen(x, size):
    none = jnp.zeros((size, x.shape[1]), x.dtype)
    return jnp.concatenate(
        [part for at in range(0, x.shape[0], size) for part in (none, x[at : at + size])], axis=0
    )


def state_kernel(n, kw, vw, *refs):
    keyed, asked = refs[:n], refs[n : 2 * n]
    value_ref, erase_ref, key_ref, row_ref, down_ref, gain_ref, keep_ref, give_ref, out_ref, kx_ref, qv_ref = refs[2 * n :]
    me = lax.axis_index("ctx")
    tokens = value_ref.shape[2]
    local = vw // DK
    group = vw // kw
    all_heads = range(local)
    for i, route in enumerate(routes(n)):
        block = moved(me, route, n, back=True)
        kx_ref[block] = keyed[i][...]
        qv_ref[block] = asked[i][...]
    row, col = iota((tokens, tokens), 0), iota((tokens, tokens), 1)
    gain = gain_ref[...]

    def prepare(block):
        down_cols = down_ref[block]
        made = []
        for g in range(local // group):
            k = kx_ref[block, 0:tokens, g * DK : (g + 1) * DK]
            q = qv_ref[block, :, g * DK : (g + 1) * DK]
            q_col = inverse_scale(q) * DK ** (-0.5)
            dots = jnp.where(row >= col, mm_nt(q, k), 0.0)
            for h in range(g * group, (g + 1) * group):
                v = qv_ref[block, :, kw + h * DK : kw + (h + 1) * DK]
                made.append(
                    dict(
                        k=jnp.concatenate([k, k], axis=1),
                        q=jnp.concatenate([q, q], axis=1),
                        scores=both_halves(dots * row_ref[block, h, 0:1]),
                        scale=down_cols[:, h : h + 1] * q_col,
                        written=mm(value_ref[block, h], jnp.concatenate([v, v], axis=0)),
                    )
                )
        return made

    def finish(block, made, held, delta):
        for h in all_heads:
            out = mm3_held(made[h]["scores"], delta[h])
            if held is not None:
                out = out + mm(made[h]["q"], held[h])
            out = made[h]["scale"] * out
            mean = jnp.mean(out * out, axis=1, keepdims=True)
            out_ref[block, :, h * DK : (h + 1) * DK] = out * lax.rsqrt(mean + EPS) * gain

    states, before, made = None, None, prepare(0)
    for block in range(n):
        held = None
        delta = [m["written"] for m in made]
        if block > 0:
            held = [jnp.concatenate(split2(s), axis=0) for s in states]
            seen = [mm(m["k"], s) for m, s in zip(made, held)]
            finish(*before)
            delta = [d - mm3_held(erase_ref[block, h], stacked(seen[h])) for h, d in enumerate(delta)]
        later = prepare(block + 1) if block < n - 1 else None
        delta = [stacked(d) for d in delta]
        if block < n - 1:
            grown = [mm3_held(key_ref[block, h], delta[h]) for h in all_heads]
            if block == 0:
                states = grown
            else:
                states = [row_ref[block, h, 1:2] * states[h] + grown[h] for h in all_heads]
        before = (block, made, held, delta)
        made = later
    finish(*before)
    for j in range(n // 2):
        keep_ref[j] = out_ref[moved(me, (j, 0), n)]
        give_ref[j] = out_ref[moved(me, (j, 1), n)].astype(bf16)


def chip_projection(me, keep, other, gate_ref, start, proj_ref, proj_other_ref, columns):
    vw = keep.shape[1]
    mixed = []
    for heads, core in ((keep, lax.rem(me, 2)), (other, 1 - lax.rem(me, 2))):
        gate = gate_ref[:, pl.ds(pl.multiple_of(start + core * vw, LANES), vw)].astype(f32)
        mixed.append((heads.astype(f32) * (gate / (1.0 + jnp.exp(-gate)))).astype(bf16))
    for at in range(0, proj_ref.shape[1], columns):
        here = slice(at, at + columns)
        yield here, mm(mixed[0], proj_ref[:, here]) + mm(mixed[1], proj_other_ref[:, here])


def far_kernel(n, *refs):
    gated = refs[: n // 2 - 1]
    keep_ref, other_ref, proj_ref, proj_other_ref, *sums = refs[n // 2 - 1 :]
    me = lax.axis_index("ctx")
    for j, (gate_ref, out) in enumerate(zip(gated, sums), 1):
        for here, part in chip_projection(me, keep_ref[j], other_ref[j], gate_ref, 0, proj_ref, proj_other_ref, 512):
            out[:, here] = part.astype(bf16)


def home_kernel(
    n,
    residual_ref,
    gate_ref,
    keep_ref,
    other_ref,
    proj_ref,
    proj_other_ref,
    ids_ref,
    weight_ref,
    base_ref,
    picker_ref,
    table_ref,
):
    me = lax.axis_index("ctx")
    start = me // 2 * 2 * keep_ref.shape[2]
    gate_ref = gate_ref.at[0]
    for here, part in chip_projection(me, keep_ref[0], other_ref[0], gate_ref, start, proj_ref, proj_other_ref, 512):
        base_ref[:, here] = residual_ref[0, :, here].astype(f32) + part
    slots, tokens = table_ref.shape
    slot = iota((slots, tokens), 0)
    place = slot // CAP
    expert = lax.rem(place, n) * (slots // CAP // n) + place // n
    named = jnp.zeros((slots, tokens), f32)
    weight = jnp.zeros((slots, tokens), f32)
    for j in range(ids_ref.shape[0]):
        hit = ids_ref[j] == expert
        named = named + hit.astype(f32)
        weight = weight + jnp.where(hit, weight_ref[j], 0.0)
    before = (iota((tokens, tokens), 0) < iota((tokens, tokens), 1)).astype(bf16)
    rank = mm(named.astype(bf16), before)
    chosen = jnp.where(rank == lax.rem(slot, CAP).astype(f32), named, 0.0)
    table_ref[...] = chosen * weight
    picker_ref[...] = chosen.astype(bf16)


def dispatch_kernel(base_ref, gain_ref, picker_ref, *refs):
    part_refs = refs[:-2]
    hidden_ref, rows_ref = refs[-2:]
    width = hidden_ref.shape[1]
    squares = 0.0
    step = 512
    for c in range(0, width, step):
        total = base_ref[:, c : c + step]
        for part in part_refs:
            total = total + part[:, c : c + step].astype(f32)
        hidden_ref[:, c : c + step] = total
        squares = squares + jnp.sum(total * total, axis=1, keepdims=True)
    scale = lax.rsqrt(squares * (1.0 / width) + EPS)
    picker = picker_ref[...]
    for c in range(0, width, step):
        normed = (hidden_ref[:, c : c + step] * scale * gain_ref[:, c : c + step]).astype(bf16)
        rows = mm(picker, normed).astype(bf16)
        rows_ref[:, :, c : c + step] = rows.reshape(*rows_ref.shape[:2], step)


def expert_kernel(rows_ref, gate_ref, up_ref, down_ref, out_ref):
    sources, cap, width = rows_ref.shape
    tile = min(sources, 128 // cap)

    def one(t, carry):
        here = pl.ds(t * tile, tile)
        x = rows_ref[here].reshape(tile * cap, width)
        gate = mm(x, gate_ref[0])
        up = mm(x, up_ref[0])
        act = (gate / (1.0 + jnp.exp(-gate)) * up).astype(bf16)
        step = 512
        for c in range(0, width, step):
            y = mm(act, down_ref[0, :, c : c + step]).astype(bf16)
            out_ref[here, :, c : c + step] = y.reshape(tile, cap, step)
        return carry

    if sources == tile:
        one(0, 0)
    else:
        lax.fori_loop(0, sources // tile, one, 0)


def combine_kernel(hidden_ref, table_ref, back_ref, mask_ref, dir_ref, out_ref, sum_ref):
    tokens, width = hidden_ref.shape
    slots = table_ref.shape[0]
    table = jnp.concatenate(split2(table_ref[...]), axis=0)
    direction = dir_ref[...]
    unit = direction / jnp.sqrt(jnp.sum(direction * direction, axis=1, keepdims=True) + EPS)
    eye = iota((tokens, tokens), 0) == iota((tokens, tokens), 1)
    mask = jnp.sum(jnp.where(eye, mask_ref[...].astype(f32), 0.0), axis=1, keepdims=True)
    along = 0.0
    step = 256
    for c in range(0, width, step):
        back = back_ref[:, :, c : c + step].reshape(slots, step)
        total = hidden_ref[:, c : c + step] + mm_tn(table, jnp.concatenate([back, back], axis=0))
        sum_ref[:, c : c + step] = total
        along = along + jnp.sum(total * unit[:, c : c + step], axis=1, keepdims=True)
    out_ref[0] = (sum_ref[...] - (mask * along) * unit).astype(bf16)


def local_part(
    n,
    devices,
    queries,
    keys,
    values,
    out_gate,
    write_rate,
    decay,
    head_gain,
    residual,
    out_proj,
    ffn_gain,
    expert_ids,
    route_weight,
    w_gate,
    w_up,
    w_down,
    ablate_mask,
    direction,
):
    tokens = queries.shape[1]
    width = residual.shape[2]
    kw, vw = keys.shape[2] // n, values.shape[2] // n
    chips = n // 2
    slots = devices * CAP
    shape = jax.ShapeDtypeStruct

    local = vw // DK
    ways = routes(n)
    keyed_shape = shape((tokens + AUX, kw), bf16)
    with jax.named_scope("pack"):
        packed = pl.pallas_call(
            functools.partial(pack_kernel, n, kw, vw),
            out_shape=[keyed_shape] * n
            + [shape((tokens, kw + vw), bf16)] * n
            + [shape((tokens, 2 * vw), bf16)] * (chips - 1),
            compiler_params=compiler_params(16),
        )(*in_hbm(keys, write_rate.transpose(0, 2, 1), decay.transpose(0, 2, 1), queries, values, out_gate))
        keyed, asked, gated = list(packed[:n]), list(packed[n : 2 * n]), packed[2 * n :]
    with jax.named_scope("heads_exchange"):
        order = [i for i, route in enumerate(ways) if route[0]] + [1]
        for i in order:
            keyed[i] = send(keyed[i], ways[i], n)
        for i in order[:-1]:
            asked[i] = send(asked[i], ways[i], n)
    with jax.named_scope("block_inverses"):
        wide = shape((n, local, tokens, 2 * tokens), bf16)
        inverses = pl.pallas_call(
            functools.partial(inverse_kernel, n, local),
            out_shape=[wide, wide, shape((n, local, DK, 2 * tokens), bf16), shape((n, local, 8, tokens), f32), shape((n, tokens, LANES), f32)],
            compiler_params=compiler_params(16),
            cost_estimate=pl.CostEstimate(flops=6 * 10**9, bytes_accessed=10**6, transcendentals=0),
        )(*keyed)
    with jax.named_scope("late_exchange"):
        proj = out_proj
        keyed, asked[1], gated = lax.optimization_barrier((keyed, asked[1], gated))
        asked[1] = send(asked[1], ways[1], n)
        gated = [send(gate, (j, 0), n) for j, gate in enumerate(gated, 1)]
        proj_other = send(proj, (0, 1), n)
    with jax.named_scope("states"):
        keep, give = pl.pallas_call(
            functools.partial(state_kernel, n, kw, vw),
            out_shape=[shape((chips, tokens, vw), f32), shape((chips, tokens, vw), bf16)],
            scratch_shapes=[
                pltpu.VMEM((n, tokens, vw), f32),
                pltpu.VMEM((n, tokens + AUX, kw), bf16),
                pltpu.VMEM((n, tokens, kw + vw), bf16),
            ],
            compiler_params=compiler_params(16),
            cost_estimate=pl.CostEstimate(flops=4 * 10**9, bytes_accessed=10**6, transcendentals=0),
        )(*keyed, *asked, *inverses, head_gain.reshape(1, -1))
    with jax.named_scope("far_projection"):
        other = send(give, (0, 1), n)
        sums = pl.pallas_call(
            functools.partial(far_kernel, n),
            out_shape=[shape((tokens, width), bf16)] * (chips - 1),
            compiler_params=compiler_params(16),
        )(*gated, keep, other, out_proj, proj_other)
    with jax.named_scope("projection_sum"):
        parts = [send(part, (j, 0), n) for j, part in enumerate(sums, 1)]
    with jax.named_scope("home"):
        base, picker, table = pl.pallas_call(
            functools.partial(home_kernel, n),
            out_shape=[shape((tokens, width), f32), shape((slots, tokens), bf16), shape((slots, tokens), f32)],
            compiler_params=compiler_params(16),
            cost_estimate=pl.CostEstimate(flops=1000, bytes_accessed=1000, transcendentals=0),
        )(
            residual,
            out_gate,
            keep,
            other,
            out_proj,
            proj_other,
            expert_ids.transpose(2, 0, 1),
            route_weight.transpose(2, 0, 1),
        )
    with jax.named_scope("dispatch"):
        hidden, rows = pl.pallas_call(
            dispatch_kernel,
            out_shape=[shape((tokens, width), f32), shape((devices, CAP, width), bf16)],
            compiler_params=compiler_params(24),
        )(base, ffn_gain.reshape(1, -1), picker, *parts)
    with jax.named_scope("to_experts"):
        came = lax.all_to_all(rows, ("exp", "ctx"), 0, 0, tiled=True)
    with jax.named_scope("experts"):
        done = pl.pallas_call(
            expert_kernel,
            out_shape=shape((devices, CAP, width), bf16),
            compiler_params=compiler_params(24),
        )(came, w_gate, w_up, w_down)
    with jax.named_scope("from_experts"):
        back = lax.all_to_all(done, ("exp", "ctx"), 0, 0, tiled=True)
    with jax.named_scope("combine"):
        return pl.pallas_call(
            combine_kernel,
            out_shape=shape((1, tokens, width), bf16),
            scratch_shapes=[pltpu.VMEM((tokens, width), f32)],
            compiler_params=compiler_params(24),
        )(hidden, table, back, ablate_mask, direction.reshape(1, -1))


def solution(mesh):
    seq = P("exp", "ctx", None)
    owned = P(("ctx", "exp"), None, None)
    placed = (
        (seq,) * 6 + (P(), seq, P("ctx", None), P(), seq, seq) + (owned,) * 3 + (P("exp", "ctx"), P())
    )
    n = mesh.shape["ctx"]
    return jax.shard_map(
        functools.partial(local_part, n, n * mesh.shape["exp"]),
        mesh=mesh,
        in_specs=placed,
        out_specs=seq,
        check_vma=False,
    )
```

```python
import functools

import jax
import jax.numpy as jnp
from jax import lax
from jax.experimental import pallas as pl
from jax.experimental.pallas import tpu as pltpu
from jax.sharding import PartitionSpec as P

DK = 128
CAP = 4
EPS = 1e-06
AUX = 16
LANES = 128

bf16 = jnp.bfloat16
f32 = jnp.float32


def mm(a, b):
    return jnp.dot(a, b, preferred_element_type=f32)


def mm_nt(a, b):
    return lax.dot_general(a, b, (((1,), (1,)), ((), ())), preferred_element_type=f32)


def mm_tn(a, b):
    return lax.dot_general(a, b, (((0,), (0,)), ((), ())), preferred_element_type=f32)


def split2(x):
    hi = x.astype(bf16)
    return hi, (x - hi.astype(f32)).astype(bf16)


def split3(x):
    hi = x.astype(bf16)
    rest = x - hi.astype(f32)
    mid = rest.astype(bf16)
    return hi, mid, (rest - mid.astype(f32)).astype(bf16)


def mm3(a, b):
    (ah, al), (bh, bl) = a, b
    return mm(jnp.concatenate([ah, al, ah], axis=1), jnp.concatenate([bh, bh, bl], axis=0))


def iota(shape, dim):
    return lax.broadcasted_iota(jnp.int32, shape, dim)


def in_hbm(*arrays):
    return [pltpu.with_memory_space_constraint(a, pltpu.HBM) for a in arrays]


def compiler_params(mib):
    return pltpu.CompilerParams(vmem_limit_bytes=mib * 1024 * 1024)


def routes(n):
    return [(chips, flip) for chips in range(n // 2) for flip in (0, 1)]


def moved(index, route, n, back=False):
    chips, flip = route
    chip = lax.rem(index // 2 + (n // 2 - chips if back else chips), n // 2)
    return chip * 2 + lax.rem(lax.rem(index, 2) + flip, 2)


def send(x, route, n):
    chips, flip = route
    pairs = [(i, (i // 2 + chips) % (n // 2) * 2 + (i % 2 + flip) % 2) for i in range(n)]
    return lax.ppermute(x, "ctx", pairs)


def pack_kernel(n, kw, vw, k_ref, w_ref, d_ref, q_ref, v_ref, *outs):
    local = vw // DK
    keyed, asked = outs[:n], outs[n:]
    me = lax.axis_index("ctx")
    tokens = k_ref.shape[1]
    heads = d_ref.shape[1]
    pieces = [p.astype(f32) for p in (*split3(d_ref[0]), *split3(w_ref[0]))]
    rates = jnp.concatenate(pieces, axis=0).astype(bf16)
    rows = AUX * kw // LANES
    row, entry = iota((rows, 6 * heads), 0), iota((rows, 6 * heads), 1)
    for i, route in enumerate(routes(n)):
        to = moved(me, route, n)
        kat = pl.ds(pl.multiple_of(to * kw, LANES), kw)
        keyed[i][0:tokens] = k_ref[0, :, kat]
        wanted = row // local * heads + to * local + lax.rem(row, local)
        aux = mm(((row < 6 * local) & (entry == wanted)).astype(bf16), rates)
        for at in range(kw // LANES):
            keyed[i][tokens:, at * LANES : (at + 1) * LANES] = aux[at * AUX : (at + 1) * AUX].astype(bf16)
        asked[i][:, 0:kw] = q_ref[0, :, kat]
        asked[i][:, kw:] = v_ref[0, :, pl.ds(pl.multiple_of(to * vw, LANES), vw)]


def pack_late_kernel(n, vw, g_ref, proj_ref, *outs):
    me = lax.axis_index("ctx")
    gated, pieces = outs[: n // 2 - 1], outs[n // 2 - 1 :]
    for j, out in enumerate(gated):
        chip = lax.rem(me // 2 + j + 1, n // 2)
        out[...] = g_ref[0, :, pl.ds(pl.multiple_of(chip * 2 * vw, LANES), 2 * vw)]
    for i, piece in enumerate(pieces):
        columns = piece.shape[1]
        piece[...] = proj_ref[:, i * columns : (i + 1) * columns]


def head_rates(local, keyed, tokens):
    aux = jnp.concatenate(
        [keyed[tokens:, i * LANES : (i + 1) * LANES] for i in range(keyed.shape[1] // LANES)], axis=0
    )
    row, col = iota((aux.shape[0], LANES), 0), iota((aux.shape[0], LANES), 1)
    same = (row < 6 * local) & (lax.rem(row, local) == lax.rem(col, local)) & (row // (3 * local) == col // local)
    return aux, (same & (col < 2 * local)).astype(bf16)


def both_halves(x):
    return jnp.concatenate(split2(x), axis=1)


def mm3_held(held, b):
    return mm(jnp.concatenate([held, held[:, : held.shape[1] // 2]], axis=1), b)


def stacked(x):
    high, low = split2(x)
    return jnp.concatenate([high, high, low], axis=0)


def inverse_scale(raw):
    raw_f = raw.astype(f32)
    return lax.rsqrt(jnp.sum(raw_f * raw_f, axis=1, keepdims=True) + EPS)


def inverse_kernel(n, local, *refs):
    keyed = refs[:n]
    value_ref, erase_ref, key_ref, row_ref, down_ref = refs[n:]
    me = lax.axis_index("ctx")
    tokens = value_ref.shape[2]
    group = local * DK // keyed[0].shape[1]
    row, col = iota((tokens, tokens), 0), iota((tokens, tokens), 1)
    apart = lax.bitwise_xor(row, col)
    eye = (row == col).astype(f32)
    ones = (row >= col).astype(bf16)
    systems, scales = [], []
    for i, route in enumerate(routes(n)):
        block = moved(me, route, n, back=True)
        aux, total = head_rates(local, keyed[i], tokens)
        as_cols, as_rows = mm_tn(aux, total), mm_tn(total, aux)
        decays = jnp.where(iota((8, tokens), 0) < local, as_rows[0:8], 1.0)
        logs = [piece.astype(f32) for piece in split3(jnp.log(decays))]
        logs = jnp.concatenate(logs, axis=0).astype(bf16)
        sums = mm_nt(logs, ones)
        sums = sums[16:24] + sums[8:16] + sums[0:8]
        sum_cols = mm_nt(ones, logs)
        down, up = jnp.exp(sums), jnp.exp(-sums)
        left = jnp.exp(sums[:, tokens - 1 :] - sums)
        down_cols = jnp.exp(sum_cols[:, 16:24] + sum_cols[:, 8:16] + sum_cols[:, 0:8])
        down_ref[block] = jnp.concatenate([down_cols, jnp.zeros((tokens, LANES - 8), f32)], axis=1)
        for g in range(local // group):
            k = keyed[i][0:tokens, g * DK : (g + 1) * DK]
            k_t = k.astype(f32).T
            dots = mm_nt(k, k)
            diag = dots * eye
            k_row = lax.rsqrt(jnp.sum(diag, axis=0, keepdims=True) + EPS)
            k_col = lax.rsqrt(jnp.sum(diag, axis=1, keepdims=True) + EPS)
            dots = jnp.where(row > col, dots * k_row, 0.0)
            for h in range(g * group, (g + 1) * group):
                write = as_rows[local + h : local + h + 1]
                scale = as_cols[:, local + h : local + h + 1] * down_cols[:, h : h + 1] * k_col
                systems.append(scale * (up[h : h + 1] * dots))
                scales.append((write, write * down[h : h + 1] * k_row))
                key_ref[block, h] = both_halves(k_t * (left[h : h + 1] * k_row))
                row_ref[block, h, 0:1] = up[h : h + 1] * k_row
                row_ref[block, h, 1:2] = jnp.broadcast_to(down[h : h + 1, tokens - 1 :], (1, tokens))
    near = [jnp.where(apart < 16, s, 0.0) for s in systems]
    power = [split2(s) for s in near]
    inverse = [eye - s for s in near]
    power = [mm3(p, p) for p in power]
    for _ in range(2):
        halves = [split2(p) for p in power]
        both = [mm3(split2(jnp.concatenate([p, x], axis=0)), ps) for p, x, ps in zip(power, inverse, halves)]
        power = [b[:tokens] for b in both]
        inverse = [x + b[tokens:] for x, b in zip(inverse, both)]
    inverse = [x + mm3(split2(x), split2(p)) for x, p in zip(inverse, power)]
    size = 16
    while size < tokens:
        odd = [slice(at, at + size) for at in range(size, tokens, 2 * size)]
        beside = (apart >= size) & (apart < 2 * size)
        below = [jnp.where(beside, s, 0.0) for s in systems]
        below = [split2(jnp.concatenate([b[o] for o in odd], axis=0)) for b in below]
        halves = [split2(x) for x in inverse]
        first = [mm3(b, x) for b, x in zip(below, halves)]
        first = [split2(widen(f, size)) for f in first]
        lower = [tuple(jnp.concatenate([part[o] for o in odd], axis=0) for part in x) for x in halves]
        inverse = [x - widen(mm3(a, b), size) for x, a, b in zip(inverse, lower, first)]
        size *= 2
    for i, route in enumerate(routes(n)):
        block = moved(me, route, n, back=True)
        for h in range(local):
            for_values, for_state = scales[i * local + h]
            value_ref[block, h] = both_halves(inverse[i * local + h] * for_values)
            erase_ref[block, h] = both_halves(inverse[i * local + h] * for_state)


def widen(x, size):
    none = jnp.zeros((size, x.shape[1]), x.dtype)
    return jnp.concatenate(
        [part for at in range(0, x.shape[0], size) for part in (none, x[at : at + size])], axis=0
    )


def state_kernel(n, kw, vw, *refs):
    keyed, asked = refs[:n], refs[n : 2 * n]
    value_ref, erase_ref, key_ref, row_ref, down_ref, gain_ref, keep_ref, give_ref, out_ref, kx_ref, qv_ref = refs[2 * n :]
    me = lax.axis_index("ctx")
    tokens = value_ref.shape[2]
    local = vw // DK
    group = vw // kw
    all_heads = range(local)
    for i, route in enumerate(routes(n)):
        block = moved(me, route, n, back=True)
        kx_ref[block] = keyed[i][...]
        qv_ref[block] = asked[i][...]
    row, col = iota((tokens, tokens), 0), iota((tokens, tokens), 1)
    gain = gain_ref[...]

    def prepare(block):
        down_cols = down_ref[block]
        made = []
        for g in range(local // group):
            k = kx_ref[block, 0:tokens, g * DK : (g + 1) * DK]
            q = qv_ref[block, :, g * DK : (g + 1) * DK]
            q_col = inverse_scale(q) * DK ** (-0.5)
            dots = jnp.where(row >= col, mm_nt(q, k), 0.0)
            for h in range(g * group, (g + 1) * group):
                v = qv_ref[block, :, kw + h * DK : kw + (h + 1) * DK]
                made.append(
                    dict(
                        k=jnp.concatenate([k, k], axis=1),
                        q=jnp.concatenate([q, q], axis=1),
                        scores=both_halves(dots * row_ref[block, h, 0:1]),
                        scale=down_cols[:, h : h + 1] * q_col,
                        written=mm(value_ref[block, h], jnp.concatenate([v, v], axis=0)),
                    )
                )
        return made

    def finish(block, made, held, delta):
        for h in all_heads:
            out = mm3_held(made[h]["scores"], delta[h])
            if held is not None:
                out = out + mm(made[h]["q"], held[h])
            out = made[h]["scale"] * out
            mean = jnp.mean(out * out, axis=1, keepdims=True)
            out_ref[block, :, h * DK : (h + 1) * DK] = out * lax.rsqrt(mean + EPS) * gain

    states, before, made = None, None, prepare(0)
    for block in range(n):
        held = None
        delta = [m["written"] for m in made]
        if block > 0:
            held = [jnp.concatenate(split2(s), axis=0) for s in states]
            seen = [mm(m["k"], s) for m, s in zip(made, held)]
            finish(*before)
            delta = [d - mm3_held(erase_ref[block, h], stacked(seen[h])) for h, d in enumerate(delta)]
        later = prepare(block + 1) if block < n - 1 else None
        delta = [stacked(d) for d in delta]
        if block < n - 1:
            grown = [mm3_held(key_ref[block, h], delta[h]) for h in all_heads]
            if block == 0:
                states = grown
            else:
                states = [row_ref[block, h, 1:2] * states[h] + grown[h] for h in all_heads]
        before = (block, made, held, delta)
        made = later
    finish(*before)
    for j in range(n // 2):
        keep_ref[j] = out_ref[moved(me, (j, 0), n)]
        give_ref[j] = out_ref[moved(me, (j, 1), n)].astype(bf16)


def chip_projection(me, keep, other, gate_ref, start, proj_ref, proj_other_refs, first=0):
    vw = keep.shape[1]
    mixed = []
    for heads, core in ((keep, lax.rem(me, 2)), (other, 1 - lax.rem(me, 2))):
        gate = gate_ref[:, pl.ds(pl.multiple_of(start + core * vw, LANES), vw)].astype(f32)
        mixed.append((heads.astype(f32) * (gate / (1.0 + jnp.exp(-gate)))).astype(bf16))
    columns = proj_other_refs[0].shape[1]
    for i, proj_other_ref in enumerate(proj_other_refs, first):
        here = slice(i * columns, (i + 1) * columns)
        yield here, mm(mixed[0], proj_ref[:, here]) + mm(mixed[1], proj_other_ref[...])


def far_kernel(n, first, *refs):
    gated = refs[: n // 2 - 1]
    keep_ref, other_ref, *refs = refs[n // 2 - 1 :]
    proj_ref, proj_other_ref, *sums = refs
    me = lax.axis_index("ctx")
    for j, (gate_ref, out) in enumerate(zip(gated, sums), 1):
        for _, part in chip_projection(me, keep_ref[j], other_ref[j], gate_ref, 0, proj_ref, [proj_other_ref], first):
            out[...] = part.astype(bf16)


def home_kernel(
    n,
    residual_ref,
    gate_ref,
    keep_ref,
    other_ref,
    ids_ref,
    weight_ref,
    *refs,
):
    proj_ref, *proj_other_refs = refs[:3]
    first_refs, (base_ref, picker_ref, table_ref) = refs[3:-3], refs[-3:]
    me = lax.axis_index("ctx")
    start = me // 2 * 2 * keep_ref.shape[2]
    gate_ref = gate_ref.at[0]
    parts = chip_projection(me, keep_ref[0], other_ref[0], gate_ref, start, proj_ref, proj_other_refs)
    for i, (here, part) in enumerate(parts):
        total = residual_ref[0, :, here].astype(f32) + part
        if i == 0:
            for first in first_refs:
                total = total + first[...].astype(f32)
        base_ref[:, here] = total
    slots, tokens = table_ref.shape
    slot = iota((slots, tokens), 0)
    place = slot // CAP
    expert = lax.rem(place, n) * (slots // CAP // n) + place // n
    named = jnp.zeros((slots, tokens), f32)
    weight = jnp.zeros((slots, tokens), f32)
    for j in range(ids_ref.shape[0]):
        hit = ids_ref[j] == expert
        named = named + hit.astype(f32)
        weight = weight + jnp.where(hit, weight_ref[j], 0.0)
    before = (iota((tokens, tokens), 0) < iota((tokens, tokens), 1)).astype(bf16)
    rank = mm(named.astype(bf16), before)
    chosen = jnp.where(rank == lax.rem(slot, CAP).astype(f32), named, 0.0)
    table_ref[...] = chosen * weight
    picker_ref[...] = chosen.astype(bf16)


def dispatch_kernel(base_ref, gain_ref, picker_ref, *refs):
    part_refs = refs[:-2]
    hidden_ref, rows_ref = refs[-2:]
    width = hidden_ref.shape[1]
    squares = 0.0
    step = 512
    for c in range(0, width, step):
        total = base_ref[:, c : c + step]
        at = c - (width - part_refs[0].shape[1])
        if at >= 0:
            for part in part_refs:
                total = total + part[:, at : at + step].astype(f32)
        hidden_ref[:, c : c + step] = total
        squares = squares + jnp.sum(total * total, axis=1, keepdims=True)
    scale = lax.rsqrt(squares * (1.0 / width) + EPS)
    picker = picker_ref[...]
    for c in range(0, width, step):
        normed = (hidden_ref[:, c : c + step] * scale * gain_ref[:, c : c + step]).astype(bf16)
        rows = mm(picker, normed).astype(bf16)
        rows_ref[:, :, c : c + step] = rows.reshape(*rows_ref.shape[:2], step)


def expert_kernel(rows_ref, gate_ref, up_ref, down_ref, out_ref):
    sources, cap, width = rows_ref.shape
    tile = min(sources, 128 // cap)

    def one(t, carry):
        here = pl.ds(t * tile, tile)
        x = rows_ref[here].reshape(tile * cap, width)
        gate = mm(x, gate_ref[0])
        up = mm(x, up_ref[0])
        act = (gate / (1.0 + jnp.exp(-gate)) * up).astype(bf16)
        step = 512
        for c in range(0, width, step):
            y = mm(act, down_ref[0, :, c : c + step]).astype(bf16)
            out_ref[here, :, c : c + step] = y.reshape(tile, cap, step)
        return carry

    if sources == tile:
        one(0, 0)
    else:
        lax.fori_loop(0, sources // tile, one, 0)


def combine_kernel(hidden_ref, table_ref, back_ref, mask_ref, dir_ref, out_ref, sum_ref):
    tokens, width = hidden_ref.shape
    slots = table_ref.shape[0]
    table = jnp.concatenate(split2(table_ref[...]), axis=0)
    direction = dir_ref[...]
    unit = direction / jnp.sqrt(jnp.sum(direction * direction, axis=1, keepdims=True) + EPS)
    eye = iota((tokens, tokens), 0) == iota((tokens, tokens), 1)
    mask = jnp.sum(jnp.where(eye, mask_ref[...].astype(f32), 0.0), axis=1, keepdims=True)
    along = 0.0
    step = 256
    for c in range(0, width, step):
        back = back_ref[:, :, c : c + step].reshape(slots, step)
        total = hidden_ref[:, c : c + step] + mm_tn(table, jnp.concatenate([back, back], axis=0))
        sum_ref[:, c : c + step] = total
        along = along + jnp.sum(total * unit[:, c : c + step], axis=1, keepdims=True)
    out_ref[0] = (sum_ref[...] - (mask * along) * unit).astype(bf16)


def local_part(
    n,
    devices,
    queries,
    keys,
    values,
    out_gate,
    write_rate,
    decay,
    head_gain,
    residual,
    out_proj,
    ffn_gain,
    expert_ids,
    route_weight,
    w_gate,
    w_up,
    w_down,
    ablate_mask,
    direction,
):
    tokens = queries.shape[1]
    width = residual.shape[2]
    kw, vw = keys.shape[2] // n, values.shape[2] // n
    chips = n // 2
    slots = devices * CAP
    shape = jax.ShapeDtypeStruct

    local = vw // DK
    ways = routes(n)
    keyed_shape = shape((tokens + AUX, kw), bf16)
    with jax.named_scope("pack"):
        packed = pl.pallas_call(
            functools.partial(pack_kernel, n, kw, vw),
            out_shape=[keyed_shape] * n
            + [shape((tokens, kw + vw), bf16)] * n,
            compiler_params=compiler_params(16),
        )(*in_hbm(keys, write_rate.transpose(0, 2, 1), decay.transpose(0, 2, 1), queries, values))
        keyed, asked = list(packed[:n]), list(packed[n:])
    with jax.named_scope("pack_late"):
        late = pl.pallas_call(
            functools.partial(pack_late_kernel, n, vw),
            out_shape=[shape((tokens, 2 * vw), bf16)] * (chips - 1) + [shape((out_proj.shape[0], width // 2), bf16)] * 2,
            compiler_params=compiler_params(16),
        )(*in_hbm(out_gate, out_proj))
        gated, pieces = late[: chips - 1], late[chips - 1 :]
    with jax.named_scope("heads_exchange"):
        order = [i for i, route in enumerate(ways) if route[0]] + [1]
        for i in order:
            keyed[i] = send(keyed[i], ways[i], n)
        for i in order[:-1]:
            asked[i] = send(asked[i], ways[i], n)
    with jax.named_scope("block_inverses"):
        wide = shape((n, local, tokens, 2 * tokens), bf16)
        inverses = pl.pallas_call(
            functools.partial(inverse_kernel, n, local),
            out_shape=[wide, wide, shape((n, local, DK, 2 * tokens), bf16), shape((n, local, 8, tokens), f32), shape((n, tokens, LANES), f32)],
            compiler_params=compiler_params(16),
            cost_estimate=pl.CostEstimate(flops=6 * 10**9, bytes_accessed=10**6, transcendentals=0),
        )(*keyed)
    with jax.named_scope("late_exchange"):
        keyed, asked[1], gated = lax.optimization_barrier((keyed, asked[1], gated))
        asked[1] = send(asked[1], ways[1], n)
        gated = [send(gate, (j, 0), n) for j, gate in enumerate(gated, 1)]
        proj_other = [send(piece, (0, 1), n) for piece in pieces]
    with jax.named_scope("states"):
        keep, give = pl.pallas_call(
            functools.partial(state_kernel, n, kw, vw),
            out_shape=[shape((chips, tokens, vw), f32), shape((chips, tokens, vw), bf16)],
            scratch_shapes=[
                pltpu.VMEM((n, tokens, vw), f32),
                pltpu.VMEM((n, tokens + AUX, kw), bf16),
                pltpu.VMEM((n, tokens, kw + vw), bf16),
            ],
            compiler_params=compiler_params(16),
            cost_estimate=pl.CostEstimate(flops=4 * 10**9, bytes_accessed=10**6, transcendentals=0),
        )(*keyed, *asked, *inverses, head_gain.reshape(1, -1))
    other = send(give, (0, 1), n)
    parts = []
    for i, piece in enumerate(proj_other):
        with jax.named_scope("far_projection"):
            sums = pl.pallas_call(
                functools.partial(far_kernel, n, i),
                out_shape=[shape((tokens, width // 2), bf16)] * (chips - 1),
                compiler_params=compiler_params(16),
                cost_estimate=pl.CostEstimate(flops=1000, bytes_accessed=1000, transcendentals=0),
            )(*gated, keep, other, out_proj, piece)
        keep = lax.optimization_barrier((sums, keep))[1]
        with jax.named_scope("projection_sum"):
            parts.append([send(part, (j, 0), n) for j, part in enumerate(sums, 1)])
    with jax.named_scope("home"):
        base, picker, table = pl.pallas_call(
            functools.partial(home_kernel, n),
            out_shape=[shape((tokens, width), f32), shape((slots, tokens), bf16), shape((slots, tokens), f32)],
            compiler_params=compiler_params(16),
            cost_estimate=pl.CostEstimate(flops=6 * 10**9, bytes_accessed=1000, transcendentals=0),
        )(
            residual,
            out_gate,
            keep,
            other,
            expert_ids.transpose(2, 0, 1),
            route_weight.transpose(2, 0, 1),
            out_proj,
            *proj_other,
            *parts[0],
        )
    with jax.named_scope("dispatch"):
        hidden, rows = pl.pallas_call(
            dispatch_kernel,
            out_shape=[shape((tokens, width), f32), shape((devices, CAP, width), bf16)],
            compiler_params=compiler_params(24),
        )(base, ffn_gain.reshape(1, -1), picker, *parts[1])
    with jax.named_scope("to_experts"):
        came = lax.all_to_all(rows, ("exp", "ctx"), 0, 0, tiled=True)
    with jax.named_scope("experts"):
        done = pl.pallas_call(
            expert_kernel,
            out_shape=shape((devices, CAP, width), bf16),
            compiler_params=compiler_params(24),
        )(came, w_gate, w_up, w_down)
    with jax.named_scope("from_experts"):
        back = lax.all_to_all(done, ("exp", "ctx"), 0, 0, tiled=True)
    with jax.named_scope("combine"):
        return pl.pallas_call(
            combine_kernel,
            out_shape=shape((1, tokens, width), bf16),
            scratch_shapes=[pltpu.VMEM((tokens, width), f32)],
            compiler_params=compiler_params(24),
        )(hidden, table, back, ablate_mask, direction.reshape(1, -1))


def solution(mesh):
    seq = P("exp", "ctx", None)
    owned = P(("ctx", "exp"), None, None)
    placed = (
        (seq,) * 6 + (P(), seq, P("ctx", None), P(), seq, seq) + (owned,) * 3 + (P("exp", "ctx"), P())
    )
    n = mesh.shape["ctx"]
    return jax.shard_map(
        functools.partial(local_part, n, n * mesh.shape["exp"]),
        mesh=mesh,
        in_specs=placed,
        out_specs=seq,
        check_vma=False,
    )
```

```python
import functools

import jax
import jax.numpy as jnp
from jax import lax
from jax.experimental import pallas as pl
from jax.experimental.pallas import tpu as pltpu
from jax.sharding import PartitionSpec as P

DK = 128
CAP = 4
EPS = 1e-06
AUX = 16
LANES = 128

bf16 = jnp.bfloat16
f32 = jnp.float32


def mm(a, b):
    return jnp.dot(a, b, preferred_element_type=f32)


def mm_nt(a, b):
    return lax.dot_general(a, b, (((1,), (1,)), ((), ())), preferred_element_type=f32)


def mm_tn(a, b):
    return lax.dot_general(a, b, (((0,), (0,)), ((), ())), preferred_element_type=f32)


def split2(x):
    hi = x.astype(bf16)
    return hi, (x - hi.astype(f32)).astype(bf16)


def split3(x):
    hi = x.astype(bf16)
    rest = x - hi.astype(f32)
    mid = rest.astype(bf16)
    return hi, mid, (rest - mid.astype(f32)).astype(bf16)


def mm3(a, b):
    (ah, al), (bh, bl) = a, b
    return mm(jnp.concatenate([ah, al, ah], axis=1), jnp.concatenate([bh, bh, bl], axis=0))


def iota(shape, dim):
    return lax.broadcasted_iota(jnp.int32, shape, dim)


def in_hbm(*arrays):
    return [pltpu.with_memory_space_constraint(a, pltpu.HBM) for a in arrays]


def compiler_params(mib):
    return pltpu.CompilerParams(vmem_limit_bytes=mib * 1024 * 1024)


def routes(n):
    return [(chips, flip) for chips in range(n // 2) for flip in (0, 1)]


def moved(index, route, n, back=False):
    chips, flip = route
    chip = lax.rem(index // 2 + (n // 2 - chips if back else chips), n // 2)
    return chip * 2 + lax.rem(lax.rem(index, 2) + flip, 2)


def send(x, route, n):
    chips, flip = route
    pairs = [(i, (i // 2 + chips) % (n // 2) * 2 + (i % 2 + flip) % 2) for i in range(n)]
    return lax.ppermute(x, "ctx", pairs)


def pack_kernel(n, kw, vw, k_ref, w_ref, d_ref, q_ref, v_ref, *outs):
    local = vw // DK
    keyed, asked = outs[:n], outs[n:]
    me = lax.axis_index("ctx")
    tokens = k_ref.shape[1]
    heads = d_ref.shape[1]
    pieces = [p.astype(f32) for p in (*split3(d_ref[0]), *split3(w_ref[0]))]
    rates = jnp.concatenate(pieces, axis=0).astype(bf16)
    rows = AUX * kw // LANES
    row, entry = iota((rows, 6 * heads), 0), iota((rows, 6 * heads), 1)
    for i, route in enumerate(routes(n)):
        to = moved(me, route, n)
        kat = pl.ds(pl.multiple_of(to * kw, LANES), kw)
        keyed[i][0:tokens] = k_ref[0, :, kat]
        wanted = row // local * heads + to * local + lax.rem(row, local)
        aux = mm(((row < 6 * local) & (entry == wanted)).astype(bf16), rates)
        for at in range(kw // LANES):
            keyed[i][tokens:, at * LANES : (at + 1) * LANES] = aux[at * AUX : (at + 1) * AUX].astype(bf16)
        asked[i][:, 0:kw] = q_ref[0, :, kat]
        asked[i][:, kw:] = v_ref[0, :, pl.ds(pl.multiple_of(to * vw, LANES), vw)]


def pack_late_kernel(n, vw, g_ref, proj_ref, *outs):
    me = lax.axis_index("ctx")
    gated, pieces = outs[: n // 2 - 1], outs[n // 2 - 1 :]
    for j, out in enumerate(gated):
        chip = lax.rem(me // 2 + j + 1, n // 2)
        out[...] = g_ref[0, :, pl.ds(pl.multiple_of(chip * 2 * vw, LANES), 2 * vw)]
    for i, piece in enumerate(pieces):
        columns = piece.shape[1]
        piece[...] = proj_ref[:, i * columns : (i + 1) * columns]


def head_rates(local, keyed, tokens):
    aux = jnp.concatenate(
        [keyed[tokens:, i * LANES : (i + 1) * LANES] for i in range(keyed.shape[1] // LANES)], axis=0
    )
    row, col = iota((aux.shape[0], LANES), 0), iota((aux.shape[0], LANES), 1)
    same = (row < 6 * local) & (lax.rem(row, local) == lax.rem(col, local)) & (row // (3 * local) == col // local)
    return aux, (same & (col < 2 * local)).astype(bf16)


def both_halves(x):
    return jnp.concatenate(split2(x), axis=1)


def mm3_held(held, b):
    return mm(jnp.concatenate([held, held[:, : held.shape[1] // 2]], axis=1), b)


def stacked(x):
    high, low = split2(x)
    return jnp.concatenate([high, high, low], axis=0)


def inverse_scale(raw):
    raw_f = raw.astype(f32)
    return lax.rsqrt(jnp.sum(raw_f * raw_f, axis=1, keepdims=True) + EPS)


def inverse_kernel(n, local, *refs):
    keyed = refs[:n]
    value_ref, erase_ref, key_ref, row_ref, down_ref = refs[n:]
    me = lax.axis_index("ctx")
    tokens = value_ref.shape[2]
    group = local * DK // keyed[0].shape[1]
    row, col = iota((tokens, tokens), 0), iota((tokens, tokens), 1)
    apart = lax.bitwise_xor(row, col)
    eye = (row == col).astype(f32)
    ones = (row >= col).astype(bf16)
    systems, scales = [], []
    for i, route in enumerate(routes(n)):
        block = moved(me, route, n, back=True)
        aux, total = head_rates(local, keyed[i], tokens)
        as_cols, as_rows = mm_tn(aux, total), mm_tn(total, aux)
        decays = jnp.where(iota((8, tokens), 0) < local, as_rows[0:8], 1.0)
        logs = [piece.astype(f32) for piece in split3(jnp.log(decays))]
        logs = jnp.concatenate(logs, axis=0).astype(bf16)
        sums = mm_nt(logs, ones)
        sums = sums[16:24] + sums[8:16] + sums[0:8]
        sum_cols = mm_nt(ones, logs)
        down, up = jnp.exp(sums), jnp.exp(-sums)
        left = jnp.exp(sums[:, tokens - 1 :] - sums)
        down_cols = jnp.exp(sum_cols[:, 16:24] + sum_cols[:, 8:16] + sum_cols[:, 0:8])
        down_ref[block] = jnp.concatenate([down_cols, jnp.zeros((tokens, LANES - 8), f32)], axis=1)
        for g in range(local // group):
            k = keyed[i][0:tokens, g * DK : (g + 1) * DK]
            k_t = k.astype(f32).T
            dots = mm_nt(k, k)
            diag = dots * eye
            k_row = lax.rsqrt(jnp.sum(diag, axis=0, keepdims=True) + EPS)
            k_col = lax.rsqrt(jnp.sum(diag, axis=1, keepdims=True) + EPS)
            dots = jnp.where(row > col, dots * k_row, 0.0)
            for h in range(g * group, (g + 1) * group):
                write = as_rows[local + h : local + h + 1]
                scale = as_cols[:, local + h : local + h + 1] * down_cols[:, h : h + 1] * k_col
                systems.append(scale * (up[h : h + 1] * dots))
                scales.append((write, write * down[h : h + 1] * k_row))
                key_ref[block, h] = both_halves(k_t * (left[h : h + 1] * k_row))
                row_ref[block, h, 0:1] = up[h : h + 1] * k_row
                row_ref[block, h, 1:2] = jnp.broadcast_to(down[h : h + 1, tokens - 1 :], (1, tokens))
    near = [jnp.where(apart < 16, s, 0.0) for s in systems]
    power = [split2(s) for s in near]
    inverse = [eye - s for s in near]
    power = [mm3(p, p) for p in power]
    for _ in range(2):
        halves = [split2(p) for p in power]
        both = [mm3(split2(jnp.concatenate([p, x], axis=0)), ps) for p, x, ps in zip(power, inverse, halves)]
        power = [b[:tokens] for b in both]
        inverse = [x + b[tokens:] for x, b in zip(inverse, both)]
    inverse = [x + mm3(split2(x), split2(p)) for x, p in zip(inverse, power)]
    size = 16
    while size < tokens:
        odd = [slice(at, at + size) for at in range(size, tokens, 2 * size)]
        beside = (apart >= size) & (apart < 2 * size)
        below = [jnp.where(beside, s, 0.0) for s in systems]
        below = [split2(jnp.concatenate([b[o] for o in odd], axis=0)) for b in below]
        halves = [split2(x) for x in inverse]
        first = [mm3(b, x) for b, x in zip(below, halves)]
        first = [split2(widen(f, size)) for f in first]
        lower = [tuple(jnp.concatenate([part[o] for o in odd], axis=0) for part in x) for x in halves]
        inverse = [x - widen(mm3(a, b), size) for x, a, b in zip(inverse, lower, first)]
        size *= 2
    for i, route in enumerate(routes(n)):
        block = moved(me, route, n, back=True)
        for h in range(local):
            for_values, for_state = scales[i * local + h]
            value_ref[block, h] = both_halves(inverse[i * local + h] * for_values)
            erase_ref[block, h] = both_halves(inverse[i * local + h] * for_state)


def widen(x, size):
    none = jnp.zeros((size, x.shape[1]), x.dtype)
    return jnp.concatenate(
        [part for at in range(0, x.shape[0], size) for part in (none, x[at : at + size])], axis=0
    )


def state_kernel(n, kw, vw, *refs):
    keyed, asked = refs[:n], refs[n : 2 * n]
    value_ref, erase_ref, key_ref, row_ref, down_ref, gain_ref, keep_ref, give_ref, out_ref, kx_ref, qv_ref = refs[2 * n :]
    me = lax.axis_index("ctx")
    tokens = value_ref.shape[2]
    local = vw // DK
    group = vw // kw
    all_heads = range(local)
    for i, route in enumerate(routes(n)):
        block = moved(me, route, n, back=True)
        kx_ref[block] = keyed[i][...]
        qv_ref[block] = asked[i][...]
    row, col = iota((tokens, tokens), 0), iota((tokens, tokens), 1)
    gain = gain_ref[...]

    def prepare(block):
        down_cols = down_ref[block]
        made = []
        for g in range(local // group):
            k = kx_ref[block, 0:tokens, g * DK : (g + 1) * DK]
            q = qv_ref[block, :, g * DK : (g + 1) * DK]
            q_col = inverse_scale(q) * DK ** (-0.5)
            dots = jnp.where(row >= col, mm_nt(q, k), 0.0)
            for h in range(g * group, (g + 1) * group):
                v = qv_ref[block, :, kw + h * DK : kw + (h + 1) * DK]
                made.append(
                    dict(
                        k=jnp.concatenate([k, k], axis=1),
                        q=jnp.concatenate([q, q], axis=1),
                        scores=both_halves(dots * row_ref[block, h, 0:1]),
                        scale=down_cols[:, h : h + 1] * q_col,
                        written=mm(value_ref[block, h], jnp.concatenate([v, v], axis=0)),
                    )
                )
        return made

    def finish(block, made, held, delta):
        for h in all_heads:
            out = mm3_held(made[h]["scores"], delta[h])
            if held is not None:
                out = out + mm(made[h]["q"], held[h])
            out = made[h]["scale"] * out
            mean = jnp.mean(out * out, axis=1, keepdims=True)
            out_ref[block, :, h * DK : (h + 1) * DK] = out * lax.rsqrt(mean + EPS) * gain

    states, before, made = None, None, prepare(0)
    for block in range(n):
        held = None
        delta = [m["written"] for m in made]
        if block > 0:
            held = [jnp.concatenate(split2(s), axis=0) for s in states]
            seen = [mm(m["k"], s) for m, s in zip(made, held)]
            finish(*before)
            delta = [d - mm3_held(erase_ref[block, h], stacked(seen[h])) for h, d in enumerate(delta)]
        later = prepare(block + 1) if block < n - 1 else None
        delta = [stacked(d) for d in delta]
        if block < n - 1:
            grown = [mm3_held(key_ref[block, h], delta[h]) for h in all_heads]
            if block == 0:
                states = grown
            else:
                states = [row_ref[block, h, 1:2] * states[h] + grown[h] for h in all_heads]
        before = (block, made, held, delta)
        made = later
    finish(*before)
    for j in range(n // 2):
        keep_ref[j] = out_ref[moved(me, (j, 0), n)]
        give_ref[j] = out_ref[moved(me, (j, 1), n)].astype(bf16)


def chip_projection(me, keep, other, gate_ref, start, proj_ref, proj_other_refs, first=0):
    vw = keep.shape[1]
    mixed = []
    for heads, core in ((keep, lax.rem(me, 2)), (other, 1 - lax.rem(me, 2))):
        gate = gate_ref[:, pl.ds(pl.multiple_of(start + core * vw, LANES), vw)].astype(f32)
        mixed.append((heads.astype(f32) * (gate / (1.0 + jnp.exp(-gate)))).astype(bf16))
    columns = proj_other_refs[0].shape[1]
    for i, proj_other_ref in enumerate(proj_other_refs, first):
        here = slice(i * columns, (i + 1) * columns)
        yield here, mm(mixed[0], proj_ref[:, here]) + mm(mixed[1], proj_other_ref[...])


def far_kernel(n, first, *refs):
    gated = refs[: n // 2 - 1]
    keep_ref, other_ref, *refs = refs[n // 2 - 1 :]
    proj_ref, proj_other_ref, *sums = refs
    me = lax.axis_index("ctx")
    for j, (gate_ref, out) in enumerate(zip(gated, sums), 1):
        for _, part in chip_projection(me, keep_ref[j], other_ref[j], gate_ref, 0, proj_ref, [proj_other_ref], first):
            out[...] = part.astype(bf16)


def home_kernel(
    n,
    residual_ref,
    gate_ref,
    keep_ref,
    other_ref,
    ids_ref,
    weight_ref,
    *refs,
):
    proj_ref, *proj_other_refs = refs[:3]
    first_refs, (base_ref, picker_ref, table_ref) = refs[3:-3], refs[-3:]
    me = lax.axis_index("ctx")
    start = me // 2 * 2 * keep_ref.shape[2]
    gate_ref = gate_ref.at[0]
    parts = chip_projection(me, keep_ref[0], other_ref[0], gate_ref, start, proj_ref, proj_other_refs)
    for i, (here, part) in enumerate(parts):
        total = residual_ref[0, :, here].astype(f32) + part
        if i == 0:
            for first in first_refs:
                total = total + first[...].astype(f32)
        base_ref[:, here] = total
    slots, tokens = table_ref.shape
    slot = iota((slots, tokens), 0)
    place = slot // CAP
    expert = lax.rem(place, n) * (slots // CAP // n) + place // n
    named = jnp.zeros((slots, tokens), f32)
    weight = jnp.zeros((slots, tokens), f32)
    for j in range(ids_ref.shape[0]):
        hit = ids_ref[j] == expert
        named = named + hit.astype(f32)
        weight = weight + jnp.where(hit, weight_ref[j], 0.0)
    before = (iota((tokens, tokens), 0) < iota((tokens, tokens), 1)).astype(bf16)
    rank = mm(named.astype(bf16), before)
    chosen = jnp.where(rank == lax.rem(slot, CAP).astype(f32), named, 0.0)
    table_ref[...] = chosen * weight
    picker_ref[...] = chosen.astype(bf16)


def dispatch_kernel(base_ref, gain_ref, picker_ref, *refs):
    part_refs = refs[:-2]
    hidden_ref, rows_ref = refs[-2:]
    width = hidden_ref.shape[1]
    squares = 0.0
    step = 512
    for c in range(0, width, step):
        total = base_ref[:, c : c + step]
        at = c - (width - part_refs[0].shape[1])
        if at >= 0:
            for part in part_refs:
                total = total + part[:, at : at + step].astype(f32)
        hidden_ref[:, c : c + step] = total
        squares = squares + jnp.sum(total * total, axis=1, keepdims=True)
    scale = lax.rsqrt(squares * (1.0 / width) + EPS)
    picker = picker_ref[...]
    for c in range(0, width, step):
        normed = (hidden_ref[:, c : c + step] * scale * gain_ref[:, c : c + step]).astype(bf16)
        rows = mm(picker, normed).astype(bf16)
        rows_ref[:, :, c : c + step] = rows.reshape(*rows_ref.shape[:2], step)


def expert_kernel(rows_ref, gate_ref, up_ref, down_ref, out_ref):
    sources, cap, width = rows_ref.shape
    tile = min(sources, 128 // cap)

    def one(t, carry):
        here = pl.ds(t * tile, tile)
        x = rows_ref[here].reshape(tile * cap, width)
        gate = mm(x, gate_ref[0])
        up = mm(x, up_ref[0])
        act = (gate / (1.0 + jnp.exp(-gate)) * up).astype(bf16)
        step = 512
        for c in range(0, width, step):
            y = mm(act, down_ref[0, :, c : c + step]).astype(bf16)
            out_ref[here, :, c : c + step] = y.reshape(tile, cap, step)
        return carry

    if sources == tile:
        one(0, 0)
    else:
        lax.fori_loop(0, sources // tile, one, 0)


def combine_kernel(hidden_ref, table_ref, back_ref, mask_ref, dir_ref, out_ref, sum_ref):
    tokens, width = hidden_ref.shape
    slots = table_ref.shape[0]
    table = jnp.concatenate(split2(table_ref[...]), axis=0)
    direction = dir_ref[...]
    unit = direction / jnp.sqrt(jnp.sum(direction * direction, axis=1, keepdims=True) + EPS)
    eye = iota((tokens, tokens), 0) == iota((tokens, tokens), 1)
    mask = jnp.sum(jnp.where(eye, mask_ref[...].astype(f32), 0.0), axis=1, keepdims=True)
    along = 0.0
    step = 512
    for c in range(0, width, step):
        back = back_ref[:, :, c : c + step].reshape(slots, step)
        total = hidden_ref[:, c : c + step] + mm_tn(table, jnp.concatenate([back, back], axis=0))
        sum_ref[:, c : c + step] = total
        along = along + jnp.sum(total * unit[:, c : c + step], axis=1, keepdims=True)
    out_ref[0] = (sum_ref[...] - (mask * along) * unit).astype(bf16)


def local_part(
    n,
    devices,
    queries,
    keys,
    values,
    out_gate,
    write_rate,
    decay,
    head_gain,
    residual,
    out_proj,
    ffn_gain,
    expert_ids,
    route_weight,
    w_gate,
    w_up,
    w_down,
    ablate_mask,
    direction,
):
    tokens = queries.shape[1]
    width = residual.shape[2]
    kw, vw = keys.shape[2] // n, values.shape[2] // n
    chips = n // 2
    slots = devices * CAP
    shape = jax.ShapeDtypeStruct

    local = vw // DK
    ways = routes(n)
    keyed_shape = shape((tokens + AUX, kw), bf16)
    with jax.named_scope("pack"):
        packed = pl.pallas_call(
            functools.partial(pack_kernel, n, kw, vw),
            out_shape=[keyed_shape] * n
            + [shape((tokens, kw + vw), bf16)] * n,
            compiler_params=compiler_params(16),
        )(*in_hbm(keys, write_rate.transpose(0, 2, 1), decay.transpose(0, 2, 1), queries, values))
        keyed, asked = list(packed[:n]), list(packed[n:])
    with jax.named_scope("pack_late"):
        late = pl.pallas_call(
            functools.partial(pack_late_kernel, n, vw),
            out_shape=[shape((tokens, 2 * vw), bf16)] * (chips - 1) + [shape((out_proj.shape[0], width // 2), bf16)] * 2,
            compiler_params=compiler_params(16),
        )(*in_hbm(out_gate, out_proj))
        gated, pieces = late[: chips - 1], late[chips - 1 :]
    with jax.named_scope("heads_exchange"):
        order = [i for i, route in enumerate(ways) if route[0]] + [1]
        for i in order:
            keyed[i] = send(keyed[i], ways[i], n)
        for i in order[:-1]:
            asked[i] = send(asked[i], ways[i], n)
    with jax.named_scope("block_inverses"):
        wide = shape((n, local, tokens, 2 * tokens), bf16)
        inverses = pl.pallas_call(
            functools.partial(inverse_kernel, n, local),
            out_shape=[wide, wide, shape((n, local, DK, 2 * tokens), bf16), shape((n, local, 8, tokens), f32), shape((n, tokens, LANES), f32)],
            compiler_params=compiler_params(16),
            cost_estimate=pl.CostEstimate(flops=6 * 10**9, bytes_accessed=10**6, transcendentals=0),
        )(*keyed)
    with jax.named_scope("late_exchange"):
        keyed, asked[1], gated = lax.optimization_barrier((keyed, asked[1], gated))
        asked[1] = send(asked[1], ways[1], n)
        gated = [send(gate, (j, 0), n) for j, gate in enumerate(gated, 1)]
        proj_other = [send(piece, (0, 1), n) for piece in pieces]
    with jax.named_scope("states"):
        keep, give = pl.pallas_call(
            functools.partial(state_kernel, n, kw, vw),
            out_shape=[shape((chips, tokens, vw), f32), shape((chips, tokens, vw), bf16)],
            scratch_shapes=[
                pltpu.VMEM((n, tokens, vw), f32),
                pltpu.VMEM((n, tokens + AUX, kw), bf16),
                pltpu.VMEM((n, tokens, kw + vw), bf16),
            ],
            compiler_params=compiler_params(16),
            cost_estimate=pl.CostEstimate(flops=4 * 10**9, bytes_accessed=10**6, transcendentals=0),
        )(*keyed, *asked, *inverses, head_gain.reshape(1, -1))
    other = send(give, (0, 1), n)
    parts = []
    for i, piece in enumerate(proj_other):
        with jax.named_scope("far_projection"):
            sums = pl.pallas_call(
                functools.partial(far_kernel, n, i),
                out_shape=[shape((tokens, width // 2), bf16)] * (chips - 1),
                compiler_params=compiler_params(16),
                cost_estimate=pl.CostEstimate(flops=1000, bytes_accessed=1000, transcendentals=0),
            )(*gated, keep, other, out_proj, piece)
        keep = lax.optimization_barrier((sums, keep))[1]
        with jax.named_scope("projection_sum"):
            parts.append([send(part, (j, 0), n) for j, part in enumerate(sums, 1)])
    with jax.named_scope("home"):
        base, picker, table = pl.pallas_call(
            functools.partial(home_kernel, n),
            out_shape=[shape((tokens, width), f32), shape((slots, tokens), bf16), shape((slots, tokens), f32)],
            compiler_params=compiler_params(16),
            cost_estimate=pl.CostEstimate(flops=6 * 10**9, bytes_accessed=1000, transcendentals=0),
        )(
            residual,
            out_gate,
            keep,
            other,
            expert_ids.transpose(2, 0, 1),
            route_weight.transpose(2, 0, 1),
            out_proj,
            *proj_other,
            *parts[0],
        )
    with jax.named_scope("dispatch"):
        hidden, rows = pl.pallas_call(
            dispatch_kernel,
            out_shape=[shape((tokens, width), f32), shape((devices, CAP, width), bf16)],
            compiler_params=compiler_params(24),
        )(base, ffn_gain.reshape(1, -1), picker, *parts[1])
    with jax.named_scope("to_experts"):
        came = lax.all_to_all(rows, ("exp", "ctx"), 0, 0, tiled=True)
    with jax.named_scope("experts"):
        done = pl.pallas_call(
            expert_kernel,
            out_shape=shape((devices, CAP, width), bf16),
            compiler_params=compiler_params(24),
        )(came, w_gate, w_up, w_down)
    with jax.named_scope("from_experts"):
        back = lax.all_to_all(done, ("exp", "ctx"), 0, 0, tiled=True)
    with jax.named_scope("combine"):
        return pl.pallas_call(
            combine_kernel,
            out_shape=shape((1, tokens, width), bf16),
            scratch_shapes=[pltpu.VMEM((tokens, width), f32)],
            compiler_params=compiler_params(24),
        )(hidden, table, back, ablate_mask, direction.reshape(1, -1))


def solution(mesh):
    seq = P("exp", "ctx", None)
    owned = P(("ctx", "exp"), None, None)
    placed = (
        (seq,) * 6 + (P(), seq, P("ctx", None), P(), seq, seq) + (owned,) * 3 + (P("exp", "ctx"), P())
    )
    n = mesh.shape["ctx"]
    return jax.shard_map(
        functools.partial(local_part, n, n * mesh.shape["exp"]),
        mesh=mesh,
        in_specs=placed,
        out_specs=seq,
        check_vma=False,
    )
```
